128 devices in a mesh: dp: 32 (over z, x, core), tensor: 4 (over y).
Axes of the slice: x: 4, y: 4, z: 4, core: 2. Of those that a mesh axis runs over, the one named last changes fastest.
Arguments:
- text_input: bfloat16 [16384, 768], P(('dp', 'tensor')), may hold values from -6 to 6
- segment_ids: int32 [1024, 16], P('dp'), may hold values from 0 to 1, as said below
- pad_mask: int32 [1024, 16], P('dp'), may hold values from 0 to 1, as said below
- pairing: int32 [2048], P(('dp', 'tensor')), may hold values from 0 to 2047, each once
- ln_first: float32 [768], replicated, may hold values from 0.1 to 1.9
- w_qkv: bfloat16 [3, 768, 768], P(None, None, 'tensor'), may hold values from -0.21875 to 0.21875
- w_out: bfloat16 [768, 768], P('tensor'), may hold values from -0.4375 to 0.4375
- ln_second: float32 [768], replicated, may hold values from 0.1 to 1.9
- w_up: bfloat16 [768, 3072], P(None, 'tensor'), may hold values from -0.21875 to 0.21875
- w_down: bfloat16 [3072, 768], P('tensor'), may hold values from -0.109375 to 0.109375
- text_proj: bfloat16 [768, 768], replicated, may hold values from -0.21875 to 0.21875
- image_tokens: bfloat16 [2048, 50, 768], P(('dp', 'tensor')), may hold values from -6 to 6
- img_ln_first: float32 [768], replicated, may hold values from 0.1 to 1.9
- img_w_qkv: bfloat16 [3, 768, 768], replicated, may hold values from -0.21875 to 0.21875
- img_w_out: bfloat16 [768, 768], replicated, may hold values from -0.875 to 0.875
- img_ln_second: float32 [768], replicated, may hold values from 0.1 to 1.9
- img_w_up: bfloat16 [768, 3072], replicated, may hold values from -0.21875 to 0.21875
- img_w_down: bfloat16 [3072, 768], replicated, may hold values from -0.109375 to 0.109375
- img_proj: bfloat16 [768, 768], replicated, may hold values from -0.21875 to 0.21875
Outputs:
- loss: float32 [], replicated
- input_grad: float32 [16384, 768], P(('dp', 'tensor'))
- ln_first_grad: float32 [768], replicated
- qkv_grad: float32 [3, 768, 768], P(None, None, 'tensor')
- out_grad: float32 [768, 768], P('tensor')
- ln_second_grad: float32 [768], replicated
- up_grad: float32 [768, 3072], P(None, 'tensor')
- down_grad: float32 [3072, 768], P('tensor')
- proj_grad: float32 [768, 768], replicated
The draws below stay inside these ranges and needn't reach their ends.
Inputs may be any that keep to these rules, and one draw needn't show every extreme that they name: `segment_ids`: each sequence holds two captions of 3 to 8 rows each, numbered 0 then 1 in order; padding rows after the second caption carry 1. `pad_mask`: 1 on the rows of the two captions of a sequence, 0 on the padding rows that follow them. `pairing`: a permutation: each image belongs to exactly one caption.
All inputs are finite; a program needn't handle non-finite values.
Results may differ from the reference program's by a relative error of at most 0.02.
Values may be sent and summed in bfloat16 or wider, within the bound.
A program may use at most 128 MiB of HBM per device.

```python
import jax
import jax.numpy as jnp
from jax import lax

D = 768
HEADS = 12
HEAD_DIM = 64
FF = 3072
EMBED = 768
IMG_LEN = 50
SEQ_LEN = 16
CAP_SEQ = 2
SEQS = 1024
ROWS = 16384
CAPTIONS = 2048
IMAGES = 2048


def caption_layout(key):
    first_len = jax.random.randint(jax.random.fold_in(key, 11), (SEQS, 1), 3, 9)
    second_len = jax.random.randint(jax.random.fold_in(key, 12), (SEQS, 1), 3, 9)
    position = jnp.arange(SEQ_LEN, dtype=jnp.int32)[None, :]
    segment = jnp.where(position < first_len, 0, 1).astype(jnp.int32)
    kept = (position < first_len + second_len).astype(jnp.int32)
    return (segment, kept)


def draw_segment_ids(key, part):
    layout = caption_layout(key)
    return layout[0]


def draw_pad_mask(key, part):
    layout = caption_layout(key)
    return layout[1]


def levels(own_key, dims, cuts, least, high):
    gain = 1.0
    for axis_at, parts in cuts:
        steps = jax.random.uniform(jax.random.fold_in(jax.random.fold_in(own_key, 6), axis_at), (parts,), jnp.float32, least / len(cuts), high / len(cuts))
        gain = gain * jnp.repeat(jnp.exp(steps), dims[axis_at] // parts).reshape((-1,) + (1,) * (len(dims) - 1 - axis_at))
    return gain


def gaussian(key, dims, width, reach, split=(), kind=jnp.bfloat16):
    factor_of = levels(key, dims, split, -0.22, 0.18) if split else 1.0
    values = jax.random.normal(key, dims, jnp.float32) * width * factor_of
    return jnp.minimum(jnp.maximum(values, -reach), reach).astype(kind)


def setup_inputs(seed: int = 0) -> dict:
    keys = jax.random.split(jax.random.key(seed), 20)
    text_input = gaussian(keys[0], (ROWS, D), 1.0, 6.0, ((0, 128),))
    segment_ids = draw_segment_ids(jax.random.fold_in(keys[19], 71), 0)
    pad_mask = draw_pad_mask(jax.random.fold_in(keys[19], 71), 0)
    pairing = jax.random.permutation(keys[3], CAPTIONS).astype(jnp.int32)
    ln_first = jnp.clip(1.0 + 0.18 * jax.random.normal(keys[4], (D,), jnp.float32), 0.1, 1.9)
    w_qkv = gaussian(keys[5], (3, D, D), D ** -0.5, 0.21875, ((2, 4),))
    w_out = gaussian(keys[6], (D, D), (D // 4) ** -0.5, 0.4375, ((0, 4),))
    ln_second = jnp.clip(1.0 + 0.18 * jax.random.normal(keys[7], (D,), jnp.float32), 0.1, 1.9)
    w_up = gaussian(keys[8], (D, FF), D ** -0.5, 0.21875, ((1, 4),))
    w_down = gaussian(keys[9], (FF, D), FF ** -0.5, 0.109375, ((0, 4),))
    text_proj = gaussian(keys[10], (D, EMBED), D ** -0.5, 0.21875)
    image_tokens = gaussian(keys[11], (IMAGES, IMG_LEN, D), 1.0, 6.0, ((0, 128),))
    img_ln_first = jnp.clip(1.0 + 0.18 * jax.random.normal(keys[12], (D,), jnp.float32), 0.1, 1.9)
    img_w_qkv = gaussian(keys[13], (3, D, D), D ** -0.5, 0.21875)
    img_w_out = gaussian(keys[14], (D, D), (D // 16) ** -0.5, 0.875)
    img_ln_second = jnp.clip(1.0 + 0.18 * jax.random.normal(keys[15], (D,), jnp.float32), 0.1, 1.9)
    img_w_up = gaussian(keys[16], (D, FF), D ** -0.5, 0.21875)
    img_w_down = gaussian(keys[17], (FF, D), FF ** -0.5, 0.109375)
    img_proj = gaussian(keys[18], (D, EMBED), D ** -0.5, 0.21875)
    return {"text_input": text_input, "segment_ids": segment_ids, "pad_mask": pad_mask, "pairing": pairing, "ln_first": ln_first, "w_qkv": w_qkv, "w_out": w_out, "ln_second": ln_second, "w_up": w_up, "w_down": w_down, "text_proj": text_proj, "image_tokens": image_tokens, "img_ln_first": img_ln_first, "img_w_qkv": img_w_qkv, "img_w_out": img_w_out, "img_ln_second": img_ln_second, "img_w_up": img_w_up, "img_w_down": img_w_down, "img_proj": img_proj}


EXACT = lax.Precision.HIGHEST
NORM_EPS = 1e-06
SCORE_SCALE = 0.125
LOGIT_SCALE = 40.0
MASKED = -1e+30

@jax.custom_vjp
def low(v):
    return lax.optimization_barrier(v.astype(jnp.bfloat16)).astype(jnp.float32)

@jax.custom_vjp
def low_back(v):
    return v

def low_keep(v):
    return (low(v), None)

def low_pass(kept, grad):
    return (grad,)

def back_keep(v):
    return (v, None)

def back_low(kept, grad):
    return (low(grad),)
low.defvjp(low_keep, low_pass)
low_back.defvjp(back_keep, back_low)

def layer_norm(values, gain_row):
    centred = values - lax.optimization_barrier(jnp.mean(values, axis=-1, keepdims=True))
    spread = lax.optimization_barrier(jnp.mean(centred * centred, axis=-1, keepdims=True))
    return centred * lax.rsqrt(spread + NORM_EPS) * gain_row

def unit_rows(values):
    return values * lax.rsqrt(lax.optimization_barrier(jnp.sum(values * values, axis=-1, keepdims=True)) + NORM_EPS)

def image_embed(image_tokens, ln_one, w_triple, w_output, ln_two, w_upper, w_lower, w_project):
    image_count = image_tokens.shape[0]
    stream = image_tokens.astype(jnp.float32).reshape(image_count * IMG_LEN, D)
    normed = low(layer_norm(stream, ln_one))
    triple = low(jnp.einsum('rd,kde->kre', normed, w_triple.astype(jnp.float32), precision=EXACT))
    shaped = triple.reshape(3, image_count, IMG_LEN, HEADS, HEAD_DIM)
    scores = jnp.einsum('bqhd,bkhd->bhqk', shaped[0], shaped[1], precision=EXACT) * SCORE_SCALE
    weights = low(jax.nn.softmax(scores, axis=-1))
    attended = low(jnp.einsum('bhqk,bkhd->bqhd', weights, shaped[2], precision=EXACT).reshape(image_count * IMG_LEN, D))
    stream = stream + jnp.dot(attended, w_output.astype(jnp.float32), precision=EXACT)
    second = low(layer_norm(stream, ln_two))
    hidden = low(jax.nn.gelu(jnp.dot(second, w_upper.astype(jnp.float32), precision=EXACT), approximate=False))
    stream = stream + jnp.dot(hidden, w_lower.astype(jnp.float32), precision=EXACT)
    pooled = low(lax.optimization_barrier(jnp.mean(stream.reshape(image_count, IMG_LEN, D), axis=1)))
    return low(unit_rows(jnp.dot(pooled, w_project.astype(jnp.float32), precision=EXACT)))

def text_loss(stream, ln_first, w_qkv, w_out, ln_second, w_up, w_down, text_proj, segment_ids, pad_mask, pairing, images):
    seq_count = segment_ids.shape[0]
    row_count = stream.shape[0]
    normed_one = low(layer_norm(stream, ln_first))
    triple = low(low_back(jnp.einsum('rd,kde->kre', normed_one, w_qkv, precision=EXACT)))
    shaped = triple.reshape(3, seq_count, SEQ_LEN, HEADS, HEAD_DIM)
    scores = low_back(jnp.einsum('sqhd,skhd->shqk', shaped[0], shaped[1], precision=EXACT) * SCORE_SCALE)
    allowed = (segment_ids[:, :, None] == segment_ids[:, None, :]) & (pad_mask[:, None, :] == 1)
    weights = jax.nn.softmax(jnp.where(allowed[:, None], scores, MASKED), axis=-1)
    attended = jnp.einsum('shqk,skhd->sqhd', low(weights), shaped[2], precision=EXACT)
    attended = low(low_back(attended.reshape(row_count, D)))
    middle = stream + low_back(jnp.dot(attended, w_out, precision=EXACT))
    second = low(layer_norm(middle, ln_second))
    before = low_back(jnp.dot(second, w_up, precision=EXACT))
    hidden = low(jax.nn.gelu(before, approximate=False))
    output_rows = middle + low_back(jnp.dot(hidden, w_down, precision=EXACT))
    caption_of = (jnp.arange(row_count).astype(jnp.int32) // SEQ_LEN * CAP_SEQ + segment_ids.reshape(-1)).astype(jnp.int32)
    weight = pad_mask.reshape(-1).astype(jnp.float32)
    caption_sums = jax.ops.segment_sum(output_rows * weight[:, None], caption_of, num_segments=CAPTIONS)
    counts = jax.ops.segment_sum(weight, caption_of, num_segments=CAPTIONS)
    pooled = low(caption_sums / counts[:, None])
    embedding = low_back(jnp.dot(pooled, text_proj, precision=EXACT))
    text_rows = low(unit_rows(embedding))
    similar = low_back(LOGIT_SCALE * jnp.dot(text_rows, images.T, precision=EXACT))
    target = jnp.take_along_axis(similar, pairing[:, None].astype(jnp.int32), axis=1)
    loss_sum = jnp.sum(jax.nn.logsumexp(similar, axis=1)) + jnp.sum(jax.nn.logsumexp(similar, axis=0)) - 2.0 * jnp.sum(target)
    return loss_sum / (2.0 * CAPTIONS)

def reference(text_input, segment_ids, pad_mask, pairing, ln_first, w_qkv, w_out, ln_second, w_up, w_down, text_proj, image_tokens, img_ln_first, img_w_qkv, img_w_out, img_ln_second, img_w_up, img_w_down, img_proj):
    floats = [item.astype(jnp.float32) for item in (text_input, ln_first, w_qkv, w_out, ln_second, w_up, w_down, text_proj)]

    def closed(*params):
        images = image_embed(image_tokens, img_ln_first, img_w_qkv, img_w_out, img_ln_second, img_w_up, img_w_down, img_proj)
        return text_loss(*params, segment_ids, pad_mask, pairing, images)
    loss_value, pullback = jax.vjp(closed, *floats)
    gradients = pullback(jnp.ones_like(loss_value) * CAPTIONS)
    return (loss_value, gradients[0], gradients[1], gradients[2], gradients[3], gradients[4], gradients[5], gradients[6], gradients[7])
```

```python
import jax, jax.numpy as jnp
from jax import lax
from jax.experimental import pallas as pl
from jax.experimental.pallas import tpu as pltpu
from jax.sharding import PartitionSpec as P

F32, BF16, I32 = jnp.float32, jnp.bfloat16, jnp.int32
VM = pltpu.VMEM
EPS = 1e-6
NEG = -1e30
D, FF, HID = 768, 3072, 768
IMGS, POS = 16, 50
IROWS = IMGS * POS
PAIR = 112
PROWS = PAIR * (IMGS // 2)
TILE = 256


def dot(a, b):
    return jnp.dot(a, b, preferred_element_type=F32)


def dot_t(a, b):
    return lax.dot_general(a, b, (((1,), (1,)), ((), ())), preferred_element_type=F32)


def t_dot(a, b):
    return lax.dot_general(a, b, (((0,), (0,)), ((), ())), preferred_element_type=F32)


def iota(shape, axis):
    return lax.broadcasted_iota(I32, shape, axis)


def normalized(values):
    centred = values - jnp.mean(values, axis=-1, keepdims=True)
    spread = jnp.mean(centred * centred, axis=-1, keepdims=True)
    scale = lax.rsqrt(spread + EPS)
    return centred * scale, scale


def normal_cdf(u):
    bell = jnp.exp(u * u * -0.5)
    t = 1.0 / (1.0 + (0.3275911 * 0.7071067811865476) * jnp.abs(u))
    poly = t * (0.5 * 0.254829592 + t * (0.5 * -0.284496736 + t * (0.5 * 1.421413741 + t * (0.5 * -1.453152027 + t * (0.5 * 1.061405429)))))
    tail = poly * bell
    return jnp.where(u < 0.0, tail, 1.0 - tail), bell


def image_masks(perm, back, bias):
    lanes = iota((PAIR, IROWS), 1)
    w = iota((PAIR, IROWS), 0)
    second = (w >= POS).astype(I32)
    for p in range(IMGS // 2):
        src = jnp.where(w < 2 * POS, (w - POS * second) * IMGS + 2 * p + second, -1)
        perm[pl.ds(p * PAIR, PAIR), :] = jnp.where(src == lanes, 1.0, 0.0).astype(BF16)

    def rows(i, c):
        r = i * 160 + iota((160, PROWS), 0)
        img, pos = r & 15, r >> 4
        col = (img >> 1) * PAIR + (img & 1) * POS + pos
        back[pl.ds(pl.multiple_of(i * 160, 160), 160), :] = jnp.where(col == iota((160, PROWS), 1), 1.0, 0.0).astype(BF16)
        return c

    lax.fori_loop(0, 5, rows, 0)
    q = iota((2 * PAIR, PAIR), 0)
    q = jnp.where(q >= PAIR, q - PAIR, q)
    k = iota((2 * PAIR, PAIR), 1)
    bias[...] = jnp.where(((q >= POS) == (k >= POS)) & (k < 2 * POS), 0.0, NEG)


def image_norm_one(tok, gain, ia):
    def rows(i, c):
        s = pl.ds(pl.multiple_of(i * 160, 160), 160)
        n, _ = normalized(tok[s, :].astype(F32))
        ia[s, :] = (n * gain).astype(BF16)
        return c

    lax.fori_loop(0, 5, rows, 0)


def tiles(n, body):
    def step(i, c):
        body(i, pl.ds(pl.multiple_of(i * TILE, TILE), TILE))
        return c

    lax.fori_loop(0, n, step, 0)


def image_permute(perm, ia, iap):
    def body(i, s):
        iap[:, s] = dot(perm[...], ia[:, s]).astype(BF16)

    tiles(3, body)


def image_qkv(iap, w, iqkv):
    for j in range(3):
        def body(i, s):
            iqkv[j, :, s] = dot(iap[...], w[j, :, s]).astype(BF16)

        tiles(3, body)


def image_attention(iqkv, bias, iatt, first, last):
    low = iota((PAIR, 128), 1) < 64

    def pair(p, c):
        rows = pl.ds(pl.multiple_of(p * PAIR, PAIR), PAIR)
        ones = jnp.ones((PAIR, 128), BF16)
        zero = jnp.zeros((PAIR, 128), BF16)
        for h in range(6):
            cols = pl.ds(h * 128, 128)
            q, k, v = iqkv[0, rows, cols], iqkv[1, rows, cols], iqkv[2, rows, cols]
            q2 = jnp.concatenate([jnp.where(low, q, zero), jnp.where(low, zero, q)], axis=0)
            s = dot_t(q2, k) * 0.125 + bias[...]
            e = jnp.exp(s - jnp.max(s, axis=-1, keepdims=True)).astype(BF16)
            o = dot(e, jnp.concatenate([v, ones], axis=1))
            o = o[:, :128] / o[:, 128:]
            iatt[rows, cols] = jnp.where(low, o[:PAIR], o[PAIR:]).astype(BF16)
        return c

    lax.fori_loop(first, last, pair, 0)


def image_out(back, iatt, spare, tok, w, iy):
    def body(i, s):
        spare[:, s] = dot(back[...], iatt[:, s]).astype(BF16)

    tiles(3, body)

    def body2(i, s):
        iy[:, s] = tok[:, s].astype(F32) + dot(spare[...], w[:, s])

    tiles(3, body2)


def image_norm_two(iy, gain, ia, ypool):
    ypool[...] = jnp.zeros_like(ypool)

    def rows(i, c):
        s = pl.ds(pl.multiple_of(i * 160, 160), 160)
        y = iy[s, :]
        ypool[...] += jnp.sum(y.reshape(10, IMGS, D), axis=0)
        n, _ = normalized(y)
        ia[s, :] = (n * gain).astype(BF16)
        return c

    lax.fori_loop(0, 5, rows, 0)


def image_up(ia, w, hsum, first, last):
    def step(i, c):
        s = pl.ds(pl.multiple_of(i * TILE, TILE), TILE)
        u = dot(ia[...], w[:, s])
        phi, _ = normal_cdf(u)
        hsum[:, s] = jnp.sum((u * phi).reshape(POS, IMGS, TILE), axis=0)
        return c

    lax.fori_loop(first, last, step, 0)


def split_rows(x):
    hi = x.astype(BF16)
    return jnp.concatenate([hi, (x - hi.astype(F32)).astype(BF16)], axis=0)


def image_finish(hsum, ypool, w_down, w_proj):
    both = dot(split_rows(hsum[...]), w_down[...])
    pooled = ((ypool[...] + both[:IMGS] + both[IMGS:]) * (1.0 / POS)).astype(BF16)
    e = dot(pooled, w_proj[...])
    return (e * lax.rsqrt(jnp.sum(e * e, axis=-1, keepdims=True) + EPS)).astype(BF16)


GROUP, RANKS, CHIPS = 4, 32, 16
OWN, ROWS = 128, 512
CAPS, OWN_CAPS = 64, 16
BAND = 192
HALF = 384
MESH = pl.DeviceIdType.MESH
VEC = 1664


class Links:
    def __init__(self):
        self.dp, self.t = lax.axis_index("dp"), lax.axis_index("tensor")
        self.core, self.chip = lax.rem(self.dp, 2), self.dp // 2

    def rank(self, k):
        return lax.rem(self.t + k, GROUP)

    def group_peer(self, k):
        return {"dp": self.dp, "tensor": self.rank(k)}

    def rank_peer(self, k):
        return {"dp": lax.rem(self.dp + k, RANKS), "tensor": self.t}

    def chip_of(self, k):
        return lax.rem(self.chip + k, CHIPS)

    def chip_peer(self, k):
        return {"dp": 2 * self.chip_of(k) + self.core, "tensor": self.t}

    def sibling(self):
        return {"dp": self.dp + 1 - 2 * self.core, "tensor": self.t}

    def greet(self):
        barrier = pltpu.get_barrier_semaphore()
        for k in range(1, GROUP):
            pl.semaphore_signal(barrier, 1, device_id=self.group_peer(k), device_id_type=MESH)
        for k in range(1, RANKS):
            pl.semaphore_signal(barrier, 1, device_id=self.rank_peer(k), device_id_type=MESH)
        pl.semaphore_wait(barrier, GROUP - 1 + RANKS - 1)


def send(src, dst, sems, at, peer):
    copy = pltpu.make_async_remote_copy(
        src, dst, sems.at[0, at], sems.at[1, at], device_id=peer, device_id_type=MESH
    )
    copy.start()
    return copy


def finish(copies):
    for copy in copies:
        copy.wait()


def group_share(links, buf, sems):
    own = buf.at[links.t]
    return [send(own, own, sems, k - 1, links.group_peer(k)) for k in (2, 1, 3)]


def group_scatter(links, parts, landed, sems):
    return [send(parts.at[links.rank(k)], landed.at[k - 1], sems, k - 1, links.group_peer(k)) for k in (2, 1, 3)]


def rank_share(links, buf, sems):
    own = buf.at[links.dp]
    return [send(own, own, sems, k - 1, links.rank_peer(k)) for k in range(1, RANKS)]


def text_masks(seg_t, pad_t, bias, mem, mem_t):
    seg, pad = seg_t[...].astype(F32).astype(BF16), pad_t[...].astype(F32).astype(BF16)

    def as_column(values):
        pick = jnp.where(iota((ROWS, 32), 0) >> 4 == iota((ROWS, 32), 1), 1.0, 0.0).astype(BF16)
        wide = dot_t(pick, values)
        return jnp.sum(jnp.where(iota((ROWS, 16), 0) & 15 == iota((ROWS, 16), 1), wide, 0.0), axis=1, keepdims=True)

    def as_row(values):
        pick = jnp.where(iota((32, ROWS), 1) >> 4 == iota((32, ROWS), 0), 1.0, 0.0).astype(BF16)
        wide = dot(values, pick)
        return jnp.sum(jnp.where(iota((16, ROWS), 1) & 15 == iota((16, ROWS), 0), wide, 0.0), axis=0, keepdims=True)

    cap_col = as_column(seg) + ((iota((ROWS, 1), 0) >> 4) * 2).astype(F32)
    key_col = jnp.where(as_column(pad) > 0.5, cap_col, -1.0)
    cap_row = as_row(seg) + ((iota((1, ROWS), 1) >> 4) * 2).astype(F32)
    key_row = jnp.where(as_row(pad) > 0.5, cap_row, -1.0)
    for b in range(4):
        rows = slice(128 * b, 128 * b + 128)
        bias[b] = jnp.where(cap_col[rows] == key_row[:, rows], 0.0, NEG)
    mem[...] = jnp.where(iota((CAPS, ROWS), 0).astype(F32) == key_row, 1.0, 0.0).astype(BF16)
    mem_t[...] = jnp.where((iota((ROWS, 128), 1) & 63).astype(F32) == key_col, 1.0, 0.0).astype(BF16)


def text_norm_one(x, gain, a1, t):
    n, _ = normalized(x[...].astype(F32))
    a1[t] = (n * gain).astype(BF16)


def low_half():
    return iota((OWN, 128), 1) < 64


def stacked(values, low):
    zero = jnp.zeros_like(values)
    return jnp.concatenate([jnp.where(low, values, zero), jnp.where(low, zero, values)], axis=0)


def text_attention(a1, w_t, bias, w_out, qkv, probs, att, parts):
    rows_all = a1[...].reshape(ROWS, D)
    for j in range(3):
        qkv[j] = dot_t(rows_all, w_t[j]).astype(BF16)
    low = low_half()

    def soft(s):
        e = jnp.exp(s - jnp.max(s, axis=-1, keepdims=True))
        return e / jnp.sum(e, axis=-1, keepdims=True)

    for b in range(4):
        rows = slice(128 * b, 128 * b + 128)
        q, k, v = qkv[0, rows, :128], qkv[1, rows, :128], qkv[2, rows, :128]
        mask = bias[b]
        p = soft(dot_t(stacked(q, low), k) * 0.125 + jnp.concatenate([mask, mask], axis=0))
        probs[b, :256] = p
        o = dot(p.astype(BF16), v)
        att[rows, :128] = jnp.where(low, o[:128], o[128:]).astype(BF16)
        q, k, v = qkv[0, rows, 128:], qkv[1, rows, 128:], qkv[2, rows, 128:]
        p = soft(dot_t(q, k) * 0.125 + mask)
        probs[b, 256:] = p
        att[rows, 128:] = dot(p.astype(BF16), v).astype(BF16)
    parts[...] = dot(att[...], w_out[...]).astype(BF16).reshape(GROUP, OWN, D)


def summed(parts, landed, t):
    return parts[t].astype(F32) + landed[0].astype(F32) + landed[1].astype(F32) + landed[2].astype(F32)


def split3(x):
    hi = x.astype(BF16)
    rest = x - hi.astype(F32)
    mid = rest.astype(BF16)
    return jnp.concatenate([hi, mid, (rest - mid.astype(F32)).astype(BF16)], axis=0)


def own_member(mem, t):
    return mem[pl.ds(pl.multiple_of(t * OWN_CAPS, OWN_CAPS), OWN_CAPS), pl.ds(pl.multiple_of(t * OWN, OWN), OWN)]


def text_norm_two(x, parts, landed, gain, mem, x1, a2, x1_pool, t):
    y = x[...].astype(F32) + summed(parts, landed, t)
    x1[...] = y
    n, _ = normalized(y)
    a2[t] = (n * gain).astype(BF16)


def text_pool_one(x1, mem, x1_pool, t):
    own = own_member(mem, t)
    x1_pool[...] = dot(jnp.concatenate([own, own, own], axis=1), split3(x1[...]))


def text_up(a2, w_up, mem, w_down, dgelu, hsum, parts):
    def body(i, s):
        u = dot(a2[...].reshape(ROWS, D), w_up[:, s])
        phi, bell = normal_cdf(u)
        dgelu[:, s] = phi + u * bell * 0.3989422804014327
        hsum[:, s] = dot(mem[...], (u * phi).astype(BF16))

    tiles(3, body)
    both = dot(split_rows(hsum[...]), w_down[...])
    parts[...] = (both[:CAPS] + both[CAPS:]).reshape(GROUP, OWN_CAPS, D)


def counts_of(mem):
    return jnp.sum(mem.astype(F32), axis=1, keepdims=True)


def text_embed(parts, landed, x1_pool, mem, w_proj, tf, scale, emb, t):
    total = x1_pool[...] + parts[t] + landed[0] + landed[1] + landed[2]
    pooled = (total / counts_of(own_member(mem, t))).astype(BF16)
    e = dot(pooled, w_proj[...])
    rs = lax.rsqrt(jnp.sum(e * e, axis=-1, keepdims=True) + EPS)
    tf[...] = rs * e
    scale[...] = jnp.broadcast_to(rs, (OWN_CAPS, 128))
    emb[t, :OWN_CAPS] = (rs * e).astype(BF16)
    emb[t, OWN_CAPS:] = pooled


def score_sums(emb, images, s_ref, e_ref, row_sums, col_sums, t, dp):
    text = emb[:, :OWN_CAPS].reshape(CAPS, D)
    s = 40.0 * dot_t(text, images[...].reshape(ROWS, D))
    s_ref[...] = s
    e = jnp.exp(s - 40.0)
    e_ref[...] = e
    row_sums[t] = jnp.broadcast_to(jnp.sum(e, axis=1, keepdims=True), (CAPS, 128))
    col_sums[dp] = jnp.sum(e, axis=0, keepdims=True)


def score_grad(s_ref, e_ref, row_sums, col_sums, pair, images, parts, vec, t):
    rows = jnp.sum(row_sums[...], axis=0)[:, :1]
    cols = col_sums[0]
    for i in range(1, RANKS):
        cols = cols + col_sums[i]
    lane = iota((CAPS, ROWS), 1)
    target = jnp.where(pair[...].reshape(CAPS, 128)[:, :1] == (lane >> 4) * CAPS + OWN_CAPS * t + (lane & 15), 1.0, 0.0)
    g = 0.5 * (e_ref[...] / rows + e_ref[...] / cols) - target
    parts[...] = (40.0 * dot(g.astype(BF16), images[...].reshape(ROWS, D))).reshape(GROUP, OWN_CAPS, D)
    loss = (
        jnp.sum(40.0 + jnp.log(rows), axis=0, keepdims=True) * (1.0 / GROUP)
        + jnp.sum(40.0 + jnp.log(cols), axis=1, keepdims=True) * (1.0 / RANKS)
        - 2.0 * jnp.sum(jnp.sum(s_ref[...] * target, axis=1, keepdims=True), axis=0, keepdims=True)
    )
    vec[t, :, 1536:] = jnp.broadcast_to(loss, (1, 128))


def embed_grad(parts, landed, tf, scale, w_proj, mem, back, dx2, t):
    dt = parts[t] + landed[0] + landed[1] + landed[2]
    f = tf[...]
    de = (scale[:, :1] * (dt - f * jnp.sum(f * dt, axis=-1, keepdims=True))).astype(BF16)
    own = own_member(mem, t)
    gp = dot_t(de, w_proj[...]) / counts_of(own)
    back[t, :OWN_CAPS] = de
    back[t, OWN_CAPS:] = gp.astype(BF16)
    dx2[...] = t_dot(jnp.concatenate([own, own, own], axis=0), split3(gp))


def hidden_grad(back, w_down, mem_t, dgelu, du):
    dz = back[:, OWN_CAPS:].reshape(CAPS, D)
    dh = split_rows(dot_t(dz, w_down[...]))
    for i in range(3):
        s = slice(i * TILE, i * TILE + TILE)
        du[:, s] = (dot(mem_t[...], dh[:, s]) * dgelu[:, s]).astype(BF16)


def hidden_spread(du, w_up, parts):
    parts[...] = dot_t(du[...], w_up[...]).astype(BF16).reshape(GROUP, OWN, D)


def put_halves(g, first, count, rows, values):
    for j in range(2):
        g[j, first : first + count] = values[:, j * HALF : (j + 1) * HALF].reshape(count, rows, HALF).astype(BF16)


def down_proj_grad(hsum, back, emb, proj, g, t):
    dz = back[:, OWN_CAPS:].reshape(CAPS, D)
    hs = split_rows(hsum[...])
    dz2 = jnp.concatenate([dz, dz], axis=0)
    for i in range(3):
        put_halves(g, 4 * i, 4, 64, t_dot(hs[:, i * TILE : (i + 1) * TILE], dz2))
    proj[...] = t_dot(emb[:, OWN_CAPS:].reshape(CAPS, D), back[:, :OWN_CAPS].reshape(CAPS, D)).astype(BF16).reshape(GROUP, BAND, D)
    put_halves(g, 12, 3, 64, proj[t])
    g[:, 15] = jnp.zeros((2, 64, HALF), BF16)


def up_grad(a2, du, g):
    for i in range(2):
        rows = a2[:, :, i * HALF : (i + 1) * HALF].reshape(ROWS, HALF)
        put_halves(g, 8 * i, 8, 48, t_dot(rows, du[...]))


def norm_two_grad(parts, landed, x1, gain, dx2, dx1, dy, vec, t):
    da = summed(parts, landed, t)
    n, scale = normalized(x1[...])
    vec[t, :, 768:1536] = jnp.sum(da * n, axis=0, keepdims=True)
    h = da * gain
    g = dx2[...] + (h - jnp.mean(h, axis=-1, keepdims=True) - n * jnp.mean(h * n, axis=-1, keepdims=True)) * scale
    dx1[...] = g
    dy[t] = g.astype(BF16)


def attention_grad(dy, w_out, w_t, qkv, probs, dqkv, parts):
    datt = dot_t(dy[...].reshape(ROWS, D), w_out[...]).astype(BF16)
    low = low_half()

    def scores(p, d, v):
        dp = dot_t(d, v)
        return (p * (dp - jnp.sum(p * dp, axis=-1, keepdims=True))).astype(BF16)

    for b in range(4):
        rows = slice(128 * b, 128 * b + 128)
        q, k, v = stacked(qkv[0, rows, :128], low), qkv[1, rows, :128], qkv[2, rows, :128]
        d = stacked(datt[rows, :128], low)
        p = probs[b, :256]
        ds = scores(p, d, v)
        o = dot(ds, k)
        dqkv[0, rows, :128] = (jnp.where(low, o[:128], o[128:]) * 0.125).astype(BF16)
        dqkv[1, rows, :128] = (t_dot(ds, q) * 0.125).astype(BF16)
        dqkv[2, rows, :128] = t_dot(p.astype(BF16), d).astype(BF16)
        q, k, v = qkv[0, rows, 128:], qkv[1, rows, 128:], qkv[2, rows, 128:]
        d = datt[rows, 128:]
        p = probs[b, 256:]
        ds = scores(p, d, v)
        dqkv[0, rows, 128:] = (dot(ds, k) * 0.125).astype(BF16)
        dqkv[1, rows, 128:] = (t_dot(ds, q) * 0.125).astype(BF16)
        dqkv[2, rows, 128:] = t_dot(p.astype(BF16), d).astype(BF16)
    total = dot(dqkv[0], w_t[0]) + dot(dqkv[1], w_t[1]) + dot(dqkv[2], w_t[2])
    parts[...] = total.astype(BF16).reshape(GROUP, OWN, D)


def out_qkv_grad(att, dy, dqkv, a1, g):
    put_halves(g, 0, 4, 48, t_dot(att[...], dy[...].reshape(ROWS, D)))
    for j in range(3):
        put_halves(g, 4 + 4 * j, 4, 48, t_dot(dqkv[j], a1[...].reshape(ROWS, D)))


def norm_one_grad(parts, landed, x, gain, dx1, out, vec, t):
    da = summed(parts, landed, t)
    n, scale = normalized(x[...].astype(F32))
    vec[t, :, :768] = jnp.sum(da * n, axis=0, keepdims=True)
    h = da * gain
    out[...] = dx1[...] + (h - jnp.mean(h, axis=-1, keepdims=True) - n * jnp.mean(h * n, axis=-1, keepdims=True)) * scale


class Reduction:
    def __init__(self, links, g, met, landed, full, sems):
        self.links, self.g, self.met, self.landed, self.full, self.sems = links, g, met, landed, full, sems

    def cores(self):
        other = 1 - self.links.core
        self.copies = [send(self.g.at[other], self.met, self.sems, 0, self.links.sibling())]

    def scatter(self):
        finish(self.copies)
        core = self.links.core
        self.met[...] = (self.g[core].astype(F32) + self.met[...].astype(F32)).astype(BF16)
        self.copies = [
            send(self.met.at[self.links.chip_of(k)], self.landed.at[k - 1], self.sems, k, self.links.chip_peer(k))
            for k in range(1, CHIPS)
        ]

    def gather(self):
        finish(self.copies)
        total = self.met[self.links.chip].astype(F32)
        for k in range(CHIPS - 1):
            total = total + self.landed[k].astype(F32)
        core, chip = self.links.core, self.links.chip
        self.full[core, chip] = total.astype(BF16)
        own = self.full.at[core, chip]
        self.copies = [send(own, own, self.sems, 15 + k, self.links.chip_peer(k)) for k in range(1, CHIPS)]

    def share(self):
        finish(self.copies)
        own = self.full.at[self.links.core]
        self.copies = [send(own, own, self.sems, 31, self.links.sibling())]

    def done(self):
        finish(self.copies)


def body(
    x, seg_t, pad_t, pair_in, gain_one, gain_two, img_gain_one, img_gain_two,
    h_tok, h_iqkv, h_iout, h_iup, h_idown, h_iproj, h_qkv, h_out, h_up, h_down, h_proj,
    o_loss, o_input, o_norms, o_a, o_b, o_c, o_proj,
    tok, iw_qkv, iw_out, iw_up, iw_down, iw_proj, w_qkv, w_out, w_up, w_down, w_proj, load,
    perm, back, ibias, ia, iap, iqkv, iy, ypool, ihsum, images,
    bias, mem, mem_t, pair, a1, qkv, probs, att, p_att, l_att, x1, x1_pool, a2, dgelu, hsum, p_pool, l_pool,
    tf, scale, emb, s_ref, e_ref, row_sums, col_sums, p_dt, l_dt, d_back, dx2, du, p_da2, l_da2, dx1, dy,
    dqkv, p_da1, l_da1, proj, proj_all, vec, vec_all,
    g_a, g_b, g_c, m_a, m_b, m_c, r_a, r_b, r_c, f_a, f_b, f_c,
    group_sems, rank_sems, sum_sems, proj_sems, store,
):
    links = Links()
    t, dp = links.t, links.dp
    loads = {}
    for i, (name, src, dst) in enumerate((
        ("tok", h_tok, tok), ("iqkv", h_iqkv, iw_qkv), ("qkv", h_qkv, w_qkv), ("out", h_out, w_out), ("iout", h_iout, iw_out),
        ("iup", h_iup, iw_up), ("up", h_up, w_up), ("down", h_down, w_down), ("idown", h_idown, iw_down),
        ("iproj", h_iproj, iw_proj), ("proj", h_proj, w_proj),
    )):
        loads[name] = pltpu.make_async_copy(src, dst, load.at[i])
        loads[name].start()

    links.greet()
    pair[t] = pair_in[...]
    pair_copies = group_share(links, pair, group_sems.at[0])
    text_norm_one(x, gain_one[...], a1, t)
    copies = group_share(links, a1, group_sems.at[1])

    text_masks(seg_t, pad_t, bias, mem, mem_t)
    image_masks(perm, back, ibias)
    loads["tok"].wait()
    image_norm_one(tok, img_gain_one[...], ia)
    image_permute(perm, ia, iap)
    loads["iqkv"].wait()
    image_qkv(iap, iw_qkv, iqkv)

    finish(copies)
    loads["qkv"].wait()
    loads["out"].wait()
    text_attention(a1, w_qkv, bias, w_out, qkv, probs, att, p_att)
    copies = group_scatter(links, p_att, l_att, group_sems.at[2])

    image_attention(iqkv, ibias, iap, 0, 8)

    finish(copies)
    text_norm_two(x, p_att, l_att, gain_two[...], mem, x1, a2, x1_pool, t)
    copies = group_share(links, a2, group_sems.at[3])
    text_pool_one(x1, mem, x1_pool, t)

    loads["iout"].wait()
    image_out(back, iap, ia, tok, iw_out, iy)
    image_norm_two(iy, img_gain_two[...], ia, ypool)
    loads["iup"].wait()
    image_up(ia, iw_up, ihsum, 0, 6)

    finish(copies)
    loads["up"].wait()
    loads["down"].wait()
    text_up(a2, w_up, mem, w_down, dgelu, hsum, p_pool)
    copies = group_scatter(links, p_pool, l_pool, group_sems.at[4])

    image_up(ia, iw_up, ihsum, 6, 12)
    loads["idown"].wait()
    loads["iproj"].wait()
    images[dp] = image_finish(ihsum, ypool, iw_down, iw_proj)
    image_copies = rank_share(links, images, rank_sems.at[0])

    finish(copies)
    loads["proj"].wait()
    text_embed(p_pool, l_pool, x1_pool, mem, w_proj, tf, scale, emb, t)
    finish(group_share(links, emb, group_sems.at[5]))
    finish(image_copies)
    finish(pair_copies)

    score_sums(emb, images, s_ref, e_ref, row_sums, col_sums, t, dp)
    row_copies = group_share(links, row_sums, group_sems.at[6])
    finish(rank_share(links, col_sums, rank_sems.at[1]))
    finish(row_copies)
    score_grad(s_ref, e_ref, row_sums, col_sums, pair, images, p_dt, vec, t)
    finish(group_scatter(links, p_dt, l_dt, group_sems.at[7]))
    embed_grad(p_dt, l_dt, tf, scale, w_proj, mem, d_back, dx2, t)
    finish(group_share(links, d_back, group_sems.at[8]))

    red_a = Reduction(links, g_a, m_a, r_a, f_a, sum_sems.at[0])
    red_b = Reduction(links, g_b, m_b, r_b, f_b, sum_sems.at[1])
    red_c = Reduction(links, g_c, m_c, r_c, f_c, sum_sems.at[2])

    hidden_grad(d_back, w_down, mem_t, dgelu, du)
    hidden_spread(du, w_up, p_da2)
    copies = group_scatter(links, p_da2, l_da2, group_sems.at[9])
    down_proj_grad(hsum, d_back, emb, proj, g_a, t)
    red_a.cores()
    up_grad(a2, du, g_b)
    red_b.cores()
    red_a.scatter()
    finish(copies)
    norm_two_grad(p_da2, l_da2, x1, gain_two[...], dx2, dx1, dy, vec, t)
    copies = group_share(links, dy, group_sems.at[10])
    red_b.scatter()
    finish(copies)
    attention_grad(dy, w_out, w_qkv, qkv, probs, dqkv, p_da1)
    copies = group_scatter(links, p_da1, l_da1, group_sems.at[11])
    out_qkv_grad(att, dy, dqkv, a1, g_c)
    red_c.cores()
    red_a.gather()
    red_b.gather()
    red_c.scatter()
    finish(copies)
    norm_one_grad(p_da1, l_da1, x, gain_one[...], dx1, o_input, vec, t)
    vec_copies = group_share(links, vec, group_sems.at[12])
    red_a.share()
    red_b.share()
    core = links.core
    proj_all[core, t] = f_a[core, 12:15]
    own = proj_all.at[core, t]
    proj_copies = [send(own, own, proj_sems, k, links.group_peer(k)) for k in (2, 1, 3)]
    red_c.gather()
    finish(vec_copies)
    vec_all[dp] = vec[0] + vec[1] + vec[2] + vec[3]
    vec_copies = rank_share(links, vec_all, rank_sems.at[2])
    finish(proj_copies)
    own = proj_all.at[core]
    proj_copies = [send(own, own, proj_sems, 0, links.sibling())]
    red_a.done()
    red_b.done()
    stores = [pltpu.make_async_copy(f_a, o_a, store.at[0]), pltpu.make_async_copy(f_b, o_b, store.at[1])]
    for copy in stores:
        copy.start()
    finish(vec_copies)
    total = vec_all[0]
    for i in range(1, RANKS):
        total = total + vec_all[i]
    o_norms[...] = total[:, :1536]
    o_loss[...] = total[:, 1536:] * (1.0 / 4096.0)
    finish(proj_copies)
    stores.append(pltpu.make_async_copy(proj_all, o_proj, store.at[2]))
    stores[-1].start()
    red_c.share()
    red_c.done()
    stores.append(pltpu.make_async_copy(f_c, o_c, store.at[3]))
    stores[-1].start()
    for copy in stores:
        copy.wait()


def on_device(
    text_input, segment_ids, pad_mask, pairing, ln_first, w_qkv, w_out, ln_second, w_up, w_down, text_proj,
    image_tokens, img_ln_first, img_w_qkv, img_w_out, img_ln_second, img_w_up, img_w_down, img_proj,
):
    vmem = pl.BlockSpec(memory_space=VM)
    hbm = pl.BlockSpec(memory_space=pl.ANY)
    shape = jax.ShapeDtypeStruct
    sums = ((16, 64, HALF), (16, 48, HALF), (16, 48, HALF))
    dma = pltpu.SemaphoreType.DMA
    scratch = [
        VM((IROWS, D), BF16), VM((3, D, D), BF16), VM((D, D), BF16), VM((D, FF), BF16), VM((FF, D), BF16), VM((D, D), BF16),
        VM((3, BAND, D), BF16), VM((BAND, D), BF16), VM((D, HID), BF16), VM((HID, D), BF16), VM((D, D), BF16), dma((11,)),
        VM((PROWS, IROWS), BF16), VM((IROWS, PROWS), BF16), VM((2 * PAIR, PAIR), F32), VM((IROWS, D), BF16), VM((PROWS, D), BF16),
        VM((3, PROWS, D), BF16), VM((IROWS, D), F32), VM((IMGS, D), F32),
        VM((IMGS, FF), F32), VM((RANKS, IMGS, D), BF16),
        VM((4, 128, 128), F32), VM((CAPS, ROWS), BF16), VM((ROWS, 128), BF16), VM((GROUP, OWN_CAPS, 128), I32),
        VM((GROUP, OWN, D), BF16), VM((3, ROWS, BAND), BF16), VM((4, HALF, 128), F32), VM((ROWS, BAND), BF16),
        VM((GROUP, OWN, D), BF16), VM((3, OWN, D), BF16), VM((OWN, D), F32), VM((OWN_CAPS, D), F32), VM((GROUP, OWN, D), BF16),
        VM((ROWS, HID), F32), VM((CAPS, HID), F32), VM((GROUP, OWN_CAPS, D), F32), VM((3, OWN_CAPS, D), F32),
        VM((OWN_CAPS, D), F32), VM((OWN_CAPS, 128), F32), VM((GROUP, 2 * OWN_CAPS, D), BF16), VM((CAPS, ROWS), F32),
        VM((CAPS, ROWS), F32), VM((GROUP, CAPS, 128), F32), VM((RANKS, 1, ROWS), F32), VM((GROUP, OWN_CAPS, D), F32),
        VM((3, OWN_CAPS, D), F32), VM((GROUP, 2 * OWN_CAPS, D), BF16),
        VM((OWN, D), F32), VM((ROWS, HID), BF16), VM((GROUP, OWN, D), BF16), VM((3, OWN, D), BF16), VM((OWN, D), F32),
        VM((GROUP, OWN, D), BF16), VM((3, ROWS, BAND), BF16), VM((GROUP, OWN, D), BF16), VM((3, OWN, D), BF16),
        VM((GROUP, BAND, D), BF16), VM((2, GROUP, 3, 64, HALF), BF16), VM((GROUP, 1, VEC), F32), VM((RANKS, 1, VEC), F32),
    ]
    scratch += [VM((2,) + s, BF16) for s in sums] + [VM(s, BF16) for s in sums]
    scratch += [VM((15,) + s[1:], BF16) for s in sums] + [VM((2,) + s, BF16) for s in sums]
    scratch += [dma((13, 2, 3)), dma((3, 2, 31)), dma((3, 2, 32)), dma((2, 4)), dma((4,))]
    loss, input_grad, norms, full_a, full_b, full_c, full_proj = pl.pallas_call(
        body,
        out_shape=(
            shape((1, 128), F32), shape((OWN, D), F32), shape((1, 1536), F32),
            *(shape((2,) + s, BF16) for s in sums), shape((2, GROUP, 3, 64, HALF), BF16),
        ),
        in_specs=[vmem] * 8 + [hbm] * 11,
        out_specs=(vmem, vmem, vmem, hbm, hbm, hbm, hbm),
        scratch_shapes=scratch,
        compiler_params=pltpu.CompilerParams(collective_id=0, has_side_effects=True, vmem_limit_bytes=63 << 20),
        name="lit",
    )(
        text_input, segment_ids.T, pad_mask.T, jnp.broadcast_to(pairing[:, None], (OWN_CAPS, 128)),
        ln_first[None], ln_second[None], img_ln_first[None], img_ln_second[None],
        image_tokens.transpose(1, 0, 2).reshape(IROWS, D), img_w_qkv, img_w_out, img_w_up, img_w_down, img_proj,
        w_qkv.swapaxes(1, 2), w_out, w_up, w_down, text_proj,
    )

    def wide(full, first, last):
        rows = (last - first) * full.shape[2]
        return jnp.concatenate([full[j, first:last].reshape(rows, HALF) for j in range(2)], axis=1).astype(F32)

    proj = jnp.concatenate([full_proj[j].reshape(D, HALF) for j in range(2)], axis=1).astype(F32)
    qkv = wide(full_c, 4, 16).reshape(3, BAND, D).swapaxes(1, 2)
    return (
        loss[0, 0], input_grad, norms[0, :D], qkv, wide(full_c, 0, 4), norms[0, D:], wide(full_b, 0, 16),
        wide(full_a, 0, 12), proj,
    )


def solution(mesh):
    rows = P(("dp", "tensor"))
    in_specs = (
        P(("dp", "tensor"), None), P("dp", None), P("dp", None), rows, P(), P(None, None, "tensor"), P("tensor", None), P(),
        P(None, "tensor"), P("tensor", None), P(), P(("dp", "tensor"), None, None), P(), P(), P(), P(), P(), P(), P(),
    )
    out_specs = (
        P(), P(("dp", "tensor"), None), P(), P(None, None, "tensor"), P("tensor", None), P(), P(None, "tensor"),
        P("tensor", None), P(),
    )
    return jax.shard_map(on_device, mesh=mesh, in_specs=in_specs, out_specs=out_specs, check_vma=False)
```

```python
import jax, jax.numpy as jnp
from jax import lax
from jax.experimental import pallas as pl
from jax.experimental.pallas import tpu as pltpu
from jax.sharding import PartitionSpec as P

F32, BF16, I32 = jnp.float32, jnp.bfloat16, jnp.int32
VM = pltpu.VMEM
EPS = 1e-6
NEG = -1e30
D, FF, HID = 768, 3072, 768
IMGS, POS = 16, 50
IROWS = IMGS * POS
PAIR = 112
PROWS = PAIR * (IMGS // 2)
TILE = 256


def dot(a, b):
    return jnp.dot(a, b, preferred_element_type=F32)


def dot_t(a, b):
    return lax.dot_general(a, b, (((1,), (1,)), ((), ())), preferred_element_type=F32)


def t_dot(a, b):
    return lax.dot_general(a, b, (((0,), (0,)), ((), ())), preferred_element_type=F32)


def iota(shape, axis):
    return lax.broadcasted_iota(I32, shape, axis)


def normalized(values):
    centred = values - jnp.mean(values, axis=-1, keepdims=True)
    spread = jnp.mean(centred * centred, axis=-1, keepdims=True)
    scale = lax.rsqrt(spread + EPS)
    return centred * scale, scale


def normal_cdf(u):
    bell = jnp.exp(u * u * -0.5)
    t = 1.0 / (1.0 + (0.3275911 * 0.7071067811865476) * jnp.abs(u))
    poly = t * (0.5 * 0.254829592 + t * (0.5 * -0.284496736 + t * (0.5 * 1.421413741 + t * (0.5 * -1.453152027 + t * (0.5 * 1.061405429)))))
    tail = poly * bell
    return jnp.where(u < 0.0, tail, 1.0 - tail), bell


def image_masks(perm, back, bias):
    lanes = iota((PAIR, IROWS), 1)
    w = iota((PAIR, IROWS), 0)
    second = (w >= POS).astype(I32)
    for p in range(IMGS // 2):
        src = jnp.where(w < 2 * POS, (w - POS * second) * IMGS + 2 * p + second, -1)
        perm[pl.ds(p * PAIR, PAIR), :] = jnp.where(src == lanes, 1.0, 0.0).astype(BF16)

    def rows(i, c):
        r = i * 160 + iota((160, PROWS), 0)
        img, pos = r & 15, r >> 4
        col = (img >> 1) * PAIR + (img & 1) * POS + pos
        back[pl.ds(pl.multiple_of(i * 160, 160), 160), :] = jnp.where(col == iota((160, PROWS), 1), 1.0, 0.0).astype(BF16)
        return c

    lax.fori_loop(0, 5, rows, 0)
    q = iota((2 * PAIR, PAIR), 0)
    q = jnp.where(q >= PAIR, q - PAIR, q)
    k = iota((2 * PAIR, PAIR), 1)
    bias[...] = jnp.where(((q >= POS) == (k >= POS)) & (k < 2 * POS), 0.0, NEG)


def image_norm_one(tok, gain, ia):
    def rows(i, c):
        s = pl.ds(pl.multiple_of(i * 160, 160), 160)
        n, _ = normalized(tok[s, :].astype(F32))
        ia[s, :] = (n * gain).astype(BF16)
        return c

    lax.fori_loop(0, 5, rows, 0)


def tiles(n, body):
    def step(i, c):
        body(i, pl.ds(pl.multiple_of(i * TILE, TILE), TILE))
        return c

    lax.fori_loop(0, n, step, 0)


def image_permute(perm, ia, iap):
    def body(i, s):
        iap[:, s] = dot(perm[...], ia[:, s]).astype(BF16)

    tiles(3, body)


def image_qkv(iap, w, iqkv):
    for j in range(3):
        def body(i, s):
            iqkv[j, :, s] = dot(iap[...], w[j, :, s]).astype(BF16)

        tiles(3, body)


def image_attention(iqkv, bias, iatt, first, last):
    low = iota((PAIR, 128), 1) < 64

    def pair(p, c):
        rows = pl.ds(pl.multiple_of(p * PAIR, PAIR), PAIR)
        ones = jnp.ones((PAIR, 128), BF16)
        zero = jnp.zeros((PAIR, 128), BF16)
        for h in range(6):
            cols = pl.ds(h * 128, 128)
            q, k, v = iqkv[0, rows, cols], iqkv[1, rows, cols], iqkv[2, rows, cols]
            q2 = jnp.concatenate([jnp.where(low, q, zero), jnp.where(low, zero, q)], axis=0)
            s = dot_t(q2, k) * 0.125 + bias[...]
            e = jnp.exp(s - jnp.max(s, axis=-1, keepdims=True)).astype(BF16)
            o = dot(e, jnp.concatenate([v, ones], axis=1))
            o = o[:, :128] / o[:, 128:]
            iatt[rows, cols] = jnp.where(low, o[:PAIR], o[PAIR:]).astype(BF16)
        return c

    lax.fori_loop(first, last, pair, 0)


def image_out(back, iatt, spare, tok, w, iy):
    def body(i, s):
        spare[:, s] = dot(back[...], iatt[:, s]).astype(BF16)

    tiles(3, body)

    def body2(i, s):
        iy[:, s] = tok[:, s].astype(F32) + dot(spare[...], w[:, s])

    tiles(3, body2)


def image_norm_two(iy, gain, ia, ypool):
    ypool[...] = jnp.zeros_like(ypool)

    def rows(i, c):
        s = pl.ds(pl.multiple_of(i * 160, 160), 160)
        y = iy[s, :]
        ypool[...] += jnp.sum(y.reshape(10, IMGS, D), axis=0)
        n, _ = normalized(y)
        ia[s, :] = (n * gain).astype(BF16)
        return c

    lax.fori_loop(0, 5, rows, 0)


def image_up(ia, w, hsum, first, last):
    def step(i, c):
        s = pl.ds(pl.multiple_of(i * TILE, TILE), TILE)
        u = dot(ia[...], w[:, s])
        phi, _ = normal_cdf(u)
        hsum[:, s] = jnp.sum((u * phi).reshape(POS, IMGS, TILE), axis=0)
        return c

    lax.fori_loop(first, last, step, 0)


def as_row(gain):
    return gain[...].reshape(1, D)


def column(values):
    rows = iota((OWN_CAPS, 128), 0)
    out = jnp.zeros((OWN_CAPS, 128), I32)
    for i in range(OWN_CAPS):
        out = jnp.where(rows == i, values[i], out)
    return out


def split_rows(x):
    hi = x.astype(BF16)
    return jnp.concatenate([hi, (x - hi.astype(F32)).astype(BF16)], axis=0)


def image_finish(hsum, ypool, w_down, w_proj):
    both = dot(split_rows(hsum[...]), w_down[...])
    pooled = ((ypool[...] + both[:IMGS] + both[IMGS:]) * (1.0 / POS)).astype(BF16)
    e = dot(pooled, w_proj[...])
    return (e * lax.rsqrt(jnp.sum(e * e, axis=-1, keepdims=True) + EPS)).astype(BF16)


GROUP, RANKS, CHIPS = 4, 32, 16
OWN, ROWS = 128, 512
CAPS, OWN_CAPS = 64, 16
BAND = 192
HALF = 384
MESH = pl.DeviceIdType.MESH
VEC = 1664


class Links:
    def __init__(self):
        self.dp, self.t = lax.axis_index("dp"), lax.axis_index("tensor")
        self.core, self.chip = lax.rem(self.dp, 2), self.dp // 2
        self.place = {"x": lax.rem(self.chip, 4), "z": self.chip // 4}

    def rank(self, k):
        return lax.rem(self.t + k, GROUP)

    def group_peer(self, k):
        return {"dp": self.dp, "tensor": self.rank(k)}

    def rank_peer(self, k):
        return {"dp": lax.rem(self.dp + k, RANKS), "tensor": self.t}

    def chip_of(self, k):
        return lax.rem(self.chip + k, CHIPS)

    def chip_peer(self, k):
        return {"dp": 2 * self.chip_of(k) + self.core, "tensor": self.t}

    def axis_rank(self, axis, k):
        return lax.rem(self.place[axis] + k, 4)

    def axis_peer(self, axis, k):
        place = dict(self.place)
        place[axis] = self.axis_rank(axis, k)
        return {"dp": 2 * (place["z"] * 4 + place["x"]) + self.core, "tensor": self.t}

    def sibling(self):
        return {"dp": self.dp + 1 - 2 * self.core, "tensor": self.t}

    def greet(self):
        barrier = pltpu.get_barrier_semaphore()
        for k in range(1, GROUP):
            pl.semaphore_signal(barrier, 1, device_id=self.group_peer(k), device_id_type=MESH)
        for k in range(1, RANKS):
            pl.semaphore_signal(barrier, 1, device_id=self.rank_peer(k), device_id_type=MESH)
        pl.semaphore_wait(barrier, GROUP - 1 + RANKS - 1)


def send(src, dst, sems, at, peer):
    copy = pltpu.make_async_remote_copy(
        src, dst, sems.at[0, at], sems.at[1, at], device_id=peer, device_id_type=MESH
    )
    copy.start()
    return copy


def finish(copies):
    for copy in copies:
        copy.wait()


def group_share(links, buf, sems):
    own = buf.at[links.t]
    return [send(own, own, sems, k - 1, links.group_peer(k)) for k in (2, 1, 3)]


def group_scatter(links, parts, landed, sems):
    return [send(parts.at[links.rank(k)], landed.at[k - 1], sems, k - 1, links.group_peer(k)) for k in (2, 1, 3)]


def rank_share(links, buf, sems):
    own = buf.at[links.dp]
    return [send(own, own, sems, k - 1, links.rank_peer(k)) for k in range(1, RANKS)]


def text_masks(seg_t, pad_t, bias, mem, mem_t):
    seg, pad = seg_t[...].astype(F32).astype(BF16), pad_t[...].astype(F32).astype(BF16)

    def as_column(values):
        pick = jnp.where(iota((ROWS, 32), 0) >> 4 == iota((ROWS, 32), 1), 1.0, 0.0).astype(BF16)
        wide = dot_t(pick, values)
        return jnp.sum(jnp.where(iota((ROWS, 16), 0) & 15 == iota((ROWS, 16), 1), wide, 0.0), axis=1, keepdims=True)

    def as_row(values):
        pick = jnp.where(iota((32, ROWS), 1) >> 4 == iota((32, ROWS), 0), 1.0, 0.0).astype(BF16)
        wide = dot(values, pick)
        return jnp.sum(jnp.where(iota((16, ROWS), 1) & 15 == iota((16, ROWS), 0), wide, 0.0), axis=0, keepdims=True)

    cap_col = as_column(seg) + ((iota((ROWS, 1), 0) >> 4) * 2).astype(F32)
    key_col = jnp.where(as_column(pad) > 0.5, cap_col, -1.0)
    cap_row = as_row(seg) + ((iota((1, ROWS), 1) >> 4) * 2).astype(F32)
    key_row = jnp.where(as_row(pad) > 0.5, cap_row, -1.0)
    for b in range(4):
        rows = slice(128 * b, 128 * b + 128)
        bias[b] = jnp.where(cap_col[rows] == key_row[:, rows], 0.0, NEG)
    mem[...] = jnp.where(iota((CAPS, ROWS), 0).astype(F32) == key_row, 1.0, 0.0).astype(BF16)
    mem_t[...] = jnp.where((iota((ROWS, 128), 1) & 63).astype(F32) == key_col, 1.0, 0.0).astype(BF16)


def text_norm_one(x, gain, a1, t):
    n, _ = normalized(x[...].astype(F32))
    a1[t] = (n * gain).astype(BF16)


def low_half():
    return iota((OWN, 128), 1) < 64


def stacked(values, low):
    zero = jnp.zeros_like(values)
    return jnp.concatenate([jnp.where(low, values, zero), jnp.where(low, zero, values)], axis=0)


def text_attention(a1, w_t, bias, w_out, qkv, probs, att, parts):
    rows_all = a1[...].reshape(ROWS, D)
    for j in range(3):
        qkv[j] = dot_t(rows_all, w_t[j]).astype(BF16)
    low = low_half()

    def soft(s):
        e = jnp.exp(s - jnp.max(s, axis=-1, keepdims=True))
        return e / jnp.sum(e, axis=-1, keepdims=True)

    for b in range(4):
        rows = slice(128 * b, 128 * b + 128)
        q, k, v = qkv[0, rows, :128], qkv[1, rows, :128], qkv[2, rows, :128]
        mask = bias[b]
        p = soft(dot_t(stacked(q, low), k) * 0.125 + jnp.concatenate([mask, mask], axis=0))
        probs[b, :256] = p
        o = dot(p.astype(BF16), v)
        att[rows, :128] = jnp.where(low, o[:128], o[128:]).astype(BF16)
        q, k, v = qkv[0, rows, 128:], qkv[1, rows, 128:], qkv[2, rows, 128:]
        p = soft(dot_t(q, k) * 0.125 + mask)
        probs[b, 256:] = p
        att[rows, 128:] = dot(p.astype(BF16), v).astype(BF16)
    parts[...] = dot(att[...], w_out[...]).astype(BF16).reshape(GROUP, OWN, D)


def summed(parts, landed, t):
    return parts[t].astype(F32) + landed[0].astype(F32) + landed[1].astype(F32) + landed[2].astype(F32)


def split3(x):
    hi = x.astype(BF16)
    rest = x - hi.astype(F32)
    mid = rest.astype(BF16)
    return jnp.concatenate([hi, mid, (rest - mid.astype(F32)).astype(BF16)], axis=0)


def own_member(mem, t):
    return mem[pl.ds(pl.multiple_of(t * OWN_CAPS, OWN_CAPS), OWN_CAPS), pl.ds(pl.multiple_of(t * OWN, OWN), OWN)]


def text_norm_two(x, parts, landed, gain, mem, x1, a2, x1_pool, t):
    y = x[...].astype(F32) + summed(parts, landed, t)
    x1[...] = y
    n, _ = normalized(y)
    a2[t] = (n * gain).astype(BF16)


def text_pool_one(x1, mem, x1_pool, t):
    own = own_member(mem, t)
    x1_pool[...] = dot(jnp.concatenate([own, own, own], axis=1), split3(x1[...]))


def text_up(a2, w_up, mem, w_down, dgelu, hsum, parts):
    def body(i, s):
        u = dot(a2[...].reshape(ROWS, D), w_up[:, s])
        phi, bell = normal_cdf(u)
        dgelu[:, s] = phi + u * bell * 0.3989422804014327
        hsum[:, s] = dot(mem[...], (u * phi).astype(BF16))

    tiles(3, body)
    both = dot(split_rows(hsum[...]), w_down[...])
    parts[...] = (both[:CAPS] + both[CAPS:]).reshape(GROUP, OWN_CAPS, D)


def counts_of(mem):
    return jnp.sum(mem.astype(F32), axis=1, keepdims=True)


def text_pool(parts, landed, x1_pool, mem, pooled, t):
    total = x1_pool[...] + parts[t] + landed[0] + landed[1] + landed[2]
    pooled[t] = (total / counts_of(own_member(mem, t))).astype(BF16)


def text_embed(pooled, w_proj, tf, scale):
    e = dot(pooled[...].reshape(CAPS, D), w_proj[...])
    rs = lax.rsqrt(jnp.sum(e * e, axis=-1, keepdims=True) + EPS)
    tf[...] = rs * e
    scale[...] = jnp.broadcast_to(rs, (CAPS, 128))


def score_sums(tf, images, s_ref, e_ref, row_sums, col_sums, t, dp):
    s = 40.0 * dot_t(tf[...].astype(BF16), images[...].reshape(ROWS, D))
    s_ref[...] = s
    e = jnp.exp(s - 40.0)
    e_ref[...] = e
    row_sums[t] = jnp.broadcast_to(jnp.sum(e, axis=1, keepdims=True), (CAPS, 128))
    col_sums[dp] = jnp.sum(e, axis=0, keepdims=True)


def score_grad(s_ref, e_ref, row_sums, col_sums, pair, images, dts, vec, t):
    rows = jnp.sum(row_sums[...], axis=0)[:, :1]
    cols = col_sums[0]
    for i in range(1, RANKS):
        cols = cols + col_sums[i]
    lane = iota((CAPS, ROWS), 1)
    image = ((lane >> 4) & 15) * (2 * CAPS) + (lane >> 8) * CAPS + (lane & 15) + OWN_CAPS * t
    target = jnp.where(pair[...].reshape(CAPS, 128)[:, :1] == image, 1.0, 0.0)
    g = 0.5 * (e_ref[...] / rows + e_ref[...] / cols) - target
    dts[t] = (40.0 * dot(g.astype(BF16), images[...].reshape(ROWS, D))).astype(BF16)
    loss = (
        jnp.sum(40.0 + jnp.log(rows), axis=0, keepdims=True) * (1.0 / GROUP)
        + jnp.sum(40.0 + jnp.log(cols), axis=1, keepdims=True) * (1.0 / RANKS)
        - 2.0 * jnp.sum(jnp.sum(s_ref[...] * target, axis=1, keepdims=True), axis=0, keepdims=True)
    )
    vec[t, :, 1536:] = jnp.broadcast_to(loss, (1, 128))


def embed_grad(dts, tf, scale, w_proj, mem, de_ref, dz_ref, gp_ref):
    dt = dts[0].astype(F32) + dts[1].astype(F32) + dts[2].astype(F32) + dts[3].astype(F32)
    f = tf[...]
    de = (scale[:, :1] * (dt - f * jnp.sum(f * dt, axis=-1, keepdims=True))).astype(BF16)
    gp = dot_t(de, w_proj[...]) / counts_of(mem[...])
    de_ref[...] = de
    gp_ref[...] = gp
    dz_ref[...] = gp.astype(BF16)


def row_grad(gp_ref, mem, dx2, t):
    own = own_member(mem, t)
    gp = gp_ref[pl.ds(pl.multiple_of(t * OWN_CAPS, OWN_CAPS), OWN_CAPS), :]
    dx2[...] = t_dot(jnp.concatenate([own, own, own], axis=0), split3(gp))


def hidden_grad(dz, w_down, mem_t, dgelu, du):
    dh = split_rows(dot_t(dz[...], w_down[...]))
    for i in range(3):
        s = slice(i * TILE, i * TILE + TILE)
        du[:, s] = (dot(mem_t[...], dh[:, s]) * dgelu[:, s]).astype(BF16)


def hidden_spread(du, w_up, parts):
    parts[...] = dot_t(du[...], w_up[...]).astype(BF16).reshape(GROUP, OWN, D)


def put_halves(g, first, count, rows, values):
    for j in range(2):
        part = values[:, j * HALF : (j + 1) * HALF].reshape(count, rows, HALF).astype(BF16)
        if len(g.shape) == 4:
            g[j, first : first + count] = part
        elif count == 3:
            g[j, first // 4, :3] = part
        else:
            g[j, first // 4 : (first + count) // 4] = part.reshape(count // 4, 4, rows, HALF)


def down_proj_grad(hsum, dz, de, pooled, proj, g, t):
    hs = split_rows(hsum[...])
    dz2 = jnp.concatenate([dz[...], dz[...]], axis=0)
    for i in range(3):
        put_halves(g, 4 * i, 4, 64, t_dot(hs[:, i * TILE : (i + 1) * TILE], dz2))
    proj[...] = t_dot(pooled[...].reshape(CAPS, D), de[...]).astype(BF16).reshape(GROUP, BAND, D)
    put_halves(g, 12, 3, 64, proj[t])
    g[:, 3, 3] = jnp.zeros((2, 64, HALF), BF16)


def up_grad(a2, du, g):
    for i in range(2):
        rows = a2[:, :, i * HALF : (i + 1) * HALF].reshape(ROWS, HALF)
        put_halves(g, 8 * i, 8, 48, t_dot(rows, du[...]))


def norm_two_grad(parts, landed, x1, gain, dx2, dx1, dy, vec, t):
    da = summed(parts, landed, t)
    n, scale = normalized(x1[...])
    vec[t, :, 768:1536] = jnp.sum(da * n, axis=0, keepdims=True)
    h = da * gain
    g = dx2[...] + (h - jnp.mean(h, axis=-1, keepdims=True) - n * jnp.mean(h * n, axis=-1, keepdims=True)) * scale
    dx1[...] = g
    dy[t] = g.astype(BF16)


def attention_grad(dy, w_out, w_t, qkv, probs, dqkv, parts):
    datt = dot_t(dy[...].reshape(ROWS, D), w_out[...]).astype(BF16)
    low = low_half()

    def scores(p, d, v):
        dp = dot_t(d, v)
        return (p * (dp - jnp.sum(p * dp, axis=-1, keepdims=True))).astype(BF16)

    for b in range(4):
        rows = slice(128 * b, 128 * b + 128)
        q, k, v = stacked(qkv[0, rows, :128], low), qkv[1, rows, :128], qkv[2, rows, :128]
        d = stacked(datt[rows, :128], low)
        p = probs[b, :256]
        ds = scores(p, d, v)
        o = dot(ds, k)
        dqkv[0, rows, :128] = (jnp.where(low, o[:128], o[128:]) * 0.125).astype(BF16)
        dqkv[1, rows, :128] = (t_dot(ds, q) * 0.125).astype(BF16)
        dqkv[2, rows, :128] = t_dot(p.astype(BF16), d).astype(BF16)
        q, k, v = qkv[0, rows, 128:], qkv[1, rows, 128:], qkv[2, rows, 128:]
        d = datt[rows, 128:]
        p = probs[b, 256:]
        ds = scores(p, d, v)
        dqkv[0, rows, 128:] = (dot(ds, k) * 0.125).astype(BF16)
        dqkv[1, rows, 128:] = (t_dot(ds, q) * 0.125).astype(BF16)
        dqkv[2, rows, 128:] = t_dot(p.astype(BF16), d).astype(BF16)
    total = dot(dqkv[0], w_t[0]) + dot(dqkv[1], w_t[1]) + dot(dqkv[2], w_t[2])
    parts[...] = total.astype(BF16).reshape(GROUP, OWN, D)


def out_qkv_grad(att, dy, dqkv, a1, g):
    put_halves(g, 0, 4, 48, t_dot(att[...], dy[...].reshape(ROWS, D)))
    for j in range(3):
        put_halves(g, 4 + 4 * j, 4, 48, t_dot(dqkv[j], a1[...].reshape(ROWS, D)))


def norm_one_grad(parts, landed, x, gain, dx1, out, vec, t):
    da = summed(parts, landed, t)
    n, scale = normalized(x[...].astype(F32))
    vec[t, :, :768] = jnp.sum(da * n, axis=0, keepdims=True)
    h = da * gain
    out[...] = dx1[...] + (h - jnp.mean(h, axis=-1, keepdims=True) - n * jnp.mean(h * n, axis=-1, keepdims=True)) * scale


class Reduction:
    def __init__(self, links, g, met, landed, full, sems):
        self.links, self.g, self.met, self.landed, self.full, self.sems = links, g, met, landed, full, sems

    def cores(self):
        other = 1 - self.links.core
        self.copies = [send(self.g.at[other], self.met, self.sems, 0, self.links.sibling())]

    def both_cores(self):
        finish(self.copies)
        self.met[...] = (self.g[self.links.core].astype(F32) + self.met[...].astype(F32)).astype(BF16)

    def scatter(self):
        self.both_cores()
        self.copies = [
            send(self.met.at[self.links.chip_of(k)], self.landed.at[k - 1], self.sems, k, self.links.chip_peer(k))
            for k in range(1, CHIPS)
        ]

    def gather(self):
        finish(self.copies)
        total = self.met[self.links.chip].astype(F32)
        for k in range(CHIPS - 1):
            total = total + self.landed[k].astype(F32)
        core, chip = self.links.core, self.links.chip
        self.full[core, chip] = total.astype(BF16)
        own = self.full.at[core, chip]
        self.copies = [send(own, own, self.sems, 15 + k, self.links.chip_peer(k)) for k in range(1, CHIPS)]

    def share(self):
        finish(self.copies)
        own = self.full.at[self.links.core]
        self.copies = [send(own, own, self.sems, 31, self.links.sibling())]

    def done(self):
        finish(self.copies)


class TwoAxes(Reduction):
    def __init__(self, links, g, met, landed, near, full, sems, first, second):
        super().__init__(links, g, met, landed, full, sems)
        self.near, self.first, self.second = near, first, second
        self.i, self.j = links.place[first], links.place[second]

    def scatter(self):
        self.both_cores()
        rank, peer = self.links.axis_rank, self.links.axis_peer
        self.copies = [
            send(self.met.at[rank(self.first, k)], self.landed.at[k - 1], self.sems, k, peer(self.first, k)) for k in (2, 1, 3)
        ]

    def scatter_second(self):
        finish(self.copies)
        total = self.met[self.i].astype(F32)
        for k in range(3):
            total = total + self.landed[k].astype(F32)
        self.met[self.i] = total.astype(BF16)
        rank, peer = self.links.axis_rank, self.links.axis_peer
        self.copies = [
            send(self.met.at[self.i, rank(self.second, k)], self.near.at[k - 1], self.sems, 3 + k, peer(self.second, k))
            for k in (2, 1, 3)
        ]

    def gather(self):
        finish(self.copies)
        total = self.met[self.i, self.j].astype(F32)
        for k in range(3):
            total = total + self.near[k].astype(F32)
        core = self.links.core
        self.full[core, self.i, self.j] = total.astype(BF16)
        own = self.full.at[core, self.i, self.j]
        self.copies = [send(own, own, self.sems, 6 + k, self.links.axis_peer(self.second, k)) for k in (2, 1, 3)]

    def gather_second(self):
        finish(self.copies)
        own = self.full.at[self.links.core, self.i]
        self.copies = [send(own, own, self.sems, 9 + k, self.links.axis_peer(self.first, k)) for k in (2, 1, 3)]


def body(
    x, seg_t, pad_t, pair_in, gain_one, gain_two, img_gain_one, img_gain_two,
    h_tok, h_iqkv, h_iout, h_iup, h_idown, h_iproj, h_qkv, h_out, h_up, h_down, h_proj,
    o_loss, o_input, o_norms, o_a, o_b, o_c, o_proj,
    tok, iw_qkv, iw_out, iw_up, iw_down, iw_proj, w_qkv, w_out, w_up, w_down, w_proj, load,
    perm, back, ibias, ia, iap, iqkv, iy, ypool, ihsum, images,
    bias, mem, mem_t, pair, a1, qkv, probs, att, p_att, l_att, x1, x1_pool, a2, dgelu, hsum, p_pool, l_pool,
    tf, scale, pooled, s_ref, e_ref, row_sums, col_sums, dts, de, dz, gp, dx2, du, p_da2, l_da2, dx1, dy,
    dqkv, p_da1, l_da1, proj, proj_all, vec, vec_all,
    g_a, g_b, g_c, m_a, m_b, m_c, r_a, r_b, r_c, n_a, n_b, f_a, f_b, f_c,
    group_sems, image_sems, rank_sems, sum_sems, proj_sems, store,
):
    links = Links()
    t, dp = links.t, links.dp
    loads = {}
    for i, (name, src, dst) in enumerate((
        ("tok", h_tok, tok), ("iqkv", h_iqkv, iw_qkv), ("qkv", h_qkv, w_qkv), ("out", h_out, w_out), ("iout", h_iout, iw_out),
        ("iup", h_iup, iw_up), ("up", h_up, w_up), ("down", h_down, w_down), ("idown", h_idown, iw_down),
        ("iproj", h_iproj, iw_proj), ("proj", h_proj, w_proj),
    )):
        loads[name] = pltpu.make_async_copy(src, dst, load.at[i])
        loads[name].start()

    links.greet()
    pair[t] = column(pair_in)
    pair_copies = group_share(links, pair, group_sems.at[0])
    text_norm_one(x, as_row(gain_one), a1, t)
    copies = group_share(links, a1, group_sems.at[1])

    text_masks(seg_t, pad_t, bias, mem, mem_t)
    image_masks(perm, back, ibias)
    loads["tok"].wait()
    image_norm_one(tok, as_row(img_gain_one), ia)
    image_permute(perm, ia, iap)
    loads["iqkv"].wait()
    image_qkv(iap, iw_qkv, iqkv)

    finish(copies)
    loads["qkv"].wait()
    loads["out"].wait()
    text_attention(a1, w_qkv, bias, w_out, qkv, probs, att, p_att)
    copies = group_scatter(links, p_att, l_att, group_sems.at[2])

    image_attention(iqkv, ibias, iap, 0, 8)

    finish(copies)
    text_norm_two(x, p_att, l_att, as_row(gain_two), mem, x1, a2, x1_pool, t)
    copies = group_share(links, a2, group_sems.at[3])
    text_pool_one(x1, mem, x1_pool, t)

    loads["iout"].wait()
    image_out(back, iap, ia, tok, iw_out, iy)
    image_norm_two(iy, as_row(img_gain_two), ia, ypool)
    loads["iup"].wait()
    image_up(ia, iw_up, ihsum, 0, 6)

    finish(copies)
    loads["up"].wait()
    loads["down"].wait()
    text_up(a2, w_up, mem, w_down, dgelu, hsum, p_pool)
    copies = group_scatter(links, p_pool, l_pool, group_sems.at[4])

    image_up(ia, iw_up, ihsum, 6, 10)
    finish(copies)
    text_pool(p_pool, l_pool, x1_pool, mem, pooled, t)
    copies = group_share(links, pooled, group_sems.at[5])

    image_up(ia, iw_up, ihsum, 10, 12)
    loads["idown"].wait()
    loads["iproj"].wait()
    core, chip = links.core, links.chip
    images[core, chip] = image_finish(ihsum, ypool, iw_down, iw_proj)
    own = images.at[core, chip]
    image_copies = [send(own, own, image_sems, k, links.chip_peer(k)) for k in range(1, CHIPS)]

    finish(copies)
    loads["proj"].wait()
    text_embed(pooled, w_proj, tf, scale)
    finish(image_copies)
    own = images.at[core]
    image_copies = [send(own, own, image_sems, 0, links.sibling())]
    finish(pair_copies)
    finish(image_copies)

    score_sums(tf, images, s_ref, e_ref, row_sums, col_sums, t, dp)
    col_copies = rank_share(links, col_sums, rank_sems.at[0])
    row_copies = group_share(links, row_sums, group_sems.at[6])
    finish(col_copies)
    finish(row_copies)
    score_grad(s_ref, e_ref, row_sums, col_sums, pair, images, dts, vec, t)
    finish(group_share(links, dts, group_sems.at[7]))
    embed_grad(dts, tf, scale, w_proj, mem, de, dz, gp)

    red_a = TwoAxes(links, g_a, m_a, r_a, n_a, f_a, sum_sems.at[0], "x", "z")
    red_b = TwoAxes(links, g_b, m_b, r_b, n_b, f_b, sum_sems.at[1], "z", "x")
    red_c = Reduction(links, g_c, m_c, r_c, f_c, sum_sems.at[2])

    hidden_grad(dz, w_down, mem_t, dgelu, du)
    hidden_spread(du, w_up, p_da2)
    copies = group_scatter(links, p_da2, l_da2, group_sems.at[8])
    down_proj_grad(hsum, dz, de, pooled, proj, g_a, t)
    red_a.cores()
    row_grad(gp, mem, dx2, t)
    up_grad(a2, du, g_b)
    red_b.cores()
    red_a.scatter()
    red_b.scatter()
    finish(copies)
    norm_two_grad(p_da2, l_da2, x1, as_row(gain_two), dx2, dx1, dy, vec, t)
    copies = group_share(links, dy, group_sems.at[9])
    red_a.scatter_second()
    red_b.scatter_second()
    red_a.gather()
    red_b.gather()
    finish(copies)
    attention_grad(dy, w_out, w_qkv, qkv, probs, dqkv, p_da1)
    copies = group_scatter(links, p_da1, l_da1, group_sems.at[10])
    out_qkv_grad(att, dy, dqkv, a1, g_c)
    red_c.cores()
    red_a.gather_second()
    red_b.gather_second()
    red_c.scatter()
    finish(copies)
    norm_one_grad(p_da1, l_da1, x, as_row(gain_one), dx1, o_input, vec, t)
    vec_copies = group_share(links, vec, group_sems.at[11])
    red_a.share()
    red_b.share()
    proj_all[core, t] = f_a[core, 3, :3]
    own = proj_all.at[core, t]
    proj_copies = [send(own, own, proj_sems, k, links.group_peer(k)) for k in (2, 1, 3)]
    finish(vec_copies)
    vec_all[dp] = vec[0] + vec[1] + vec[2] + vec[3]
    vec_copies = rank_share(links, vec_all, rank_sems.at[1])
    red_c.gather()
    finish(proj_copies)
    own = proj_all.at[core]
    proj_copies = [send(own, own, proj_sems, 0, links.sibling())]
    red_a.done()
    red_b.done()
    stores = [pltpu.make_async_copy(f_a, o_a, store.at[0]), pltpu.make_async_copy(f_b, o_b, store.at[1])]
    for copy in stores:
        copy.start()
    finish(vec_copies)
    total = vec_all[0]
    for i in range(1, RANKS):
        total = total + vec_all[i]
    o_norms[...] = total[:, :1536]
    o_loss[...] = total[:, 1536:] * (1.0 / 4096.0)
    finish(proj_copies)
    stores.append(pltpu.make_async_copy(proj_all, o_proj, store.at[2]))
    stores[-1].start()
    red_c.share()
    red_c.done()
    stores.append(pltpu.make_async_copy(f_c, o_c, store.at[3]))
    stores[-1].start()
    for copy in stores:
        copy.wait()


def widen(
    loss, norms, h_input, h_a, h_b, h_c, h_proj,
    o_loss, o_input, o_one, o_two, o_down, o_up, o_out, o_qkv, o_proj,
    grad, full_a, full_b, full_c, full_proj, down, up, out, qkv, proj, loaded, stored,
):
    sources = ((h_a, full_a), (h_b, full_b), (h_proj, full_proj), (h_c, full_c), (h_input, grad))
    loads = [pltpu.make_async_copy(src, dst, loaded.at[i]) for i, (src, dst) in enumerate(sources)]
    for copy in loads:
        copy.start()
    stores = []

    def write(buf, target):
        stores.append(pltpu.make_async_copy(buf, target, stored.at[len(stores)]))
        stores[-1].start()

    def halves(target, parts, rows):
        for j in range(2):
            target[:, j * HALF : (j + 1) * HALF] = parts[j].reshape(rows, HALF).astype(F32)

    loads[0].wait()
    halves(down, full_a[:, :3], HID)
    write(down, o_down)
    loads[1].wait()
    halves(up, full_b, D)
    write(up, o_up)
    loads[2].wait()
    halves(proj, full_proj, D)
    write(proj, o_proj)
    loads[3].wait()
    halves(out, full_c[:, :4], BAND)
    write(out, o_out)
    halves(qkv, full_c[:, 4:], 3 * BAND)
    write(qkv, o_qkv)
    loads[4].wait()
    write(grad, o_input)
    o_loss[0, 0] = loss[0, 0]
    o_one[...] = norms[:, :D].reshape(D)
    o_two[...] = norms[:, D:].reshape(D)
    for copy in stores:
        copy.wait()


def on_device(
    text_input, segment_ids, pad_mask, pairing, ln_first, w_qkv, w_out, ln_second, w_up, w_down, text_proj,
    image_tokens, img_ln_first, img_w_qkv, img_w_out, img_ln_second, img_w_up, img_w_down, img_proj,
):
    vmem = pl.BlockSpec(memory_space=VM)
    hbm = pl.BlockSpec(memory_space=pl.ANY)
    shape = jax.ShapeDtypeStruct
    sums = ((4, 4, 64, HALF), (4, 4, 48, HALF), (16, 48, HALF))
    dma = pltpu.SemaphoreType.DMA
    scratch = [
        VM((IROWS, D), BF16), VM((3, D, D), BF16), VM((D, D), BF16), VM((D, FF), BF16), VM((FF, D), BF16), VM((D, D), BF16),
        VM((3, BAND, D), BF16), VM((BAND, D), BF16), VM((D, HID), BF16), VM((HID, D), BF16), VM((D, D), BF16), dma((11,)),
        VM((PROWS, IROWS), BF16), VM((IROWS, PROWS), BF16), VM((2 * PAIR, PAIR), F32), VM((IROWS, D), BF16), VM((PROWS, D), BF16),
        VM((3, PROWS, D), BF16), VM((IROWS, D), F32), VM((IMGS, D), F32),
        VM((IMGS, FF), F32), VM((2, CHIPS, IMGS, D), BF16),
        VM((4, 128, 128), F32), VM((CAPS, ROWS), BF16), VM((ROWS, 128), BF16), VM((GROUP, OWN_CAPS, 128), I32),
        VM((GROUP, OWN, D), BF16), VM((3, ROWS, BAND), BF16), VM((4, HALF, 128), F32), VM((ROWS, BAND), BF16),
        VM((GROUP, OWN, D), BF16), VM((3, OWN, D), BF16), VM((OWN, D), F32), VM((OWN_CAPS, D), F32), VM((GROUP, OWN, D), BF16),
        VM((ROWS, HID), F32), VM((CAPS, HID), F32), VM((GROUP, OWN_CAPS, D), F32), VM((3, OWN_CAPS, D), F32),
        VM((CAPS, D), F32), VM((CAPS, 128), F32), VM((GROUP, OWN_CAPS, D), BF16), VM((CAPS, ROWS), F32),
        VM((CAPS, ROWS), F32), VM((GROUP, CAPS, 128), F32), VM((RANKS, 1, ROWS), F32), VM((GROUP, CAPS, D), BF16),
        VM((CAPS, D), BF16), VM((CAPS, D), BF16), VM((CAPS, D), F32),
        VM((OWN, D), F32), VM((ROWS, HID), BF16), VM((GROUP, OWN, D), BF16), VM((3, OWN, D), BF16), VM((OWN, D), F32),
        VM((GROUP, OWN, D), BF16), VM((3, ROWS, BAND), BF16), VM((GROUP, OWN, D), BF16), VM((3, OWN, D), BF16),
        VM((GROUP, BAND, D), BF16), VM((2, GROUP, 3, 64, HALF), BF16), VM((GROUP, 1, VEC), F32), VM((RANKS, 1, VEC), F32),
    ]
    scratch += [VM((2,) + s, BF16) for s in sums] + [VM(s, BF16) for s in sums]
    scratch += [VM((3,) + sums[0][1:], BF16), VM((3,) + sums[1][1:], BF16), VM((15,) + sums[2][1:], BF16)]
    scratch += [VM((3,) + s[2:], BF16) for s in sums[:2]] + [VM((2,) + s, BF16) for s in sums]
    scratch += [dma((12, 2, 3)), dma((2, 16)), dma((2, 2, 31)), dma((3, 2, 32)), dma((2, 4)), dma((4,))]
    loss, input_grad, norms, full_a, full_b, full_c, full_proj = pl.pallas_call(
        body,
        out_shape=(
            shape((1, 128), F32), shape((OWN, D), F32), shape((1, 1536), F32),
            *(shape((2,) + s, BF16) for s in sums), shape((2, GROUP, 3, 64, HALF), BF16),
        ),
        in_specs=[vmem] * 3 + [pl.BlockSpec(memory_space=pltpu.SMEM)] + [vmem] * 4 + [hbm] * 11,
        out_specs=(vmem, vmem, vmem, hbm, hbm, hbm, hbm),
        scratch_shapes=scratch,
        compiler_params=pltpu.CompilerParams(collective_id=0, has_side_effects=True, vmem_limit_bytes=63 << 20),
        name="lit",
    )(
        text_input, segment_ids.T, pad_mask.T, pairing, ln_first, ln_second, img_ln_first, img_ln_second,
        image_tokens.transpose(1, 0, 2).reshape(IROWS, D), img_w_qkv, img_w_out, img_w_up, img_w_down, img_proj,
        w_qkv.swapaxes(1, 2), w_out, w_up, w_down, text_proj,
    )

    loss, input_grad, one, two, down, up, out, qkv, proj = pl.pallas_call(
        widen,
        out_shape=(
            shape((1, 1), F32), shape((OWN, D), F32), shape((D,), F32), shape((D,), F32), shape((HID, D), F32),
            shape((D, HID), F32), shape((BAND, D), F32), shape((3 * BAND, D), F32), shape((D, D), F32),
        ),
        in_specs=[vmem] * 2 + [hbm] * 5,
        out_specs=(pl.BlockSpec(memory_space=pltpu.SMEM), hbm, vmem, vmem, hbm, hbm, hbm, hbm, hbm),
        scratch_shapes=[
            VM((OWN, D), F32), *(VM((2,) + s, BF16) for s in sums), VM((2, GROUP, 3, 64, HALF), BF16),
            VM((HID, D), F32), VM((D, HID), F32), VM((BAND, D), F32), VM((3 * BAND, D), F32), VM((D, D), F32),
            dma((5,)), dma((6,)),
        ],
        compiler_params=pltpu.CompilerParams(vmem_limit_bytes=60 << 20),
        name="widen",
    )(loss, norms, input_grad, full_a, full_b, full_c, full_proj)
    return (loss.reshape(()), input_grad, one, qkv.reshape(3, BAND, D).swapaxes(1, 2), out, two, up, down, proj)


def solution(mesh):
    rows = P(("dp", "tensor"))
    in_specs = (
        P(("dp", "tensor"), None), P("dp", None), P("dp", None), rows, P(), P(None, None, "tensor"), P("tensor", None), P(),
        P(None, "tensor"), P("tensor", None), P(), P(("dp", "tensor"), None, None), P(), P(), P(), P(), P(), P(), P(),
    )
    out_specs = (
        P(), P(("dp", "tensor"), None), P(), P(None, None, "tensor"), P("tensor", None), P(), P(None, "tensor"),
        P("tensor", None), P(),
    )
    return jax.shard_map(on_device, mesh=mesh, in_specs=in_specs, out_specs=out_specs, check_vma=False)
```

```python
import jax, jax.numpy as jnp
from jax import lax
from jax.experimental import pallas as pl
from jax.experimental.pallas import tpu as pltpu
from jax.sharding import PartitionSpec as P

F32, BF16, I32 = jnp.float32, jnp.bfloat16, jnp.int32
VM = pltpu.VMEM
EPS = 1e-6
NEG = -1e30
D, FF, HID = 768, 3072, 768
IMGS, POS = 16, 50
IROWS = IMGS * POS
HALFP = 56
PAIR = 2 * HALFP
PROWS = PAIR * (IMGS // 2)
TILE = 256
UP_TILE = 768


def dot(a, b):
    return jnp.dot(a, b, preferred_element_type=F32)


def dot_t(a, b):
    return lax.dot_general(a, b, (((1,), (1,)), ((), ())), preferred_element_type=F32)


def t_dot(a, b):
    return lax.dot_general(a, b, (((0,), (0,)), ((), ())), preferred_element_type=F32)


def iota(shape, axis):
    return lax.broadcasted_iota(I32, shape, axis)


def normalized(values):
    centred = values - jnp.mean(values, axis=-1, keepdims=True)
    spread = jnp.mean(centred * centred, axis=-1, keepdims=True)
    scale = lax.rsqrt(spread + EPS)
    return centred * scale, scale


def normal_cdf(u):
    return 0.5 + 0.5 * lax.erf(u * 0.7071067811865476)


def image_bias(bias):
    q, k = iota((2 * PAIR, PAIR), 0), iota((2 * PAIR, PAIR), 1)
    q = jnp.where(q >= PAIR, q - PAIR, q)
    place = jnp.where(k >= HALFP, k - HALFP, k)
    bias[...] = jnp.where(((q >= HALFP) == (k >= HALFP)) & (place < POS), 0.0, NEG)


def image_norm_one(tok, gain, stage):
    def rows(i, c):
        s = pl.ds(pl.multiple_of(i * 160, 160), 160)
        n, _ = normalized(tok[s, :].astype(F32))
        n = n * gain
        for h in range(6):
            stage[h, s, :] = n[:, h * 128 : h * 128 + 128]
        return c

    lax.fori_loop(0, 5, rows, 0)
    stage[:, IROWS:, :] = jnp.zeros((6, PROWS - IROWS, 128), F32)


def tiles(n, body):
    def step(i, c):
        body(i, pl.ds(pl.multiple_of(i * TILE, TILE), TILE))
        return c

    lax.fori_loop(0, n, step, 0)


def image_permute(stage, iap):
    def pair(p, c):
        for h in range(6):
            both = [stage[h, pl.ds(2 * p + i, HALFP, stride=IMGS), :] for i in range(2)]
            iap[pl.ds(pl.multiple_of(p * PAIR, PAIR), PAIR), h * 128 : h * 128 + 128] = jnp.concatenate(both, axis=0).astype(BF16)
        return c
    lax.fori_loop(0, IMGS // 2, pair, 0)


def image_qkv(iap, w, iqkv):
    def step(j, c):
        iqkv[j] = dot(iap[...], w[j]).astype(BF16)
        return c
    lax.fori_loop(0, 3, step, 0)


def stacked(values, low):
    zero = jnp.zeros_like(values)
    return jnp.concatenate([jnp.where(low, values, zero), jnp.where(low, zero, values)], axis=0)


def image_attention(iqkv, bias, stage, first, last, unroll=1):
    low = iota((PAIR, 128), 1) < 64

    def pair(p, c):
        rows = pl.ds(pl.multiple_of(p * PAIR, PAIR), PAIR)
        ones = jnp.ones((PAIR, 128), BF16)
        cols = [pl.ds(h * 128, 128) for h in range(6)]
        s = [dot_t(stacked(iqkv[0, rows, h], low), iqkv[1, rows, h]) * 0.125 + bias[...] for h in cols]
        e = [jnp.exp(x - jnp.max(x, axis=-1, keepdims=True)).astype(BF16) for x in s]
        for i, (h, x) in enumerate(zip(cols, e)):
            o = dot(x, jnp.concatenate([iqkv[2, rows, h], ones], axis=1))
            o = jnp.where(low, o[:PAIR, :128], o[PAIR:, :128]) / jnp.where(low, o[:PAIR, 128:], o[PAIR:, 128:])
            stage[i, pl.ds(2 * p, HALFP, stride=IMGS), :] = o[:HALFP]
            stage[i, pl.ds(2 * p + 1, HALFP, stride=IMGS), :] = o[HALFP:]
        return c

    lax.fori_loop(first, last, pair, 0, unroll=unroll)


def image_out(stage, tok, w, iy):
    def rows(i, c):
        s = pl.ds(pl.multiple_of(i * 160, 160), 160)
        iy[s, :] = tok[s, :].astype(F32) + dot(jnp.concatenate([stage[h, s, :].astype(BF16) for h in range(6)], axis=1), w[...])
        return c
    lax.fori_loop(0, 5, rows, 0)


def image_norm_two(iy, gain, ia, ypool):
    ypool[...] = jnp.zeros_like(ypool)
    def rows(i, c):
        s = pl.ds(pl.multiple_of(i * 160, 160), 160)
        y = iy[s, :]
        ypool[...] += jnp.sum(y.reshape(10, IMGS, D), axis=0)
        n, _ = normalized(y)
        ia[s, :] = (n * gain).astype(BF16)
        return c
    lax.fori_loop(0, 5, rows, 0)


def image_up(ia, w, hsum, first, last):
    def step(i, c):
        s = pl.ds(pl.multiple_of(i * UP_TILE, UP_TILE), UP_TILE)
        for m in range(5):
            u = dot(ia[160 * m : 160 * m + 160, :], w[:, s])
            part = jnp.sum((u * normal_cdf(u)).reshape(10, IMGS, UP_TILE), axis=0)
            total = part if m == 0 else total + part
        hsum[:, s] = total
        return c
    lax.fori_loop(first, last, step, 0)


def as_row(gain):
    return gain[...].reshape(1, D)


def column(values):
    rows = iota((OWN_CAPS, 128), 0)
    out = jnp.zeros((OWN_CAPS, 128), I32)
    for i in range(OWN_CAPS):
        out = jnp.where(rows == i, values[i], out)
    return out


def split_rows(x):
    hi = x.astype(BF16)
    return jnp.concatenate([hi, (x - hi.astype(F32)).astype(BF16)], axis=0)


def image_finish(hsum, ypool, w_down, w_proj):
    both = dot(split_rows(hsum[...]), w_down[...])
    pooled = ((ypool[...] + both[:IMGS] + both[IMGS:]) * (1.0 / POS)).astype(BF16)
    e = dot(pooled, w_proj[...])
    return (e * lax.rsqrt(jnp.sum(e * e, axis=-1, keepdims=True) + EPS)).astype(BF16)


GROUP, RANKS, CHIPS = 4, 32, 16
OWN, ROWS = 128, 512
CAPS, OWN_CAPS = 64, 16
BAND = 192
HALF = 384
MESH = pl.DeviceIdType.MESH
VEC = 1664


class Links:
    def __init__(self):
        self.dp, self.t = lax.axis_index("dp"), lax.axis_index("tensor")
        self.core, self.chip = lax.rem(self.dp, 2), self.dp // 2
        self.place = {"x": lax.rem(self.chip, 4), "z": self.chip // 4}

    def rank(self, k):
        return lax.rem(self.t + k, GROUP)

    def group_peer(self, k):
        return {"dp": self.dp, "tensor": self.rank(k)}

    def rank_peer(self, k):
        return {"dp": lax.rem(self.dp + k, RANKS), "tensor": self.t}

    def chip_of(self, k):
        return lax.rem(self.chip + k, CHIPS)

    def chip_peer(self, k):
        return {"dp": 2 * self.chip_of(k) + self.core, "tensor": self.t}

    def axis_rank(self, axis, k):
        return lax.rem(self.place[axis] + k, 4)

    def axis_peer(self, axis, k):
        place = dict(self.place)
        place[axis] = self.axis_rank(axis, k)
        return {"dp": 2 * (place["z"] * 4 + place["x"]) + self.core, "tensor": self.t}

    def sibling(self):
        return {"dp": self.dp + 1 - 2 * self.core, "tensor": self.t}

    def greet(self):
        barrier = pltpu.get_barrier_semaphore()
        for k in range(1, GROUP):
            pl.semaphore_signal(barrier, 1, device_id=self.group_peer(k), device_id_type=MESH)
        for k in range(1, RANKS):
            pl.semaphore_signal(barrier, 1, device_id=self.rank_peer(k), device_id_type=MESH)

    def met(self):
        pl.semaphore_wait(pltpu.get_barrier_semaphore(), GROUP - 1 + RANKS - 1)


def send(src, dst, sems, at, peer):
    copy = pltpu.make_async_remote_copy(
        src, dst, sems.at[0, at], sems.at[1, at], device_id=peer, device_id_type=MESH
    )
    copy.start()
    return copy


def finish(copies):
    for copy in copies:
        copy.wait()


def group_share(links, buf, sems):
    own = buf.at[links.t]
    return [send(own, own, sems, k - 1, links.group_peer(k)) for k in (2, 1, 3)]


def group_scatter(links, parts, landed, sems):
    return [send(parts.at[links.rank(k)], landed.at[k - 1], sems, k - 1, links.group_peer(k)) for k in (2, 1, 3)]


def rank_share(links, buf, sems):
    own = buf.at[links.dp]
    return [send(own, own, sems, k - 1, links.rank_peer(k)) for k in range(1, RANKS)]


def text_masks(seg_t, pad_t, bias, mem, mem_t):
    seg, pad = seg_t[...].astype(F32).astype(BF16), pad_t[...].astype(F32).astype(BF16)

    def as_column(values):
        pick = jnp.where(iota((ROWS, 32), 0) >> 4 == iota((ROWS, 32), 1), 1.0, 0.0).astype(BF16)
        wide = dot_t(pick, values)
        return jnp.sum(jnp.where(iota((ROWS, 16), 0) & 15 == iota((ROWS, 16), 1), wide, 0.0), axis=1, keepdims=True)

    def as_row(values):
        pick = jnp.where(iota((32, ROWS), 1) >> 4 == iota((32, ROWS), 0), 1.0, 0.0).astype(BF16)
        wide = dot(values, pick)
        return jnp.sum(jnp.where(iota((16, ROWS), 1) & 15 == iota((16, ROWS), 0), wide, 0.0), axis=0, keepdims=True)

    cap_col = as_column(seg) + ((iota((ROWS, 1), 0) >> 4) * 2).astype(F32)
    key_col = jnp.where(as_column(pad) > 0.5, cap_col, -1.0)
    cap_row = as_row(seg) + ((iota((1, ROWS), 1) >> 4) * 2).astype(F32)
    key_row = jnp.where(as_row(pad) > 0.5, cap_row, -1.0)
    for b in range(4):
        rows = slice(128 * b, 128 * b + 128)
        bias[b] = jnp.where(cap_col[rows] == key_row[:, rows], 0.0, NEG)
    mem[...] = jnp.where(iota((CAPS, ROWS), 0).astype(F32) == key_row, 1.0, 0.0).astype(BF16)
    mem_t[...] = jnp.where((iota((ROWS, 128), 1) & 63).astype(F32) == key_col, 1.0, 0.0).astype(BF16)


def text_norm_one(x, gain, a1, t):
    n, _ = normalized(x[...].astype(F32))
    a1[t] = (n * gain).astype(BF16)


def low_half():
    return iota((OWN, 128), 1) < 64


def text_attention(a1, w_t, bias, w_out, qkv, probs, att, parts):
    rows_all = a1[...].reshape(ROWS, D)
    for j in range(3):
        qkv[j] = dot_t(rows_all, w_t[j]).astype(BF16)
    low = low_half()
    blocks = [slice(128 * b, 128 * b + 128) for b in range(4)]
    scores = []
    for b, rows in enumerate(blocks):
        mask = bias[b]
        scores.append(dot_t(stacked(qkv[0, rows, :128], low), qkv[1, rows, :128]) * 0.125 + jnp.concatenate([mask, mask], axis=0))
        scores.append(dot_t(qkv[0, rows, 128:], qkv[1, rows, 128:]) * 0.125 + mask)
    powers = [jnp.exp(x - jnp.max(x, axis=-1, keepdims=True)) for x in scores]
    shares = [x / jnp.sum(x, axis=-1, keepdims=True) for x in powers]
    for b, rows in enumerate(blocks):
        probs[b, :256] = shares[2 * b]
        probs[b, 256:] = shares[2 * b + 1]
        o = dot(shares[2 * b].astype(BF16), qkv[2, rows, :128])
        att[rows, :128] = jnp.where(low, o[:128], o[128:]).astype(BF16)
        att[rows, 128:] = dot(shares[2 * b + 1].astype(BF16), qkv[2, rows, 128:]).astype(BF16)
    parts[...] = dot(att[...], w_out[...]).astype(BF16).reshape(GROUP, OWN, D)


def summed(parts, landed, t):
    return parts[t].astype(F32) + landed[0].astype(F32) + landed[1].astype(F32) + landed[2].astype(F32)


def split3(x):
    hi = x.astype(BF16)
    rest = x - hi.astype(F32)
    mid = rest.astype(BF16)
    return jnp.concatenate([hi, mid, (rest - mid.astype(F32)).astype(BF16)], axis=0)


def own_member(mem, t):
    return mem[pl.ds(pl.multiple_of(t * OWN_CAPS, OWN_CAPS), OWN_CAPS), pl.ds(pl.multiple_of(t * OWN, OWN), OWN)]


def text_norm_two(x, parts, landed, gain, mem, x1, a2, x1_pool, t):
    y = x[...].astype(F32) + summed(parts, landed, t)
    x1[...] = y
    n, _ = normalized(y)
    a2[t] = (n * gain).astype(BF16)


def text_pool_one(x1, mem, x1_pool, t):
    own = own_member(mem, t)
    x1_pool[...] = dot(jnp.concatenate([own, own, own], axis=1), split3(x1[...]))


def text_up(a2, w_up, mem, w_down, x1_pool, dgelu, hidden, hsum, part, parts, t):
    for r in range(GROUP):
        rows = slice(r * OWN, r * OWN + OWN)
        u = dot(a2[r], w_up[...])
        phi = normal_cdf(u)
        dgelu[rows, :] = phi + u * (jnp.exp(u * u * -0.5) * 0.3989422804014327)
        hidden[rows, :] = (u * phi).astype(BF16)
    hsum[...] = dot(mem[...], hidden[...])
    both = dot(split_rows(hsum[...]), w_down[...])
    part[...] = (both[:CAPS] + both[CAPS:]).reshape(GROUP, OWN_CAPS, D)
    part[t] += x1_pool[...]
    parts[t] = part[...].reshape(CAPS, D).astype(BF16)


def counts_of(mem):
    return jnp.sum(mem.astype(F32), axis=1, keepdims=True)


def text_embed(parts, mem, w_proj, pooled, tf, scale):
    total = parts[0].astype(F32) + parts[1].astype(F32) + parts[2].astype(F32) + parts[3].astype(F32)
    rows = (total / counts_of(mem[...])).astype(BF16)
    pooled[...] = rows
    e = dot(rows, w_proj[...])
    rs = lax.rsqrt(jnp.sum(e * e, axis=-1, keepdims=True) + EPS)
    tf[...] = rs * e
    scale[...] = jnp.broadcast_to(rs, (CAPS, 128))


def score_sums(tf, images, s_ref, e_ref, row_sums, col_sums, t, dp):
    s = 40.0 * dot_t(tf[...].astype(BF16), images[...].reshape(ROWS, D))
    s_ref[...] = s
    e = jnp.exp(s - 40.0)
    e_ref[...] = e
    row_sums[t] = jnp.broadcast_to(jnp.sum(e, axis=1, keepdims=True), (CAPS, 128))
    col_sums[dp] = jnp.sum(e, axis=0, keepdims=True)


def score_grad(s_ref, e_ref, row_sums, col_sums, pair, images, dts, vec, t):
    rows = jnp.sum(row_sums[...], axis=0)[:, :1]
    cols = col_sums[0]
    for i in range(1, RANKS):
        cols = cols + col_sums[i]
    lane = iota((CAPS, ROWS), 1)
    image = ((lane >> 4) & 15) * (2 * CAPS) + (lane >> 8) * CAPS + (lane & 15) + OWN_CAPS * t
    target = jnp.where(pair[...].reshape(CAPS, 128)[:, :1] == image, 1.0, 0.0)
    g = 0.5 * (e_ref[...] / rows + e_ref[...] / cols) - target
    dts[t] = (40.0 * dot(g.astype(BF16), images[...].reshape(ROWS, D))).astype(BF16)
    loss = (
        jnp.sum(40.0 + jnp.log(rows), axis=0, keepdims=True) * (1.0 / GROUP)
        + jnp.sum(40.0 + jnp.log(cols), axis=1, keepdims=True) * (1.0 / RANKS)
        - 2.0 * jnp.sum(jnp.sum(s_ref[...] * target, axis=1, keepdims=True), axis=0, keepdims=True)
    )
    vec[t, :, 1536:] = jnp.broadcast_to(loss, (1, 128))


def embed_grad(dts, tf, scale, w_proj, mem, de_ref, dz_ref, gp_ref):
    dt = dts[0].astype(F32) + dts[1].astype(F32) + dts[2].astype(F32) + dts[3].astype(F32)
    f = tf[...]
    de = (scale[:, :1] * (dt - f * jnp.sum(f * dt, axis=-1, keepdims=True))).astype(BF16)
    gp = dot_t(de, w_proj[...]) / counts_of(mem[...])
    de_ref[...] = de
    gp_ref[...] = gp
    dz_ref[...] = gp.astype(BF16)


def row_grad(gp_ref, mem, dx2, t):
    own = own_member(mem, t)
    gp = gp_ref[pl.ds(pl.multiple_of(t * OWN_CAPS, OWN_CAPS), OWN_CAPS), :]
    dx2[...] = t_dot(jnp.concatenate([own, own, own], axis=0), split3(gp))


def hidden_grad(dz, w_down, mem_t, dgelu, du):
    dh = split_rows(dot_t(dz[...], w_down[...]))
    for i in range(3):
        s = slice(i * TILE, i * TILE + TILE)
        du[:, s] = (dot(mem_t[...], dh[:, s]) * dgelu[:, s]).astype(BF16)


def hidden_spread(du, w_up, parts):
    parts[...] = dot_t(du[...], w_up[...]).astype(BF16).reshape(GROUP, OWN, D)


def put_halves(g, first, count, rows, values):
    for j in range(2):
        part = values[:, j * HALF : (j + 1) * HALF].reshape(count, rows, HALF).astype(BF16)
        if len(g.shape) == 4:
            g[j, first : first + count] = part
        elif count == 3:
            g[j, first // 4, :3] = part
        else:
            g[j, first // 4 : (first + count) // 4] = part.reshape(count // 4, 4, rows, HALF)


def down_proj_grad(hsum, dz, de, pooled, proj, g, t):
    hs = split_rows(hsum[...])
    dz2 = jnp.concatenate([dz[...], dz[...]], axis=0)
    for i in range(3):
        put_halves(g, 4 * i, 4, 64, t_dot(hs[:, i * TILE : (i + 1) * TILE], dz2))
    proj[...] = t_dot(pooled[...], de[...]).astype(BF16).reshape(GROUP, BAND, D)
    put_halves(g, 12, 3, 64, proj[t])
    g[:, 3, 3] = jnp.zeros((2, 64, HALF), BF16)


def up_grad(a2, du, g):
    for i in range(2):
        rows = a2[:, :, i * HALF : (i + 1) * HALF].reshape(ROWS, HALF)
        put_halves(g, 8 * i, 8, 48, t_dot(rows, du[...]))


def norm_two_grad(parts, landed, x1, gain, dx2, dx1, dy, vec, t):
    da = summed(parts, landed, t)
    n, scale = normalized(x1[...])
    vec[t, :, 768:1536] = jnp.sum(da * n, axis=0, keepdims=True)
    h = da * gain
    g = dx2[...] + (h - jnp.mean(h, axis=-1, keepdims=True) - n * jnp.mean(h * n, axis=-1, keepdims=True)) * scale
    dx1[...] = g
    dy[t] = g.astype(BF16)


def attention_grad(dy, w_out, w_t, qkv, probs, dqkv, parts):
    datt = dot_t(dy[...].reshape(ROWS, D), w_out[...]).astype(BF16)
    low = low_half()
    blocks = [slice(128 * b, 128 * b + 128) for b in range(4)]
    sides, raw = [], []
    for b, rows in enumerate(blocks):
        sides.append((stacked(qkv[0, rows, :128], low), stacked(datt[rows, :128], low)))
        sides.append((qkv[0, rows, 128:], datt[rows, 128:]))
        raw.append(dot_t(sides[-2][1], qkv[2, rows, :128]))
        raw.append(dot_t(sides[-1][1], qkv[2, rows, 128:]))
    probs_of = [probs[b, part] for b in range(4) for part in (slice(0, 256), slice(256, 384))]
    ds = [(p * (x - jnp.sum(p * x, axis=-1, keepdims=True))).astype(BF16) for p, x in zip(probs_of, raw)]
    for b, rows in enumerate(blocks):
        for i, cols in ((2 * b, slice(0, 128)), (2 * b + 1, slice(128, BAND))):
            o = dot(ds[i], qkv[1, rows, cols])
            if i % 2 == 0:
                o = jnp.where(low, o[:128], o[128:])
            dqkv[0, rows, cols] = (o * 0.125).astype(BF16)
            dqkv[1, rows, cols] = (t_dot(ds[i], sides[i][0]) * 0.125).astype(BF16)
            dqkv[2, rows, cols] = t_dot(probs_of[i].astype(BF16), sides[i][1]).astype(BF16)
    total = dot(dqkv[0], w_t[0]) + dot(dqkv[1], w_t[1]) + dot(dqkv[2], w_t[2])
    parts[...] = total.astype(BF16).reshape(GROUP, OWN, D)


def out_qkv_grad(att, dy, dqkv, a1, g):
    put_halves(g, 0, 4, 48, t_dot(att[...], dy[...].reshape(ROWS, D)))
    for j in range(3):
        put_halves(g, 4 + 4 * j, 4, 48, t_dot(dqkv[j], a1[...].reshape(ROWS, D)))


def norm_one_grad(parts, landed, x, gain, dx1, out, vec, t):
    da = summed(parts, landed, t)
    n, scale = normalized(x[...].astype(F32))
    vec[t, :, :768] = jnp.sum(da * n, axis=0, keepdims=True)
    h = da * gain
    out[...] = dx1[...] + (h - jnp.mean(h, axis=-1, keepdims=True) - n * jnp.mean(h * n, axis=-1, keepdims=True)) * scale


class Reduction:
    def __init__(self, links, g, met, landed, full, sems):
        self.links, self.g, self.met, self.landed, self.full, self.sems = links, g, met, landed, full, sems

    def cores(self):
        other = 1 - self.links.core
        self.copies = [send(self.g.at[other], self.met, self.sems, 0, self.links.sibling())]

    def both_cores(self):
        finish(self.copies)
        self.met[...] = (self.g[self.links.core].astype(F32) + self.met[...].astype(F32)).astype(BF16)

    def scatter(self):
        self.both_cores()
        self.copies = [
            send(self.met.at[self.links.chip_of(k)], self.landed.at[k - 1], self.sems, k, self.links.chip_peer(k))
            for k in range(1, CHIPS)
        ]

    def gather(self):
        finish(self.copies)
        total = self.met[self.links.chip].astype(F32)
        for k in range(CHIPS - 1):
            total = total + self.landed[k].astype(F32)
        core, chip = self.links.core, self.links.chip
        self.full[core, chip] = total.astype(BF16)
        own = self.full.at[core, chip]
        self.copies = [send(own, own, self.sems, 15 + k, self.links.chip_peer(k)) for k in range(1, CHIPS)]

    def share(self):
        finish(self.copies)
        own = self.full.at[self.links.core]
        self.copies = [send(own, own, self.sems, 31, self.links.sibling())]

    def done(self):
        finish(self.copies)


class TwoAxes(Reduction):
    def __init__(self, links, g, met, landed, near, full, sems, first, second):
        super().__init__(links, g, met, landed, full, sems)
        self.near, self.first, self.second = near, first, second
        self.i, self.j = links.place[first], links.place[second]

    def scatter(self):
        self.both_cores()
        rank, peer = self.links.axis_rank, self.links.axis_peer
        self.copies = [
            send(self.met.at[rank(self.first, k)], self.landed.at[k - 1], self.sems, k, peer(self.first, k)) for k in (2, 1, 3)
        ]

    def scatter_second(self):
        finish(self.copies)
        total = self.met[self.i].astype(F32)
        for k in range(3):
            total = total + self.landed[k].astype(F32)
        self.met[self.i] = total.astype(BF16)
        rank, peer = self.links.axis_rank, self.links.axis_peer
        self.copies = [
            send(self.met.at[self.i, rank(self.second, k)], self.near.at[k - 1], self.sems, 3 + k, peer(self.second, k))
            for k in (2, 1, 3)
        ]

    def gather(self):
        finish(self.copies)
        total = self.met[self.i, self.j].astype(F32)
        for k in range(3):
            total = total + self.near[k].astype(F32)
        core = self.links.core
        self.full[core, self.i, self.j] = total.astype(BF16)
        own = self.full.at[core, self.i, self.j]
        self.copies = [send(own, own, self.sems, 6 + k, self.links.axis_peer(self.second, k)) for k in (2, 1, 3)]

    def gather_second(self):
        finish(self.copies)
        own = self.full.at[self.links.core, self.i]
        self.copies = [send(own, own, self.sems, 9 + k, self.links.axis_peer(self.first, k)) for k in (2, 1, 3)]


def body(
    x, seg_t, pad_t, pair_in, gain_one, gain_two, img_gain_one, img_gain_two,
    h_tok, h_iqkv, h_iout, h_iup, h_idown, h_iproj, h_qkv, h_out, h_up, h_down, h_proj,
    o_loss, o_input, o_norms, o_a, o_b, o_c, o_proj,
    tok, iw_qkv, iw_out, iw_up, iw_down, iw_proj, w_qkv, w_out, w_up, w_down, w_proj, load,
    ibias, iap, iqkv, stage, iy, ypool, ihsum, images,
    bias, mem, mem_t, pair, a1, qkv, probs, att, p_att, l_att, x1, x1_pool, a2, dgelu, hsum, p_pool, pools,
    tf, scale, pooled, s_ref, e_ref, row_sums, col_sums, dts, de, dz, gp, dx2, du, p_da2, l_da2, dx1, dy,
    dqkv, p_da1, l_da1, proj, proj_all, vec, vec_all,
    g_a, g_b, g_c, m_a, m_b, m_c, r_a, r_b, r_c, n_a, n_b, f_a, f_b, f_c,
    group_sems, image_sems, rank_sems, sum_sems, proj_sems, store_sems,
):
    links = Links()
    t, dp, core, chip = links.t, links.dp, links.core, links.chip
    loads = {}

    def fetch(at, name, src, dst):
        loads[name] = pltpu.make_async_copy(src, dst, load.at[at])
        loads[name].start()

    fetch(0, "tok", h_tok, tok)
    fetch(1, "iqkv", h_iqkv, iw_qkv)
    links.greet()
    text_norm_one(x, as_row(gain_one), a1, t)
    pair[t] = column(pair_in)
    links.met()
    copies = group_share(links, a1, group_sems.at[1])
    pair_copies = group_share(links, pair, group_sems.at[0])
    fetch(2, "qkv", h_qkv, w_qkv)
    fetch(3, "out", h_out, w_out)
    fetch(4, "iout", h_iout, iw_out)

    text_masks(seg_t, pad_t, bias, mem, mem_t)
    image_bias(ibias)
    loads["tok"].wait()
    image_norm_one(tok, as_row(img_gain_one), stage)
    fetch(5, "iup", h_iup, iw_up)
    fetch(6, "up", h_up, w_up)
    fetch(7, "down", h_down, w_down)
    fetch(8, "idown", h_idown, iw_down)
    fetch(9, "iproj", h_iproj, iw_proj)
    fetch(10, "proj", h_proj, w_proj)
    image_permute(stage, iap)
    loads["iqkv"].wait()
    image_qkv(iap, iw_qkv, iqkv)

    finish(copies)
    loads["qkv"].wait()
    loads["out"].wait()
    text_attention(a1, w_qkv, bias, w_out, qkv, probs, att, p_att)
    copies = group_scatter(links, p_att, l_att, group_sems.at[2])

    image_attention(iqkv, ibias, stage, 0, 8)
    loads["iout"].wait()
    image_out(stage, tok, iw_out, iy)
    image_norm_two(iy, as_row(img_gain_two), iap.at[:IROWS], ypool)

    finish(copies)
    text_norm_two(x, p_att, l_att, as_row(gain_two), mem, x1, a2, x1_pool, t)
    copies = group_share(links, a2, group_sems.at[3])
    text_pool_one(x1, mem, x1_pool, t)

    loads["iup"].wait()
    image_up(iap.at[:IROWS], iw_up, ihsum, 0, FF // UP_TILE)
    loads["idown"].wait()
    loads["iproj"].wait()
    images[core, chip] = image_finish(ihsum, ypool, iw_down, iw_proj)
    own = images.at[core, chip]
    image_copies = [send(own, own, image_sems, k, links.chip_peer(k)) for k in range(1, CHIPS)]

    finish(copies)
    loads["up"].wait()
    loads["down"].wait()
    text_up(a2, w_up, mem, w_down, x1_pool, dgelu, du, hsum, p_pool, pools, t)
    copies = group_share(links, pools, group_sems.at[4])
    finish(image_copies)
    own = images.at[core]
    image_copies = [send(own, own, image_sems, 0, links.sibling())]
    finish(pair_copies)
    loads["proj"].wait()
    finish(copies)
    text_embed(pools, mem, w_proj, pooled, tf, scale)
    finish(image_copies)

    score_sums(tf, images, s_ref, e_ref, row_sums, col_sums, t, dp)
    col_copies = rank_share(links, col_sums, rank_sems.at[0])
    row_copies = group_share(links, row_sums, group_sems.at[6])
    finish(col_copies)
    finish(row_copies)
    score_grad(s_ref, e_ref, row_sums, col_sums, pair, images, dts, vec, t)
    finish(group_share(links, dts, group_sems.at[7]))
    embed_grad(dts, tf, scale, w_proj, mem, de, dz, gp)

    red_a = TwoAxes(links, g_a, m_a, r_a, n_a, f_a, sum_sems.at[0], "x", "z")
    red_b = TwoAxes(links, g_b, m_b, r_b, n_b, f_b, sum_sems.at[1], "z", "x")
    red_c = Reduction(links, g_c, m_c, r_c, f_c, sum_sems.at[2])

    hidden_grad(dz, w_down, mem_t, dgelu, du)
    hidden_spread(du, w_up, p_da2)
    copies = group_scatter(links, p_da2, l_da2, group_sems.at[8])
    down_proj_grad(hsum, dz, de, pooled, proj, g_a, t)
    red_a.cores()
    row_grad(gp, mem, dx2, t)
    up_grad(a2, du, g_b)
    red_b.cores()
    red_a.scatter()
    red_b.scatter()
    finish(copies)
    norm_two_grad(p_da2, l_da2, x1, as_row(gain_two), dx2, dx1, dy, vec, t)
    copies = group_share(links, dy, group_sems.at[9])
    red_a.scatter_second()
    red_b.scatter_second()
    red_a.gather()
    red_b.gather()
    finish(copies)
    attention_grad(dy, w_out, w_qkv, qkv, probs, dqkv, p_da1)
    copies = group_scatter(links, p_da1, l_da1, group_sems.at[10])
    out_qkv_grad(att, dy, dqkv, a1, g_c)
    red_c.cores()
    red_a.gather_second()
    red_b.gather_second()
    red_c.scatter()
    finish(copies)
    norm_one_grad(p_da1, l_da1, x, as_row(gain_one), dx1, o_input, vec, t)
    vec_copies = group_share(links, vec, group_sems.at[11])
    red_a.share()
    red_b.share()
    proj_all[core, t] = f_a[core, 3, :3]
    own = proj_all.at[core, t]
    proj_copies = [send(own, own, proj_sems, k, links.group_peer(k)) for k in (2, 1, 3)]
    finish(vec_copies)
    vec_all[dp] = vec[0] + vec[1] + vec[2] + vec[3]
    vec_copies = rank_share(links, vec_all, rank_sems.at[1])
    red_c.gather()
    finish(proj_copies)
    own = proj_all.at[core]
    proj_copies = [send(own, own, proj_sems, 0, links.sibling())]
    red_a.done()
    red_b.done()
    stores = [pltpu.make_async_copy(f_a, o_a, store_sems.at[0]), pltpu.make_async_copy(f_b, o_b, store_sems.at[1])]
    for copy in stores:
        copy.start()
    finish(vec_copies)
    total = vec_all[0]
    for i in range(1, RANKS):
        total = total + vec_all[i]
    o_norms[...] = total[:, :1536]
    o_loss[...] = total[:, 1536:] * (1.0 / 4096.0)
    finish(proj_copies)
    stores.append(pltpu.make_async_copy(proj_all, o_proj, store_sems.at[2]))
    stores[-1].start()
    red_c.share()
    red_c.done()
    stores.append(pltpu.make_async_copy(f_c, o_c, store_sems.at[3]))
    stores[-1].start()
    for copy in stores:
        copy.wait()


def widen(
    loss, norms, h_input, h_a, h_b, h_c, h_proj,
    o_loss, o_input, o_one, o_two, o_down, o_up, o_out, o_qkv, o_proj,
    grad, full_a, full_b, full_c, full_proj, down, up, out, qkv, proj, loaded, stored,
):
    sources = ((h_a, full_a), (h_b, full_b), (h_proj, full_proj), (h_c, full_c), (h_input, grad))
    loads = [pltpu.make_async_copy(src, dst, loaded.at[i]) for i, (src, dst) in enumerate(sources)]
    for copy in loads:
        copy.start()
    stores = []

    def write(buf, target):
        stores.append(pltpu.make_async_copy(buf, target, stored.at[len(stores)]))
        stores[-1].start()

    def halves(target, parts, rows):
        for j in range(2):
            target[:, j * HALF : (j + 1) * HALF] = parts[j].reshape(rows, HALF).astype(F32)

    loads[0].wait()
    halves(down, full_a[:, :3], HID)
    write(down, o_down)
    loads[1].wait()
    halves(up, full_b, D)
    write(up, o_up)
    loads[2].wait()
    halves(proj, full_proj, D)
    write(proj, o_proj)
    loads[3].wait()
    halves(out, full_c[:, :4], BAND)
    write(out, o_out)
    halves(qkv, full_c[:, 4:], 3 * BAND)
    write(qkv, o_qkv)
    loads[4].wait()
    write(grad, o_input)
    o_loss[0, 0] = loss[0, 0]
    o_one[...] = norms[:, :D].reshape(D)
    o_two[...] = norms[:, D:].reshape(D)
    for copy in stores:
        copy.wait()


def on_device(
    text_input, segment_ids, pad_mask, pairing, ln_first, w_qkv, w_out, ln_second, w_up, w_down, text_proj,
    image_tokens, img_ln_first, img_w_qkv, img_w_out, img_ln_second, img_w_up, img_w_down, img_proj,
):
    vmem = pl.BlockSpec(memory_space=VM)
    hbm = pl.BlockSpec(memory_space=pl.ANY)
    shape = jax.ShapeDtypeStruct
    sums = ((4, 4, 64, HALF), (4, 4, 48, HALF), (16, 48, HALF))
    dma = pltpu.SemaphoreType.DMA
    scratch = [
        VM((IROWS, D), BF16), VM((3, D, D), BF16), VM((D, D), BF16), VM((D, FF), BF16), VM((FF, D), BF16), VM((D, D), BF16),
        VM((3, BAND, D), BF16), VM((BAND, D), BF16), VM((D, HID), BF16), VM((HID, D), BF16), VM((D, D), BF16), dma((11,)),
        VM((2 * PAIR, PAIR), F32), VM((PROWS, D), BF16), VM((3, PROWS, D), BF16), VM((6, PROWS, 128), F32), VM((IROWS, D), F32),
        VM((IMGS, D), F32), VM((IMGS, FF), F32), VM((2, CHIPS, IMGS, D), BF16),
        VM((4, 128, 128), F32), VM((CAPS, ROWS), BF16), VM((ROWS, 128), BF16), VM((GROUP, OWN_CAPS, 128), I32),
        VM((GROUP, OWN, D), BF16), VM((3, ROWS, BAND), BF16), VM((4, HALF, 128), F32), VM((ROWS, BAND), BF16),
        VM((GROUP, OWN, D), BF16), VM((3, OWN, D), BF16), VM((OWN, D), F32), VM((OWN_CAPS, D), F32), VM((GROUP, OWN, D), BF16),
        VM((ROWS, HID), F32), VM((CAPS, HID), F32), VM((GROUP, OWN_CAPS, D), F32), VM((GROUP, CAPS, D), BF16),
        VM((CAPS, D), F32), VM((CAPS, 128), F32), VM((CAPS, D), BF16), VM((CAPS, ROWS), F32),
        VM((CAPS, ROWS), F32), VM((GROUP, CAPS, 128), F32), VM((RANKS, 1, ROWS), F32), VM((GROUP, CAPS, D), BF16),
        VM((CAPS, D), BF16), VM((CAPS, D), BF16), VM((CAPS, D), F32),
        VM((OWN, D), F32), VM((ROWS, HID), BF16), VM((GROUP, OWN, D), BF16), VM((3, OWN, D), BF16), VM((OWN, D), F32),
        VM((GROUP, OWN, D), BF16), VM((3, ROWS, BAND), BF16), VM((GROUP, OWN, D), BF16), VM((3, OWN, D), BF16),
        VM((GROUP, BAND, D), BF16), VM((2, GROUP, 3, 64, HALF), BF16), VM((GROUP, 1, VEC), F32), VM((RANKS, 1, VEC), F32),
    ]
    scratch += [VM((2,) + s, BF16) for s in sums] + [VM(s, BF16) for s in sums]
    scratch += [VM((3,) + sums[0][1:], BF16), VM((3,) + sums[1][1:], BF16), VM((15,) + sums[2][1:], BF16)]
    scratch += [VM((3,) + s[2:], BF16) for s in sums[:2]] + [VM((2,) + s, BF16) for s in sums]
    scratch += [dma((12, 2, 3)), dma((2, 16)), dma((2, 2, 31)), dma((3, 2, 32)), dma((2, 4)), dma((4,))]
    loss, input_grad, norms, full_a, full_b, full_c, full_proj = pl.pallas_call(
        body,
        out_shape=(
            shape((1, 128), F32), shape((OWN, D), F32), shape((1, 1536), F32),
            *(shape((2,) + s, BF16) for s in sums), shape((2, GROUP, 3, 64, HALF), BF16),
        ),
        in_specs=[vmem] * 3 + [pl.BlockSpec(memory_space=pltpu.SMEM)] + [vmem] * 4 + [hbm] * 11,
        out_specs=(vmem, vmem, vmem, hbm, hbm, hbm, hbm),
        scratch_shapes=scratch,
        compiler_params=pltpu.CompilerParams(collective_id=0, has_side_effects=True, vmem_limit_bytes=63 << 20),
        name="lit",
    )(
        text_input, segment_ids.T, pad_mask.T, pairing, ln_first, ln_second, img_ln_first, img_ln_second,
        image_tokens.transpose(1, 0, 2).reshape(IROWS, D), img_w_qkv, img_w_out, img_w_up, img_w_down, img_proj,
        w_qkv.swapaxes(1, 2), w_out, w_up, w_down, text_proj,
    )

    loss, input_grad, one, two, down, up, out, qkv, proj = pl.pallas_call(
        widen,
        out_shape=(
            shape((1, 1), F32), shape((OWN, D), F32), shape((D,), F32), shape((D,), F32), shape((HID, D), F32),
            shape((D, HID), F32), shape((BAND, D), F32), shape((3 * BAND, D), F32), shape((D, D), F32),
        ),
        in_specs=[vmem] * 2 + [hbm] * 5,
        out_specs=(pl.BlockSpec(memory_space=pltpu.SMEM), hbm, vmem, vmem, hbm, hbm, hbm, hbm, hbm),
        scratch_shapes=[
            VM((OWN, D), F32), *(VM((2,) + s, BF16) for s in sums), VM((2, GROUP, 3, 64, HALF), BF16),
            VM((HID, D), F32), VM((D, HID), F32), VM((BAND, D), F32), VM((3 * BAND, D), F32), VM((D, D), F32),
            dma((5,)), dma((6,)),
        ],
        compiler_params=pltpu.CompilerParams(vmem_limit_bytes=60 << 20),
        name="widen",
    )(loss, norms, input_grad, full_a, full_b, full_c, full_proj)
    return (loss.reshape(()), input_grad, one, qkv.reshape(3, BAND, D).swapaxes(1, 2), out, two, up, down, proj)


def solution(mesh):
    rows = P(("dp", "tensor"))
    in_specs = (
        P(("dp", "tensor"), None), P("dp", None), P("dp", None), rows, P(), P(None, None, "tensor"), P("tensor", None), P(),
        P(None, "tensor"), P("tensor", None), P(), P(("dp", "tensor"), None, None), P(), P(), P(), P(), P(), P(), P(),
    )
    out_specs = (
        P(), P(("dp", "tensor"), None), P(), P(None, None, "tensor"), P("tensor", None), P(), P(None, "tensor"),
        P("tensor", None), P(),
    )
    return jax.shard_map(on_device, mesh=mesh, in_specs=in_specs, out_specs=out_specs, check_vma=False)
```

```python
import jax, jax.numpy as jnp
from jax import lax
from jax.experimental import pallas as pl
from jax.experimental.pallas import tpu as pltpu
from jax.sharding import PartitionSpec as P

F32, BF16, I32 = jnp.float32, jnp.bfloat16, jnp.int32
VM = pltpu.VMEM
EPS = 1e-6
NEG = -1e30
D, FF, HID = 768, 3072, 768
IMGS, POS = 16, 50
IROWS = IMGS * POS
HALFP = 56
PAIR = 2 * HALFP
PROWS = PAIR * (IMGS // 2)
TILE = 256
UP_TILE = 768


def dot(a, b):
    return jnp.dot(a, b, preferred_element_type=F32)


def dot_t(a, b):
    return lax.dot_general(a, b, (((1,), (1,)), ((), ())), preferred_element_type=F32)


def t_dot(a, b):
    return lax.dot_general(a, b, (((0,), (0,)), ((), ())), preferred_element_type=F32)


def iota(shape, axis):
    return lax.broadcasted_iota(I32, shape, axis)


def normalized(values):
    centred = values - jnp.mean(values, axis=-1, keepdims=True)
    spread = jnp.mean(centred * centred, axis=-1, keepdims=True)
    scale = lax.rsqrt(spread + EPS)
    return centred * scale, scale


def normal_cdf(u):
    return 0.5 + 0.5 * lax.erf(u * 0.7071067811865476)


def image_bias(bias):
    q, k = iota((2 * PAIR, PAIR), 0), iota((2 * PAIR, PAIR), 1)
    q = jnp.where(q >= PAIR, q - PAIR, q)
    place = jnp.where(k >= HALFP, k - HALFP, k)
    bias[...] = jnp.where(((q >= HALFP) == (k >= HALFP)) & (place < POS), 0.0, NEG)


def image_norm_one(tok, gain, stage):
    def rows(i, c):
        s = pl.ds(pl.multiple_of(i * 160, 160), 160)
        n, _ = normalized(tok[s, :].astype(F32))
        n = n * gain
        for h in range(6):
            stage[h, s, :] = n[:, h * 128 : h * 128 + 128]
        return c

    lax.fori_loop(0, 5, rows, 0)
    stage[:, IROWS:, :] = jnp.zeros((6, PROWS - IROWS, 128), F32)


def tiles(n, body):
    def step(i, c):
        body(i, pl.ds(pl.multiple_of(i * TILE, TILE), TILE))
        return c

    lax.fori_loop(0, n, step, 0)


def image_permute(stage, iap):
    def pair(p, c):
        for h in range(6):
            both = [stage[h, pl.ds(2 * p + i, HALFP, stride=IMGS), :] for i in range(2)]
            iap[pl.ds(pl.multiple_of(p * PAIR, PAIR), PAIR), h * 128 : h * 128 + 128] = jnp.concatenate(both, axis=0).astype(BF16)
        return c
    lax.fori_loop(0, IMGS // 2, pair, 0)


def image_qkv(iap, w, iqkv):
    def step(j, c):
        iqkv[j] = dot(iap[...], w[j]).astype(BF16)
        return c
    lax.fori_loop(0, 3, step, 0)


def stacked(values, low):
    zero = jnp.zeros_like(values)
    return jnp.concatenate([jnp.where(low, values, zero), jnp.where(low, zero, values)], axis=0)


def image_attention(iqkv, bias, stage, first, last, unroll=1):
    low = iota((PAIR, 128), 1) < 64

    def pair(p, c):
        rows = pl.ds(pl.multiple_of(p * PAIR, PAIR), PAIR)
        ones = jnp.ones((PAIR, 128), BF16)
        cols = [pl.ds(h * 128, 128) for h in range(6)]
        s = [dot_t(stacked(iqkv[0, rows, h], low), iqkv[1, rows, h]) * 0.125 + bias[...] for h in cols]
        e = [jnp.exp(x - jnp.max(x, axis=-1, keepdims=True)).astype(BF16) for x in s]
        for i, (h, x) in enumerate(zip(cols, e)):
            o = dot(x, jnp.concatenate([iqkv[2, rows, h], ones], axis=1))
            o = jnp.where(low, o[:PAIR, :128], o[PAIR:, :128]) / jnp.where(low, o[:PAIR, 128:], o[PAIR:, 128:])
            stage[i, pl.ds(2 * p, HALFP, stride=IMGS), :] = o[:HALFP]
            stage[i, pl.ds(2 * p + 1, HALFP, stride=IMGS), :] = o[HALFP:]
        return c

    lax.fori_loop(first, last, pair, 0, unroll=unroll)


def image_out(stage, tok, w, iy):
    def rows(i, c):
        s = pl.ds(pl.multiple_of(i * 160, 160), 160)
        iy[s, :] = tok[s, :].astype(F32) + dot(jnp.concatenate([stage[h, s, :].astype(BF16) for h in range(6)], axis=1), w[...])
        return c
    lax.fori_loop(0, 5, rows, 0)


def image_norm_two(iy, gain, ia, ypool):
    ypool[...] = jnp.zeros_like(ypool)
    def rows(i, c):
        s = pl.ds(pl.multiple_of(i * 160, 160), 160)
        y = iy[s, :]
        ypool[...] += jnp.sum(y.reshape(10, IMGS, D), axis=0)
        n, _ = normalized(y)
        ia[s, :] = (n * gain).astype(BF16)
        return c
    lax.fori_loop(0, 5, rows, 0)


def image_up(ia, w, hsum, first, last):
    def step(i, c):
        s = pl.ds(pl.multiple_of(i * UP_TILE, UP_TILE), UP_TILE)
        for m in range(5):
            u = dot(ia[160 * m : 160 * m + 160, :], w[:, s])
            part = jnp.sum((u * normal_cdf(u)).reshape(10, IMGS, UP_TILE), axis=0)
            total = part if m == 0 else total + part
        hsum[:, s] = total
        return c
    lax.fori_loop(first, last, step, 0)


def as_row(gain):
    return gain[...].reshape(1, D)


def column(values):
    rows = iota((OWN_CAPS, 128), 0)
    out = jnp.zeros((OWN_CAPS, 128), I32)
    for i in range(OWN_CAPS):
        out = jnp.where(rows == i, values[i], out)
    return out


def split_rows(x):
    hi = x.astype(BF16)
    return jnp.concatenate([hi, (x - hi.astype(F32)).astype(BF16)], axis=0)


def image_finish(hsum, ypool, w_down, w_proj):
    both = dot(split_rows(hsum[...]), w_down[...])
    pooled = ((ypool[...] + both[:IMGS] + both[IMGS:]) * (1.0 / POS)).astype(BF16)
    e = dot(pooled, w_proj[...])
    return (e * lax.rsqrt(jnp.sum(e * e, axis=-1, keepdims=True) + EPS)).astype(BF16)


GROUP, RANKS, CHIPS = 4, 32, 16
OWN, ROWS = 128, 512
CAPS, OWN_CAPS = 64, 16
BAND = 192
HALF = 384
MESH = pl.DeviceIdType.MESH
VEC = 1664
PAIRS = 34


class Links:
    def __init__(self):
        self.dp, self.t = lax.axis_index("dp"), lax.axis_index("tensor")
        self.core, self.chip = lax.rem(self.dp, 2), self.dp // 2
        self.place = {"x": lax.rem(self.chip, 4), "z": self.chip // 4}

    def rank(self, k):
        return lax.rem(self.t + k, GROUP)

    def group_peer(self, k):
        return {"dp": self.dp, "tensor": self.rank(k)}

    def rank_peer(self, k):
        return {"dp": lax.rem(self.dp + k, RANKS), "tensor": self.t}

    def chip_of(self, k):
        return lax.rem(self.chip + k, CHIPS)

    def chip_peer(self, k):
        return {"dp": 2 * self.chip_of(k) + self.core, "tensor": self.t}

    def axis_rank(self, axis, k):
        return lax.rem(self.place[axis] + k, 4)

    def axis_peer(self, axis, k):
        place = dict(self.place)
        place[axis] = self.axis_rank(axis, k)
        return {"dp": 2 * (place["z"] * 4 + place["x"]) + self.core, "tensor": self.t}

    def sibling(self):
        return {"dp": self.dp + 1 - 2 * self.core, "tensor": self.t}

    def greet(self):
        barrier = pltpu.get_barrier_semaphore()
        for k in range(1, GROUP):
            pl.semaphore_signal(barrier, 1, device_id=self.group_peer(k), device_id_type=MESH)
        for k in range(1, RANKS):
            pl.semaphore_signal(barrier, 1, device_id=self.rank_peer(k), device_id_type=MESH)

    def met(self):
        pl.semaphore_wait(pltpu.get_barrier_semaphore(), GROUP - 1 + RANKS - 1)


def send(src, dst, sems, peer):
    pltpu.make_async_remote_copy(src, dst, sems.at[0], sems.at[1], device_id=peer, device_id_type=MESH).start()


def finish(exchange):
    sems, span = exchange
    for i in range(2):
        pltpu.make_async_copy(span, span, sems.at[i]).wait()


def group_share(links, buf, sems):
    own = buf.at[links.t]
    for k in (2, 1, 3):
        send(own, own, sems, links.group_peer(k))
    return sems, buf.at[pl.ds(0, 3)]


def group_scatter(links, parts, landed, sems):
    for k in (2, 1, 3):
        send(parts.at[links.rank(k)], landed.at[k - 1], sems, links.group_peer(k))
    return sems, landed


def rank_share(links, buf, sems):
    own = buf.at[links.dp]
    for k in range(1, RANKS):
        send(own, own, sems, links.rank_peer(k))
    return sems, buf.at[pl.ds(0, RANKS - 1)]


def chip_share(links, buf, sems):
    own = buf.at[links.chip]
    for k in range(1, CHIPS):
        send(own, own, sems, links.chip_peer(k))
    return sems, buf.at[pl.ds(0, CHIPS - 1)]


def sibling_send(links, src, dst, sems):
    send(src, dst, sems, links.sibling())
    return sems, src


def text_masks(seg_t, pad_t, bias, mem, mem_t):
    seg, pad = seg_t[...].astype(F32).astype(BF16), pad_t[...].astype(F32).astype(BF16)

    def as_column(values):
        pick = jnp.where(iota((ROWS, 32), 0) >> 4 == iota((ROWS, 32), 1), 1.0, 0.0).astype(BF16)
        wide = dot_t(pick, values)
        return jnp.sum(jnp.where(iota((ROWS, 16), 0) & 15 == iota((ROWS, 16), 1), wide, 0.0), axis=1, keepdims=True)

    def as_row(values):
        pick = jnp.where(iota((32, ROWS), 1) >> 4 == iota((32, ROWS), 0), 1.0, 0.0).astype(BF16)
        wide = dot(values, pick)
        return jnp.sum(jnp.where(iota((16, ROWS), 1) & 15 == iota((16, ROWS), 0), wide, 0.0), axis=0, keepdims=True)

    cap_col = as_column(seg) + ((iota((ROWS, 1), 0) >> 4) * 2).astype(F32)
    key_col = jnp.where(as_column(pad) > 0.5, cap_col, -1.0)
    cap_row = as_row(seg) + ((iota((1, ROWS), 1) >> 4) * 2).astype(F32)
    key_row = jnp.where(as_row(pad) > 0.5, cap_row, -1.0)
    for b in range(4):
        rows = slice(128 * b, 128 * b + 128)
        bias[b] = jnp.where(cap_col[rows] == key_row[:, rows], 0.0, NEG)
    mem[...] = jnp.where(iota((CAPS, ROWS), 0).astype(F32) == key_row, 1.0, 0.0).astype(BF16)
    mem_t[...] = jnp.where((iota((ROWS, 128), 1) & 63).astype(F32) == key_col, 1.0, 0.0).astype(BF16)


def text_norm_one(x, gain, a1, t):
    n, _ = normalized(x[...].astype(F32))
    a1[t] = (n * gain).astype(BF16)


def low_half():
    return iota((OWN, 128), 1) < 64


def text_attention(a1, w_t, bias, w_out, qkv, probs, att, parts):
    rows_all = a1[...].reshape(ROWS, D)
    for j in range(3):
        qkv[j] = dot_t(rows_all, w_t[j]).astype(BF16)
    low = low_half()
    blocks = [slice(128 * b, 128 * b + 128) for b in range(4)]
    scores = []
    for b, rows in enumerate(blocks):
        mask = bias[b]
        scores.append(dot_t(stacked(qkv[0, rows, :128], low), qkv[1, rows, :128]) * 0.125 + jnp.concatenate([mask, mask], axis=0))
        scores.append(dot_t(qkv[0, rows, 128:], qkv[1, rows, 128:]) * 0.125 + mask)
    powers = [jnp.exp(x - jnp.max(x, axis=-1, keepdims=True)) for x in scores]
    shares = [x / jnp.sum(x, axis=-1, keepdims=True) for x in powers]
    for b, rows in enumerate(blocks):
        probs[b, :256] = shares[2 * b]
        probs[b, 256:] = shares[2 * b + 1]
        o = dot(shares[2 * b].astype(BF16), qkv[2, rows, :128])
        att[rows, :128] = jnp.where(low, o[:128], o[128:]).astype(BF16)
        att[rows, 128:] = dot(shares[2 * b + 1].astype(BF16), qkv[2, rows, 128:]).astype(BF16)
    parts[...] = dot(att[...], w_out[...]).astype(BF16).reshape(GROUP, OWN, D)


def summed(parts, landed, t):
    return parts[t].astype(F32) + landed[0].astype(F32) + landed[1].astype(F32) + landed[2].astype(F32)


def split3(x):
    hi = x.astype(BF16)
    rest = x - hi.astype(F32)
    mid = rest.astype(BF16)
    return jnp.concatenate([hi, mid, (rest - mid.astype(F32)).astype(BF16)], axis=0)


def own_member(mem, t):
    return mem[pl.ds(pl.multiple_of(t * OWN_CAPS, OWN_CAPS), OWN_CAPS), pl.ds(pl.multiple_of(t * OWN, OWN), OWN)]


def text_norm_two(x, parts, landed, gain, mem, x1, a2, x1_pool, t):
    y = x[...].astype(F32) + summed(parts, landed, t)
    x1[...] = y
    n, _ = normalized(y)
    a2[t] = (n * gain).astype(BF16)


def text_pool_one(x1, mem, x1_pool, t):
    own = own_member(mem, t)
    x1_pool[...] = dot(jnp.concatenate([own, own, own], axis=1), split3(x1[...]))


def text_up(a2, w_up, mem, w_down, x1_pool, dgelu, hidden, hsum, part, parts, t):
    for r in range(GROUP):
        rows = slice(r * OWN, r * OWN + OWN)
        u = dot(a2[r], w_up[...])
        phi = normal_cdf(u)
        dgelu[rows, :] = phi + u * (jnp.exp(u * u * -0.5) * 0.3989422804014327)
        hidden[rows, :] = (u * phi).astype(BF16)
    hsum[...] = dot(mem[...], hidden[...])
    both = dot(split_rows(hsum[...]), w_down[...])
    part[...] = (both[:CAPS] + both[CAPS:]).reshape(GROUP, OWN_CAPS, D)
    part[t] += x1_pool[...]
    parts[t] = part[...].reshape(CAPS, D).astype(BF16)


def counts_of(mem):
    return jnp.sum(mem.astype(F32), axis=1, keepdims=True)


def text_embed(parts, mem, w_proj, pooled, tf, scale):
    total = parts[0].astype(F32) + parts[1].astype(F32) + parts[2].astype(F32) + parts[3].astype(F32)
    rows = (total / counts_of(mem[...])).astype(BF16)
    pooled[...] = rows
    e = dot(rows, w_proj[...])
    rs = lax.rsqrt(jnp.sum(e * e, axis=-1, keepdims=True) + EPS)
    tf[...] = rs * e
    scale[...] = jnp.broadcast_to(rs, (CAPS, 128))


def score_sums(tf, images, s_ref, e_ref, row_sums, col_sums, t, dp):
    s = 40.0 * dot_t(tf[...].astype(BF16), images[...].reshape(ROWS, D))
    s_ref[...] = s
    e = jnp.exp(s - 40.0)
    e_ref[...] = e
    row_sums[t] = jnp.broadcast_to(jnp.sum(e, axis=1, keepdims=True), (CAPS, 128))
    col_sums[dp] = jnp.sum(e, axis=0, keepdims=True)


def score_grad(s_ref, e_ref, row_sums, col_sums, pair, images, dts, vec, t):
    rows = jnp.sum(row_sums[...], axis=0)[:, :1]
    cols = col_sums[0]
    for i in range(1, RANKS):
        cols = cols + col_sums[i]
    lane = iota((CAPS, ROWS), 1)
    image = ((lane >> 4) & 15) * (2 * CAPS) + (lane >> 8) * CAPS + (lane & 15) + OWN_CAPS * t
    target = jnp.where(pair[...].reshape(CAPS, 128)[:, :1] == image, 1.0, 0.0)
    g = 0.5 * (e_ref[...] / rows + e_ref[...] / cols) - target
    dts[t] = (40.0 * dot(g.astype(BF16), images[...].reshape(ROWS, D))).astype(BF16)
    loss = (
        jnp.sum(40.0 + jnp.log(rows), axis=0, keepdims=True) * (1.0 / GROUP)
        + jnp.sum(40.0 + jnp.log(cols), axis=1, keepdims=True) * (1.0 / RANKS)
        - 2.0 * jnp.sum(jnp.sum(s_ref[...] * target, axis=1, keepdims=True), axis=0, keepdims=True)
    )
    vec[t, :, 1536:] = jnp.broadcast_to(loss, (1, 128))


def embed_grad(dts, tf, scale, w_proj, mem, de_ref, dz_ref, gp_ref):
    dt = dts[0].astype(F32) + dts[1].astype(F32) + dts[2].astype(F32) + dts[3].astype(F32)
    f = tf[...]
    de = (scale[:, :1] * (dt - f * jnp.sum(f * dt, axis=-1, keepdims=True))).astype(BF16)
    gp = dot_t(de, w_proj[...]) / counts_of(mem[...])
    de_ref[...] = de
    gp_ref[...] = gp
    dz_ref[...] = gp.astype(BF16)


def row_grad(gp_ref, mem, dx2, t):
    own = own_member(mem, t)
    gp = gp_ref[pl.ds(pl.multiple_of(t * OWN_CAPS, OWN_CAPS), OWN_CAPS), :]
    dx2[...] = t_dot(jnp.concatenate([own, own, own], axis=0), split3(gp))


def hidden_grad(dz, w_down, mem_t, dgelu, du):
    dh = split_rows(dot_t(dz[...], w_down[...]))
    for i in range(3):
        s = slice(i * TILE, i * TILE + TILE)
        du[:, s] = (dot(mem_t[...], dh[:, s]) * dgelu[:, s]).astype(BF16)


def hidden_spread(du, w_up, parts):
    parts[...] = dot_t(du[...], w_up[...]).astype(BF16).reshape(GROUP, OWN, D)


def put_halves(g, first, count, rows, values):
    for j in range(2):
        part = values[:, j * HALF : (j + 1) * HALF].reshape(count, rows, HALF).astype(BF16)
        if len(g.shape) == 4:
            g[j, first : first + count] = part
        elif count == 3:
            g[j, first // 4, :3] = part
        else:
            g[j, first // 4 : (first + count) // 4] = part.reshape(count // 4, 4, rows, HALF)


def down_proj_grad(hsum, dz, de, pooled, proj, g, t):
    hs = split_rows(hsum[...])
    dz2 = jnp.concatenate([dz[...], dz[...]], axis=0)
    for i in range(3):
        put_halves(g, 4 * i, 4, 64, t_dot(hs[:, i * TILE : (i + 1) * TILE], dz2))
    proj[...] = t_dot(pooled[...], de[...]).astype(BF16).reshape(GROUP, BAND, D)
    put_halves(g, 12, 3, 64, proj[t])
    g[:, 3, 3] = jnp.zeros((2, 64, HALF), BF16)


def up_grad(a2, du, g):
    for i in range(2):
        rows = a2[:, :, i * HALF : (i + 1) * HALF].reshape(ROWS, HALF)
        put_halves(g, 8 * i, 8, 48, t_dot(rows, du[...]))


def norm_two_grad(parts, landed, x1, gain, dx2, dx1, dy, vec, t):
    da = summed(parts, landed, t)
    n, scale = normalized(x1[...])
    vec[t, :, 768:1536] = jnp.sum(da * n, axis=0, keepdims=True)
    h = da * gain
    g = dx2[...] + (h - jnp.mean(h, axis=-1, keepdims=True) - n * jnp.mean(h * n, axis=-1, keepdims=True)) * scale
    dx1[...] = g
    dy[t] = g.astype(BF16)


def attention_grad(dy, w_out, w_t, qkv, probs, dqkv, parts):
    datt = dot_t(dy[...].reshape(ROWS, D), w_out[...]).astype(BF16)
    low = low_half()
    blocks = [slice(128 * b, 128 * b + 128) for b in range(4)]
    sides, raw = [], []
    for b, rows in enumerate(blocks):
        sides.append((stacked(qkv[0, rows, :128], low), stacked(datt[rows, :128], low)))
        sides.append((qkv[0, rows, 128:], datt[rows, 128:]))
        raw.append(dot_t(sides[-2][1], qkv[2, rows, :128]))
        raw.append(dot_t(sides[-1][1], qkv[2, rows, 128:]))
    probs_of = [probs[b, part] for b in range(4) for part in (slice(0, 256), slice(256, 384))]
    ds = [(p * (x - jnp.sum(p * x, axis=-1, keepdims=True))).astype(BF16) for p, x in zip(probs_of, raw)]
    for b, rows in enumerate(blocks):
        for i, cols in ((2 * b, slice(0, 128)), (2 * b + 1, slice(128, BAND))):
            o = dot(ds[i], qkv[1, rows, cols])
            if i % 2 == 0:
                o = jnp.where(low, o[:128], o[128:])
            dqkv[0, rows, cols] = (o * 0.125).astype(BF16)
            dqkv[1, rows, cols] = (t_dot(ds[i], sides[i][0]) * 0.125).astype(BF16)
            dqkv[2, rows, cols] = t_dot(probs_of[i].astype(BF16), sides[i][1]).astype(BF16)
    total = dot(dqkv[0], w_t[0]) + dot(dqkv[1], w_t[1]) + dot(dqkv[2], w_t[2])
    parts[...] = total.astype(BF16).reshape(GROUP, OWN, D)


def out_qkv_grad(att, dy, dqkv, a1, g):
    put_halves(g, 0, 4, 48, t_dot(att[...], dy[...].reshape(ROWS, D)))
    for j in range(3):
        put_halves(g, 4 + 4 * j, 4, 48, t_dot(dqkv[j], a1[...].reshape(ROWS, D)))


def norm_one_grad(parts, landed, x, gain, dx1, out, vec, t):
    da = summed(parts, landed, t)
    n, scale = normalized(x[...].astype(F32))
    vec[t, :, :768] = jnp.sum(da * n, axis=0, keepdims=True)
    h = da * gain
    out[...] = dx1[...] + (h - jnp.mean(h, axis=-1, keepdims=True) - n * jnp.mean(h * n, axis=-1, keepdims=True)) * scale


class Reduction:
    def __init__(self, links, g, met, landed, full, pair):
        self.links, self.g, self.met, self.landed, self.full, self.pair = links, g, met, landed, full, pair

    def cores(self):
        self.open = sibling_send(self.links, self.g.at[1 - self.links.core], self.met, self.pair())

    def both_cores(self):
        finish(self.open)
        self.met[...] = (self.g[self.links.core].astype(F32) + self.met[...].astype(F32)).astype(BF16)

    def scatter(self):
        self.both_cores()
        sems = self.pair()
        for k in range(1, CHIPS):
            send(self.met.at[self.links.chip_of(k)], self.landed.at[k - 1], sems, self.links.chip_peer(k))
        self.open = sems, self.landed

    def gather(self):
        finish(self.open)
        total = self.met[self.links.chip].astype(F32)
        for k in range(CHIPS - 1):
            total = total + self.landed[k].astype(F32)
        half = self.full.at[self.links.core]
        half[self.links.chip] = total.astype(BF16)
        self.open = chip_share(self.links, half, self.pair())

    def share(self):
        finish(self.open)
        half = self.full.at[self.links.core]
        self.open = sibling_send(self.links, half, half, self.pair())

    def done(self):
        finish(self.open)


class TwoAxes(Reduction):
    def __init__(self, links, g, met, landed, near, full, pair, first, second):
        super().__init__(links, g, met, landed, full, pair)
        self.near, self.first, self.second = near, first, second
        self.i, self.j = links.place[first], links.place[second]

    def spread(self, axis, source, target):
        sems = self.pair()
        for k in (2, 1, 3):
            send(source(k), target(k), sems, self.links.axis_peer(axis, k))
        return sems

    def scatter(self):
        self.both_cores()
        sems = self.spread(
            self.first, lambda k: self.met.at[self.links.axis_rank(self.first, k)], lambda k: self.landed.at[k - 1]
        )
        self.open = sems, self.landed

    def scatter_second(self):
        finish(self.open)
        total = self.met[self.i].astype(F32)
        for k in range(3):
            total = total + self.landed[k].astype(F32)
        self.met[self.i] = total.astype(BF16)
        sems = self.spread(
            self.second, lambda k: self.met.at[self.i, self.links.axis_rank(self.second, k)], lambda k: self.near.at[k - 1]
        )
        self.open = sems, self.near

    def gather(self):
        finish(self.open)
        total = self.met[self.i, self.j].astype(F32)
        for k in range(3):
            total = total + self.near[k].astype(F32)
        core = self.links.core
        self.full[core, self.i, self.j] = total.astype(BF16)
        own = self.full.at[core, self.i, self.j]
        self.open = self.spread(self.second, lambda k: own, lambda k: own), self.full.at[0, 0, pl.ds(0, 3)]

    def gather_second(self):
        finish(self.open)
        own = self.full.at[self.links.core, self.i]
        self.open = self.spread(self.first, lambda k: own, lambda k: own), self.full.at[0, pl.ds(0, 3)]


def body(
    x, seg_t, pad_t, pair_in, gain_one, gain_two, img_gain_one, img_gain_two,
    h_tok, h_iqkv, h_iout, h_iup, h_idown, h_iproj, h_qkv, h_out, h_up, h_down, h_proj,
    o_loss, o_input, o_norms, f_a, f_b, f_c, proj_all,
    tok, iw_qkv, iw_out, iw_up, iw_down, iw_proj, w_qkv, w_out, w_up, w_down, w_proj, load,
    ibias, iap, iqkv, stage, iy, ypool, ihsum, images,
    bias, mem, mem_t, pair, a1, qkv, probs, att, p_att, l_att, x1, x1_pool, a2, dgelu, hsum, p_pool, pools,
    tf, scale, pooled, s_ref, e_ref, row_sums, col_sums, dts, de, dz, gp, dx2, du, p_da2, l_da2, dx1, dy,
    dqkv, p_da1, l_da1, proj, vec, vec_all,
    g_a, g_b, g_c, m_a, m_b, m_c, r_a, r_b, r_c, n_a, n_b,
    sems,
):
    links = Links()
    t, dp, core, chip = links.t, links.dp, links.core, links.chip
    loads = {}
    count = iter(range(PAIRS))

    def pair_of():
        return sems.at[next(count)]


    def fetch(at, name, src, dst):
        loads[name] = pltpu.make_async_copy(src, dst, load.at[at])
        loads[name].start()

    fetch(0, "tok", h_tok, tok)
    fetch(1, "iqkv", h_iqkv, iw_qkv)
    links.greet()
    text_norm_one(x, as_row(gain_one), a1, t)
    pair[t] = column(pair_in)
    links.met()
    copies = group_share(links, a1, pair_of())
    pair_copies = group_share(links, pair, pair_of())
    fetch(2, "qkv", h_qkv, w_qkv)
    fetch(3, "out", h_out, w_out)
    fetch(4, "iout", h_iout, iw_out)

    text_masks(seg_t, pad_t, bias, mem, mem_t)
    image_bias(ibias)
    loads["tok"].wait()
    image_norm_one(tok, as_row(img_gain_one), stage)
    fetch(5, "iup", h_iup, iw_up)
    fetch(6, "up", h_up, w_up)
    fetch(7, "down", h_down, w_down)
    fetch(8, "idown", h_idown, iw_down)
    fetch(9, "iproj", h_iproj, iw_proj)
    fetch(10, "proj", h_proj, w_proj)
    image_permute(stage, iap)
    loads["iqkv"].wait()
    image_qkv(iap, iw_qkv, iqkv)

    finish(copies)
    loads["qkv"].wait()
    loads["out"].wait()
    text_attention(a1, w_qkv, bias, w_out, qkv, probs, att, p_att)
    copies = group_scatter(links, p_att, l_att, pair_of())

    image_attention(iqkv, ibias, stage, 0, 8)
    loads["iout"].wait()
    image_out(stage, tok, iw_out, iy)
    image_norm_two(iy, as_row(img_gain_two), iap.at[:IROWS], ypool)

    loads["iup"].wait()
    image_up(iap.at[:IROWS], iw_up, ihsum, 0, 1)
    finish(copies)
    text_norm_two(x, p_att, l_att, as_row(gain_two), mem, x1, a2, x1_pool, t)
    copies = group_share(links, a2, pair_of())
    text_pool_one(x1, mem, x1_pool, t)

    image_up(iap.at[:IROWS], iw_up, ihsum, 1, FF // UP_TILE)
    loads["idown"].wait()
    loads["iproj"].wait()
    images[core, chip] = image_finish(ihsum, ypool, iw_down, iw_proj)
    image_copies = chip_share(links, images.at[core], pair_of())

    finish(copies)
    loads["up"].wait()
    loads["down"].wait()
    text_up(a2, w_up, mem, w_down, x1_pool, dgelu, du, hsum, p_pool, pools, t)
    copies = group_share(links, pools, pair_of())
    finish(image_copies)
    image_copies = sibling_send(links, images.at[core], images.at[core], pair_of())
    finish(pair_copies)
    loads["proj"].wait()
    finish(copies)
    text_embed(pools, mem, w_proj, pooled, tf, scale)
    finish(image_copies)

    score_sums(tf, images, s_ref, e_ref, row_sums, col_sums, t, dp)
    col_copies = rank_share(links, col_sums, pair_of())
    row_copies = group_share(links, row_sums, pair_of())
    finish(col_copies)
    finish(row_copies)
    score_grad(s_ref, e_ref, row_sums, col_sums, pair, images, dts, vec, t)
    finish(group_share(links, dts, pair_of()))
    embed_grad(dts, tf, scale, w_proj, mem, de, dz, gp)

    red_a = TwoAxes(links, g_a, m_a, r_a, n_a, f_a, pair_of, "x", "z")
    red_b = TwoAxes(links, g_b, m_b, r_b, n_b, f_b, pair_of, "z", "x")
    red_c = Reduction(links, g_c, m_c, r_c, f_c, pair_of)

    hidden_grad(dz, w_down, mem_t, dgelu, du)
    hidden_spread(du, w_up, p_da2)
    copies = group_scatter(links, p_da2, l_da2, pair_of())
    down_proj_grad(hsum, dz, de, pooled, proj, g_a, t)
    red_a.cores()
    row_grad(gp, mem, dx2, t)
    up_grad(a2, du, g_b)
    red_b.cores()
    red_a.scatter()
    red_b.scatter()
    finish(copies)
    norm_two_grad(p_da2, l_da2, x1, as_row(gain_two), dx2, dx1, dy, vec, t)
    copies = group_share(links, dy, pair_of())
    red_a.scatter_second()
    red_b.scatter_second()
    red_a.gather()
    red_b.gather()
    finish(copies)
    attention_grad(dy, w_out, w_qkv, qkv, probs, dqkv, p_da1)
    copies = group_scatter(links, p_da1, l_da1, pair_of())
    out_qkv_grad(att, dy, dqkv, a1, g_c)
    red_c.cores()
    red_a.gather_second()
    red_b.gather_second()
    red_c.scatter()
    finish(copies)
    norm_one_grad(p_da1, l_da1, x, as_row(gain_one), dx1, o_input, vec, t)
    vec_copies = group_share(links, vec, pair_of())
    red_a.share()
    red_b.share()
    proj_all[core, t] = f_a[core, 3, :3]
    proj_copies = group_share(links, proj_all.at[core], pair_of())
    finish(vec_copies)
    vec_all[dp] = vec[0] + vec[1] + vec[2] + vec[3]
    vec_copies = rank_share(links, vec_all, pair_of())
    red_c.gather()
    finish(proj_copies)
    proj_copies = sibling_send(links, proj_all.at[core], proj_all.at[core], pair_of())
    red_a.done()
    red_b.done()
    finish(vec_copies)
    total = vec_all[0]
    for i in range(1, RANKS):
        total = total + vec_all[i]
    o_norms[...] = total[:, :1536]
    o_loss[...] = total[:, 1536:] * (1.0 / 4096.0)
    finish(proj_copies)
    red_c.share()
    red_c.done()


def widen(
    loss, norms, grad, full_a, full_b, full_c, full_proj,
    o_loss, o_input, o_one, o_two, o_down, o_up, o_out, o_qkv, o_proj,
    down, up, out, qkv, proj, stored,
):
    stores = []

    def write(buf, target):
        stores.append(pltpu.make_async_copy(buf, target, stored.at[len(stores)]))
        stores[-1].start()

    def halves(target, parts, rows):
        for j in range(2):
            target[:, j * HALF : (j + 1) * HALF] = parts[j].reshape(rows, HALF).astype(F32)

    write(grad, o_input)
    halves(down, full_a[:, :3], HID)
    write(down, o_down)
    halves(up, full_b, D)
    write(up, o_up)
    halves(proj, full_proj, D)
    write(proj, o_proj)
    halves(out, full_c[:, :4], BAND)
    write(out, o_out)
    halves(qkv, full_c[:, 4:], 3 * BAND)
    write(qkv, o_qkv)
    o_loss[0, 0] = loss[0, 0]
    o_one[...] = norms[:, :D].reshape(D)
    o_two[...] = norms[:, D:].reshape(D)
    for copy in stores:
        copy.wait()


def on_device(
    text_input, segment_ids, pad_mask, pairing, ln_first, w_qkv, w_out, ln_second, w_up, w_down, text_proj,
    image_tokens, img_ln_first, img_w_qkv, img_w_out, img_ln_second, img_w_up, img_w_down, img_proj,
):
    vmem = pl.BlockSpec(memory_space=VM)
    hbm = pl.BlockSpec(memory_space=pl.ANY)
    shape = jax.ShapeDtypeStruct
    sums = ((4, 4, 64, HALF), (4, 4, 48, HALF), (16, 48, HALF))
    dma = pltpu.SemaphoreType.DMA
    scratch = [
        VM((IROWS, D), BF16), VM((3, D, D), BF16), VM((D, D), BF16), VM((D, FF), BF16), VM((FF, D), BF16), VM((D, D), BF16),
        VM((3, BAND, D), BF16), VM((BAND, D), BF16), VM((D, HID), BF16), VM((HID, D), BF16), VM((D, D), BF16), dma((11,)),
        VM((2 * PAIR, PAIR), F32), VM((PROWS, D), BF16), VM((3, PROWS, D), BF16), VM((6, PROWS, 128), F32), VM((IROWS, D), F32),
        VM((IMGS, D), F32), VM((IMGS, FF), F32), VM((2, CHIPS, IMGS, D), BF16),
        VM((4, 128, 128), F32), VM((CAPS, ROWS), BF16), VM((ROWS, 128), BF16), VM((GROUP, OWN_CAPS, 128), I32),
        VM((GROUP, OWN, D), BF16), VM((3, ROWS, BAND), BF16), VM((4, HALF, 128), F32), VM((ROWS, BAND), BF16),
        VM((GROUP, OWN, D), BF16), VM((3, OWN, D), BF16), VM((OWN, D), F32), VM((OWN_CAPS, D), F32), VM((GROUP, OWN, D), BF16),
        VM((ROWS, HID), F32), VM((CAPS, HID), F32), VM((GROUP, OWN_CAPS, D), F32), VM((GROUP, CAPS, D), BF16),
        VM((CAPS, D), F32), VM((CAPS, 128), F32), VM((CAPS, D), BF16), VM((CAPS, ROWS), F32),
        VM((CAPS, ROWS), F32), VM((GROUP, CAPS, 128), F32), VM((RANKS, 1, ROWS), F32), VM((GROUP, CAPS, D), BF16),
        VM((CAPS, D), BF16), VM((CAPS, D), BF16), VM((CAPS, D), F32),
        VM((OWN, D), F32), VM((ROWS, HID), BF16), VM((GROUP, OWN, D), BF16), VM((3, OWN, D), BF16), VM((OWN, D), F32),
        VM((GROUP, OWN, D), BF16), VM((3, ROWS, BAND), BF16), VM((GROUP, OWN, D), BF16), VM((3, OWN, D), BF16),
        VM((GROUP, BAND, D), BF16), VM((GROUP, 1, VEC), F32), VM((RANKS, 1, VEC), F32),
    ]
    scratch += [VM((2,) + s, BF16) for s in sums] + [VM(s, BF16) for s in sums]
    scratch += [VM((3,) + sums[0][1:], BF16), VM((3,) + sums[1][1:], BF16), VM((15,) + sums[2][1:], BF16)]
    scratch += [VM((3,) + s[2:], BF16) for s in sums[:2]]
    scratch += [dma((PAIRS, 2))]
    loss, input_grad, norms, full_a, full_b, full_c, full_proj = pl.pallas_call(
        body,
        out_shape=(
            VM((1, 128), F32), VM((OWN, D), F32), VM((1, 1536), F32),
            *(VM((2,) + s, BF16) for s in sums), VM((2, GROUP, 3, 64, HALF), BF16),
        ),
        in_specs=[vmem] * 3 + [pl.BlockSpec(memory_space=pltpu.SMEM)] + [vmem] * 4 + [hbm] * 11,
        out_specs=(vmem,) * 7,
        scratch_shapes=scratch,
        compiler_params=pltpu.CompilerParams(collective_id=0, has_side_effects=True, vmem_limit_bytes=57 << 20),
        name="lit",
    )(
        text_input, segment_ids.T, pad_mask.T, pairing, ln_first, ln_second, img_ln_first, img_ln_second,
        image_tokens.transpose(1, 0, 2).reshape(IROWS, D), img_w_qkv, img_w_out, img_w_up, img_w_down, img_proj,
        w_qkv.swapaxes(1, 2), w_out, w_up, w_down, text_proj,
    )

    loss, input_grad, one, two, down, up, out, qkv, proj = pl.pallas_call(
        widen,
        out_shape=(
            shape((1, 1), F32), shape((OWN, D), F32), shape((D,), F32), shape((D,), F32), shape((HID, D), F32),
            shape((D, HID), F32), shape((BAND, D), F32), shape((3 * BAND, D), F32), shape((D, D), F32),
        ),
        in_specs=[vmem] * 7,
        out_specs=(pl.BlockSpec(memory_space=pltpu.SMEM), hbm, vmem, vmem, hbm, hbm, hbm, hbm, hbm),
        scratch_shapes=[
            VM((HID, D), F32), VM((D, HID), F32), VM((BAND, D), F32), VM((3 * BAND, D), F32), VM((D, D), F32),
            dma((6,)),
        ],
        compiler_params=pltpu.CompilerParams(vmem_limit_bytes=40 << 20),
        name="widen",
    )(loss, norms, input_grad, full_a, full_b, full_c, full_proj)
    return (loss.reshape(()), input_grad, one, qkv.reshape(3, BAND, D).swapaxes(1, 2), out, two, up, down, proj)


def solution(mesh):
    rows = P(("dp", "tensor"))
    in_specs = (
        P(("dp", "tensor"), None), P("dp", None), P("dp", None), rows, P(), P(None, None, "tensor"), P("tensor", None), P(),
        P(None, "tensor"), P("tensor", None), P(), P(("dp", "tensor"), None, None), P(), P(), P(), P(), P(), P(), P(),
    )
    out_specs = (
        P(), P(("dp", "tensor"), None), P(), P(None, None, "tensor"), P("tensor", None), P(), P(None, "tensor"),
        P("tensor", None), P(),
    )
    return jax.shard_map(on_device, mesh=mesh, in_specs=in_specs, out_specs=out_specs, check_vma=False)
```

```python
import jax, jax.numpy as jnp
from jax import lax
from jax.experimental import pallas as pl
from jax.experimental.pallas import tpu as pltpu
from jax.sharding import PartitionSpec as P

F32, BF16, I32 = jnp.float32, jnp.bfloat16, jnp.int32
VM = pltpu.VMEM
EPS = 1e-6
NEG = -1e30
D, FF, HID = 768, 3072, 768
IMGS, POS = 16, 50
IROWS = IMGS * POS
HALFP = 56
PAIR = 2 * HALFP
PROWS = PAIR * (IMGS // 2)
TILE = 256
UP_TILE = 768


def dot(a, b):
    return jnp.dot(a, b, preferred_element_type=F32)


def dot_t(a, b):
    return lax.dot_general(a, b, (((1,), (1,)), ((), ())), preferred_element_type=F32)


def t_dot(a, b):
    return lax.dot_general(a, b, (((0,), (0,)), ((), ())), preferred_element_type=F32)


def iota(shape, axis):
    return lax.broadcasted_iota(I32, shape, axis)


def normalized(values):
    centred = values - jnp.mean(values, axis=-1, keepdims=True)
    spread = jnp.mean(centred * centred, axis=-1, keepdims=True)
    scale = lax.rsqrt(spread + EPS)
    return centred * scale, scale


def normal_cdf(u):
    return 0.5 + 0.5 * lax.erf(u * 0.7071067811865476)


def image_bias(bias):
    q, k = iota((2 * PAIR, PAIR), 0), iota((2 * PAIR, PAIR), 1)
    q = jnp.where(q >= PAIR, q - PAIR, q)
    place = jnp.where(k >= HALFP, k - HALFP, k)
    bias[...] = jnp.where(((q >= HALFP) == (k >= HALFP)) & (place < POS), 0.0, NEG)


def image_norm_one(tok, gain, stage):
    def rows(i, c):
        s = pl.ds(pl.multiple_of(i * 160, 160), 160)
        n, _ = normalized(tok[s, :].astype(F32))
        n = n * gain
        for h in range(6):
            stage[h, s, :] = n[:, h * 128 : h * 128 + 128]
        return c

    lax.fori_loop(0, 5, rows, 0)
    stage[:, IROWS:, :] = jnp.zeros((6, PROWS - IROWS, 128), F32)


def tiles(n, body):
    def step(i, c):
        body(i, pl.ds(pl.multiple_of(i * TILE, TILE), TILE))
        return c

    lax.fori_loop(0, n, step, 0)


def image_permute(stage, iap):
    def pair(p, c):
        for h in range(6):
            both = [stage[h, pl.ds(2 * p + i, HALFP, stride=IMGS), :] for i in range(2)]
            iap[pl.ds(pl.multiple_of(p * PAIR, PAIR), PAIR), h * 128 : h * 128 + 128] = jnp.concatenate(both, axis=0).astype(BF16)
        return c
    lax.fori_loop(0, IMGS // 2, pair, 0)


def image_qkv(iap, w, iqkv):
    def step(j, c):
        iqkv[j] = dot(iap[...], w[j]).astype(BF16)
        return c
    lax.fori_loop(0, 3, step, 0)


def stacked(values, low):
    zero = jnp.zeros_like(values)
    return jnp.concatenate([jnp.where(low, values, zero), jnp.where(low, zero, values)], axis=0)


def image_attention(iqkv, bias, stage, first, last, unroll=1):
    low = iota((PAIR, 128), 1) < 64

    def pair(p, c):
        rows = pl.ds(pl.multiple_of(p * PAIR, PAIR), PAIR)
        ones = jnp.ones((PAIR, 128), BF16)
        cols = [pl.ds(h * 128, 128) for h in range(6)]
        s = [dot_t(stacked(iqkv[0, rows, h], low), iqkv[1, rows, h]) * 0.125 + bias[...] for h in cols]
        e = [jnp.exp(x - jnp.max(x, axis=-1, keepdims=True)).astype(BF16) for x in s]
        for i, (h, x) in enumerate(zip(cols, e)):
            o = dot(x, jnp.concatenate([iqkv[2, rows, h], ones], axis=1))
            o = jnp.where(low, o[:PAIR, :128], o[PAIR:, :128]) / jnp.where(low, o[:PAIR, 128:], o[PAIR:, 128:])
            stage[i, pl.ds(2 * p, HALFP, stride=IMGS), :] = o[:HALFP]
            stage[i, pl.ds(2 * p + 1, HALFP, stride=IMGS), :] = o[HALFP:]
        return c

    lax.fori_loop(first, last, pair, 0, unroll=unroll)


def image_out(stage, tok, w, iy):
    def rows(i, c):
        s = pl.ds(pl.multiple_of(i * 160, 160), 160)
        iy[s, :] = tok[s, :].astype(F32) + dot(jnp.concatenate([stage[h, s, :].astype(BF16) for h in range(6)], axis=1), w[...])
        return c
    lax.fori_loop(0, 5, rows, 0)


def image_norm_two(iy, gain, ia, ypool):
    ypool[...] = jnp.zeros_like(ypool)
    def rows(i, c):
        s = pl.ds(pl.multiple_of(i * 160, 160), 160)
        y = iy[s, :]
        ypool[...] += jnp.sum(y.reshape(10, IMGS, D), axis=0)
        n, _ = normalized(y)
        ia[s, :] = (n * gain).astype(BF16)
        return c
    lax.fori_loop(0, 5, rows, 0)


def image_up(ia, w, hsum, first, last):
    def step(i, c):
        s = pl.ds(pl.multiple_of(i * UP_TILE, UP_TILE), UP_TILE)
        for m in range(5):
            u = dot(ia[160 * m : 160 * m + 160, :], w[:, s])
            part = jnp.sum((u * normal_cdf(u)).reshape(10, IMGS, UP_TILE), axis=0)
            total = part if m == 0 else total + part
        hsum[:, s] = total
        return c
    lax.fori_loop(first, last, step, 0)


def as_row(gain):
    return gain[...].reshape(1, D)


def column(values):
    rows = iota((OWN_CAPS, 128), 0)
    out = jnp.zeros((OWN_CAPS, 128), I32)
    for i in range(OWN_CAPS):
        out = jnp.where(rows == i, values[i], out)
    return out


def split_rows(x):
    hi = x.astype(BF16)
    return jnp.concatenate([hi, (x - hi.astype(F32)).astype(BF16)], axis=0)


def image_finish(hsum, ypool, w_down, w_proj):
    both = dot(split_rows(hsum[...]), w_down[...])
    pooled = ((ypool[...] + both[:IMGS] + both[IMGS:]) * (1.0 / POS)).astype(BF16)
    e = dot(pooled, w_proj[...])
    return (e * lax.rsqrt(jnp.sum(e * e, axis=-1, keepdims=True) + EPS)).astype(BF16)


GROUP, RANKS, CHIPS = 4, 32, 16
OWN, ROWS = 128, 512
CAPS, OWN_CAPS = 64, 16
PART = OWN // 2
BAND = 192
HALF = 384
MESH = pl.DeviceIdType.MESH
VEC = 1664
PAIRS = 53


class Links:
    def __init__(self):
        self.dp, self.t = lax.axis_index("dp"), lax.axis_index("tensor")
        self.core, self.chip = lax.rem(self.dp, 2), self.dp // 2
        self.place = {"x": lax.rem(self.chip, 4), "z": self.chip // 4}

    def rank(self, k):
        return lax.rem(self.t + k, GROUP)

    def group_peer(self, k):
        return {"dp": self.dp, "tensor": self.rank(k)}

    def rank_peer(self, k):
        return {"dp": lax.rem(self.dp + k, RANKS), "tensor": self.t}

    def chip_of(self, k):
        return lax.rem(self.chip + k, CHIPS)

    def chip_peer(self, k):
        return {"dp": 2 * self.chip_of(k) + self.core, "tensor": self.t}

    def axis_rank(self, axis, k):
        return lax.rem(self.place[axis] + k, 4)

    def axis_peer(self, axis, k):
        place = dict(self.place)
        place[axis] = self.axis_rank(axis, k)
        return {"dp": 2 * (place["z"] * 4 + place["x"]) + self.core, "tensor": self.t}

    def sibling(self):
        return {"dp": self.dp + 1 - 2 * self.core, "tensor": self.t}

    def greet(self):
        barrier = pltpu.get_barrier_semaphore()
        for k in range(1, GROUP):
            pl.semaphore_signal(barrier, 1, device_id=self.group_peer(k), device_id_type=MESH)
        for k in range(1, RANKS):
            pl.semaphore_signal(barrier, 1, device_id=self.rank_peer(k), device_id_type=MESH)

    def met(self):
        pl.semaphore_wait(pltpu.get_barrier_semaphore(), GROUP - 1 + RANKS - 1)


def send(src, dst, sems, peer):
    pltpu.make_async_remote_copy(src, dst, sems.at[0], sems.at[1], device_id=peer, device_id_type=MESH).start()


def finish(exchange):
    sems, span = exchange
    for i in range(2):
        pltpu.make_async_copy(span, span, sems.at[i]).wait()


def sent(exchange):
    sems, span = exchange
    pltpu.make_async_copy(span, span, sems.at[0]).wait()


def arrived(exchange):
    sems, span = exchange
    pltpu.make_async_copy(span, span, sems.at[1]).wait()


def group_share(links, buf, sems):
    own = buf.at[links.t]
    for k in (1, 3, 2):
        send(own, own, sems, links.group_peer(k))
    return sems, buf.at[pl.ds(0, 3)]


def group_scatter(links, parts, landed, sems):
    for k in (1, 3, 2):
        send(parts.at[links.rank(k)], landed.at[k - 1], sems, links.group_peer(k))
    return sems, landed


def half_rows(h):
    return pl.ds(h * PART, PART)


def share_half(links, buf, sems, h):
    own = buf.at[links.t, half_rows(h)]
    for k in (1, 3, 2):
        send(own, own, sems, links.group_peer(k))
    return sems, buf.at[pl.ds(0, 3), half_rows(h)]


def scatter_half(links, parts, landed, sems, h):
    for k in (1, 3, 2):
        send(parts.at[links.rank(k), half_rows(h)], landed.at[k - 1, half_rows(h)], sems, links.group_peer(k))
    return sems, landed.at[pl.ds(0, 3), half_rows(h)]


def rank_share(links, buf, sems):
    own = buf.at[links.dp]
    for k in range(1, RANKS):
        send(own, own, sems, links.rank_peer(k))
    return sems, buf.at[pl.ds(0, RANKS - 1)]


def chip_share(links, buf, sems):
    own = buf.at[links.chip]
    for k in range(1, CHIPS):
        send(own, own, sems, links.chip_peer(k))
    return sems, buf.at[pl.ds(0, CHIPS - 1)]


def sibling_send(links, src, dst, sems):
    send(src, dst, sems, links.sibling())
    return sems, src


def text_masks(seg_t, pad_t, bias, mem, mem_t):
    seg, pad = seg_t[...].astype(F32).astype(BF16), pad_t[...].astype(F32).astype(BF16)

    def as_column(values):
        pick = jnp.where(iota((ROWS, 32), 0) >> 4 == iota((ROWS, 32), 1), 1.0, 0.0).astype(BF16)
        wide = dot_t(pick, values)
        return jnp.sum(jnp.where(iota((ROWS, 16), 0) & 15 == iota((ROWS, 16), 1), wide, 0.0), axis=1, keepdims=True)

    def as_row(values):
        pick = jnp.where(iota((32, ROWS), 1) >> 4 == iota((32, ROWS), 0), 1.0, 0.0).astype(BF16)
        wide = dot(values, pick)
        return jnp.sum(jnp.where(iota((16, ROWS), 1) & 15 == iota((16, ROWS), 0), wide, 0.0), axis=0, keepdims=True)

    cap_col = as_column(seg) + ((iota((ROWS, 1), 0) >> 4) * 2).astype(F32)
    key_col = jnp.where(as_column(pad) > 0.5, cap_col, -1.0)
    cap_row = as_row(seg) + ((iota((1, ROWS), 1) >> 4) * 2).astype(F32)
    key_row = jnp.where(as_row(pad) > 0.5, cap_row, -1.0)
    for b in range(4):
        rows = slice(128 * b, 128 * b + 128)
        bias[b] = jnp.where(cap_col[rows] == key_row[:, rows], 0.0, NEG)
    mem[...] = jnp.where(iota((CAPS, ROWS), 0).astype(F32) == key_row, 1.0, 0.0).astype(BF16)
    mem_t[...] = jnp.where((iota((ROWS, 128), 1) & 63).astype(F32) == key_col, 1.0, 0.0).astype(BF16)


def text_norm_one(x, gain, a1, t):
    n, _ = normalized(x[...].astype(F32))
    a1[t] = (n * gain).astype(BF16)


def low_half():
    return iota((OWN, 128), 1) < 64


def text_attention(a1, w_t, bias, w_out, qkv, probs, att, parts):
    rows_all = a1[...].reshape(ROWS, D)
    for j in range(3):
        qkv[j] = dot_t(rows_all, w_t[j]).astype(BF16)
    low = low_half()
    blocks = [slice(128 * b, 128 * b + 128) for b in range(4)]
    scores = []
    for b, rows in enumerate(blocks):
        mask = bias[b]
        scores.append(dot_t(stacked(qkv[0, rows, :128], low), qkv[1, rows, :128]) * 0.125 + jnp.concatenate([mask, mask], axis=0))
        scores.append(dot_t(qkv[0, rows, 128:], qkv[1, rows, 128:]) * 0.125 + mask)
    powers = [jnp.exp(x - jnp.max(x, axis=-1, keepdims=True)) for x in scores]
    shares = [x / jnp.sum(x, axis=-1, keepdims=True) for x in powers]
    for b, rows in enumerate(blocks):
        probs[b, :256] = shares[2 * b]
        probs[b, 256:] = shares[2 * b + 1]
        o = dot(shares[2 * b].astype(BF16), qkv[2, rows, :128])
        att[rows, :128] = jnp.where(low, o[:128], o[128:]).astype(BF16)
        att[rows, 128:] = dot(shares[2 * b + 1].astype(BF16), qkv[2, rows, 128:]).astype(BF16)
    parts[...] = dot(att[...], w_out[...]).astype(BF16).reshape(GROUP, OWN, D)


def summed(parts, landed, t, rows):
    return parts[t, rows].astype(F32) + landed[0, rows].astype(F32) + landed[1, rows].astype(F32) + landed[2, rows].astype(F32)


def split3(x):
    hi = x.astype(BF16)
    rest = x - hi.astype(F32)
    mid = rest.astype(BF16)
    return jnp.concatenate([hi, mid, (rest - mid.astype(F32)).astype(BF16)], axis=0)


def own_member(mem, t):
    return mem[pl.ds(pl.multiple_of(t * OWN_CAPS, OWN_CAPS), OWN_CAPS), pl.ds(pl.multiple_of(t * OWN, OWN), OWN)]


def text_norm_two(h, x, parts, landed, gain, x1, a2, t):
    rows = half_rows(h)
    y = x[rows, :].astype(F32) + summed(parts, landed, t, rows)
    x1[rows, :] = y
    n, _ = normalized(y)
    a2[t, rows] = (n * gain).astype(BF16)


def text_pool_one(x1, mem, x1_pool, t):
    own = own_member(mem, t)
    x1_pool[...] = dot(jnp.concatenate([own, own, own], axis=1), split3(x1[...]))


def text_up(a2, w_up, mem, w_down, x1_pool, dgelu, hidden, hsum, part, parts, t):
    for r in range(GROUP):
        rows = slice(r * OWN, r * OWN + OWN)
        u = dot(a2[r], w_up[...])
        phi = normal_cdf(u)
        dgelu[rows, :] = phi + u * (jnp.exp(u * u * -0.5) * 0.3989422804014327)
        hidden[rows, :] = (u * phi).astype(BF16)
    hsum[...] = dot(mem[...], hidden[...])
    both = dot(split_rows(hsum[...]), w_down[...])
    part[...] = (both[:CAPS] + both[CAPS:]).reshape(GROUP, OWN_CAPS, D)
    part[t] += x1_pool[...]
    parts[t] = part[...].reshape(CAPS, D).astype(BF16)


def counts_of(mem):
    return jnp.sum(mem.astype(F32), axis=1, keepdims=True)


def text_embed(parts, mem, w_proj, pooled, tf, scale):
    total = parts[0].astype(F32) + parts[1].astype(F32) + parts[2].astype(F32) + parts[3].astype(F32)
    rows = (total / counts_of(mem[...])).astype(BF16)
    pooled[...] = rows
    e = dot(rows, w_proj[...])
    rs = lax.rsqrt(jnp.sum(e * e, axis=-1, keepdims=True) + EPS)
    tf[...] = rs * e
    scale[...] = jnp.broadcast_to(rs, (CAPS, 128))


def score_sums(tf, images, s_ref, e_ref, row_sums, col_sums, t, dp):
    s = 40.0 * dot_t(tf[...].astype(BF16), images[...].reshape(ROWS, D))
    s_ref[...] = s
    e = jnp.exp(s - 40.0)
    e_ref[...] = e
    diagonal = iota((CAPS, 128), 0) == iota((CAPS, 128), 1)
    row_sums[t] = jnp.sum(jnp.where(diagonal, jnp.sum(e, axis=1, keepdims=True), 0.0), axis=0, keepdims=True)
    col_sums[dp] = jnp.sum(e, axis=0, keepdims=True)


def score_grad(s_ref, e_ref, row_sums, col_sums, pair, images, dts, vec, t):
    diagonal = iota((CAPS, 128), 0) == iota((CAPS, 128), 1)
    rows = jnp.sum(jnp.where(diagonal, row_sums[0] + row_sums[1] + row_sums[2] + row_sums[3], 0.0), axis=1, keepdims=True)
    cols = col_sums[0]
    for i in range(1, RANKS):
        cols = cols + col_sums[i]
    lane = iota((CAPS, ROWS), 1)
    image = ((lane >> 4) & 15) * (2 * CAPS) + (lane >> 8) * CAPS + (lane & 15) + OWN_CAPS * t
    target = jnp.where(pair[...].reshape(CAPS, 128)[:, :1] == image, 1.0, 0.0)
    g = 0.5 * (e_ref[...] / rows + e_ref[...] / cols) - target
    dts[t] = (40.0 * dot(g.astype(BF16), images[...].reshape(ROWS, D))).astype(BF16)
    loss = (
        jnp.sum(40.0 + jnp.log(rows), axis=0, keepdims=True) * (1.0 / GROUP)
        + jnp.sum(40.0 + jnp.log(cols), axis=1, keepdims=True) * (1.0 / RANKS)
        - 2.0 * jnp.sum(jnp.sum(s_ref[...] * target, axis=1, keepdims=True), axis=0, keepdims=True)
    )
    vec[t, :, 1536:] = jnp.broadcast_to(loss, (1, 128))


def embed_grad(dts, tf, scale, w_proj, mem, de_ref, dz_ref, gp_ref):
    dt = dts[0].astype(F32) + dts[1].astype(F32) + dts[2].astype(F32) + dts[3].astype(F32)
    f = tf[...]
    de = (scale[:, :1] * (dt - f * jnp.sum(f * dt, axis=-1, keepdims=True))).astype(BF16)
    gp = dot_t(de, w_proj[...]) / counts_of(mem[...])
    de_ref[...] = de
    gp_ref[...] = gp
    dz_ref[...] = gp.astype(BF16)


def row_grad(gp_ref, mem, dx2, t):
    own = own_member(mem, t)
    gp = gp_ref[pl.ds(pl.multiple_of(t * OWN_CAPS, OWN_CAPS), OWN_CAPS), :]
    dx2[...] = t_dot(jnp.concatenate([own, own, own], axis=0), split3(gp))


def hidden_grad(dz, w_down):
    return split_rows(dot_t(dz[...], w_down[...]))


def hidden_spread(h, dh, mem_t, dgelu, w_up, du, parts):
    blocks = [pl.ds(r * OWN + h * PART, PART) for r in range(GROUP)]
    member = jnp.concatenate([mem_t[b, :] for b in blocks], axis=0)
    slope = jnp.concatenate([dgelu[b, :] for b in blocks], axis=0)
    rows = (dot(member, dh) * slope).astype(BF16)
    total = dot_t(rows, w_up[...]).astype(BF16)
    for r, b in enumerate(blocks):
        du[b, :] = rows[r * PART : (r + 1) * PART]
        parts[r, half_rows(h)] = total[r * PART : (r + 1) * PART]


def gain_grad(parts, normed, gain):
    total = jnp.zeros((1, D), F32)
    for r in range(GROUP):
        total = total + jnp.sum(parts[r].astype(F32) * normed[r].astype(F32), axis=0, keepdims=True)
    return total / gain


def put_chunks(g, first, values):
    rows = g.shape[-2]
    for c in range(values.shape[0] // rows):
        at = first + c
        place = (at,) if len(g.shape) == 4 else (at // 4, at % 4)
        for j in range(2):
            g[(j, *place)] = values[c * rows : (c + 1) * rows, j * HALF : (j + 1) * HALF].astype(BF16)


def down_proj_grad(hsum, dz, de, pooled, proj, g, h, t):
    hs = split_rows(hsum[...])
    dz2 = jnp.concatenate([dz[...], dz[...]], axis=0)
    put_chunks(g, 0, t_dot(hs[:, :256], dz2))
    put_chunks(g, 8, t_dot(hs[:, 256:512], dz2))
    put_chunks(h, 0, t_dot(hs[:, 512:], dz2))
    proj[...] = t_dot(pooled[...], de[...]).astype(BF16).reshape(GROUP, BAND, D)
    put_chunks(h, 8, proj[t])
    h[:, 3, 2:] = jnp.zeros((2, 2, 32, HALF), BF16)


def up_grad(a2, du, g, h):
    for i in range(3):
        rows = t_dot(a2[:, :, i * 256 : (i + 1) * 256].reshape(ROWS, 256), du[...])
        put_chunks(g if i < 2 else h, 8 * i if i < 2 else 0, rows)


def norm_two_grad(h, parts, landed, x1, gain, dx2, dx1, dy, t):
    rows = half_rows(h)
    da = summed(parts, landed, t, rows)
    n, scale = normalized(x1[rows, :])
    d = da * gain
    g = dx2[rows, :] + (d - jnp.mean(d, axis=-1, keepdims=True) - n * jnp.mean(d * n, axis=-1, keepdims=True)) * scale
    dx1[rows, :] = g
    dy[t, rows] = g.astype(BF16)


def attention_grad(dy, w_out, w_t, qkv, probs, dqkv, parts):
    datt = dot_t(dy[...].reshape(ROWS, D), w_out[...]).astype(BF16)
    low = low_half()
    blocks = [slice(128 * b, 128 * b + 128) for b in range(4)]
    sides, raw = [], []
    for b, rows in enumerate(blocks):
        sides.append((stacked(qkv[0, rows, :128], low), stacked(datt[rows, :128], low)))
        sides.append((qkv[0, rows, 128:], datt[rows, 128:]))
        raw.append(dot_t(sides[-2][1], qkv[2, rows, :128]))
        raw.append(dot_t(sides[-1][1], qkv[2, rows, 128:]))
    probs_of = [probs[b, part] for b in range(4) for part in (slice(0, 256), slice(256, 384))]
    ds = [(p * (x - jnp.sum(p * x, axis=-1, keepdims=True))).astype(BF16) for p, x in zip(probs_of, raw)]
    for b, rows in enumerate(blocks):
        for i, cols in ((2 * b, slice(0, 128)), (2 * b + 1, slice(128, BAND))):
            o = dot(ds[i], qkv[1, rows, cols])
            if i % 2 == 0:
                o = jnp.where(low, o[:128], o[128:])
            dqkv[0, rows, cols] = (o * 0.125).astype(BF16)
            dqkv[1, rows, cols] = (t_dot(ds[i], sides[i][0]) * 0.125).astype(BF16)
            dqkv[2, rows, cols] = t_dot(probs_of[i].astype(BF16), sides[i][1]).astype(BF16)
    total = dot(dqkv[0], w_t[0]) + dot(dqkv[1], w_t[1]) + dot(dqkv[2], w_t[2])
    parts[...] = total.astype(BF16).reshape(GROUP, OWN, D)


def out_grad(att, dy, g):
    put_chunks(g, 0, t_dot(att[...], dy[...].reshape(ROWS, D)))


def qkv_grad(dqkv, a1, g, h):
    rows = a1[...].reshape(ROWS, D)
    put_chunks(g, 6, t_dot(dqkv[0], rows))
    keys = t_dot(dqkv[1], rows)
    put_chunks(g, 12, keys[:128])
    put_chunks(h, 0, keys[128:])
    put_chunks(h, 4, t_dot(dqkv[2], rows))


def norm_one_grad(parts, landed, x, gain, dx1, out, t):
    da = summed(parts, landed, t, slice(0, OWN))
    n, scale = normalized(x[...].astype(F32))
    h = da * gain
    out[...] = dx1[...] + (h - jnp.mean(h, axis=-1, keepdims=True) - n * jnp.mean(h * n, axis=-1, keepdims=True)) * scale


class Reduction:
    def __init__(self, links, g, met, landed, full, pair):
        self.links, self.g, self.met, self.landed, self.full, self.pair = links, g, met, landed, full, pair

    def cores(self):
        self.open = sibling_send(self.links, self.g.at[1 - self.links.core], self.met, self.pair())

    def both_cores(self):
        finish(self.open)
        self.met[...] = (self.g[self.links.core].astype(F32) + self.met[...].astype(F32)).astype(BF16)

    def scatter(self):
        self.both_cores()
        sems = self.pair()
        for k in range(1, CHIPS):
            send(self.met.at[self.links.chip_of(k)], self.landed.at[k - 1], sems, self.links.chip_peer(k))
        self.open = sems, self.landed

    def gather(self):
        finish(self.open)
        total = self.met[self.links.chip].astype(F32)
        for k in range(CHIPS - 1):
            total = total + self.landed[k].astype(F32)
        half = self.full.at[self.links.core]
        half[self.links.chip] = total.astype(BF16)
        self.open = chip_share(self.links, half, self.pair())

    def share(self):
        finish(self.open)
        half = self.full.at[self.links.core]
        self.open = sibling_send(self.links, half, half, self.pair())

    def done(self):
        finish(self.open)


class TwoAxes(Reduction):
    def __init__(self, links, g, met, landed, near, full, pair, first, second):
        super().__init__(links, g, met, landed, full, pair)
        self.near, self.first, self.second = near, first, second
        self.i, self.j = links.place[first], links.place[second]

    def spread(self, axis, source, target):
        sems = self.pair()
        for k in (1, 3, 2):
            send(source(k), target(k), sems, self.links.axis_peer(axis, k))
        return sems

    def scatter(self):
        self.both_cores()
        sems = self.spread(
            self.first, lambda k: self.met.at[self.links.axis_rank(self.first, k)], lambda k: self.landed.at[k - 1]
        )
        self.open = sems, self.landed

    def scatter_second(self):
        finish(self.open)
        total = self.met[self.i].astype(F32)
        for k in range(3):
            total = total + self.landed[k].astype(F32)
        self.met[self.i] = total.astype(BF16)
        sems = self.spread(
            self.second, lambda k: self.met.at[self.i, self.links.axis_rank(self.second, k)], lambda k: self.near.at[k - 1]
        )
        self.open = sems, self.near

    def gather(self):
        finish(self.open)
        total = self.met[self.i, self.j].astype(F32)
        for k in range(3):
            total = total + self.near[k].astype(F32)
        core = self.links.core
        self.full[core, self.i, self.j] = total.astype(BF16)
        own = self.full.at[core, self.i, self.j]
        self.open = self.spread(self.second, lambda k: own, lambda k: own), self.full.at[0, 0, pl.ds(0, 3)]

    def gather_second(self):
        finish(self.open)
        own = self.full.at[self.links.core, self.i]
        self.open = self.spread(self.first, lambda k: own, lambda k: own), self.full.at[0, pl.ds(0, 3)]


def body(
    x, seg_t, pad_t, pair_in, gain_one, gain_two, img_gain_one, img_gain_two,
    h_tok, h_iqkv, h_iout, h_iup, h_idown, h_iproj, h_qkv, h_out, h_up, h_down, h_proj,
    o_loss, o_input, o_norms, f_a0, f_a1, f_b0, f_b1, f_c0, f_c1, proj_all,
    tok, iw_qkv, iw_out, iw_up, iw_down, iw_proj, w_qkv, w_out, w_up, w_down, w_proj, load,
    ibias, iap, iqkv, stage, iy, ypool, ihsum, images,
    bias, mem, mem_t, pair, a1, qkv, probs, att, p_att, l_att, x1, x1_pool, a2, dgelu, hsum, p_pool, pools,
    tf, scale, pooled, s_ref, e_ref, row_sums, col_sums, dts, de, dz, gp, dx2, du, p_da2, l_da2, dx1, dy,
    dqkv, p_da1, l_da1, proj, vec, vec_all,
    *work,
):
    g_a, g_b, g_c, m_a, m_b, m_c, r_a, r_b, r_c, n_a, n_b = (work[i : i + 2] for i in range(0, 22, 2))
    f_a, f_b, f_c = (f_a0, f_a1), (f_b0, f_b1), (f_c0, f_c1)
    sems = work[22]
    links = Links()
    t, dp, core, chip = links.t, links.dp, links.core, links.chip
    loads = {}
    count = iter(range(PAIRS))

    def pair_of():
        return sems.at[next(count)]


    def fetch(at, name, src, dst):
        loads[name] = pltpu.make_async_copy(src, dst, load.at[at])
        loads[name].start()

    fetch(0, "tok", h_tok, tok)
    fetch(1, "iqkv", h_iqkv, iw_qkv)
    links.greet()
    text_norm_one(x, as_row(gain_one), a1, t)
    pair[t] = column(pair_in)
    links.met()
    copies = group_share(links, a1, pair_of())
    pair_copies = group_share(links, pair, pair_of())
    fetch(2, "qkv", h_qkv, w_qkv)
    fetch(3, "out", h_out, w_out)
    fetch(4, "iout", h_iout, iw_out)

    text_masks(seg_t, pad_t, bias, mem, mem_t)
    image_bias(ibias)
    loads["tok"].wait()
    image_norm_one(tok, as_row(img_gain_one), stage)
    fetch(5, "iup", h_iup, iw_up)
    fetch(6, "up", h_up, w_up)
    fetch(7, "down", h_down, w_down)
    fetch(8, "idown", h_idown, iw_down)
    fetch(9, "iproj", h_iproj, iw_proj)
    fetch(10, "proj", h_proj, w_proj)
    image_permute(stage, iap)
    loads["iqkv"].wait()
    image_qkv(iap, iw_qkv, iqkv)

    finish(copies)
    loads["qkv"].wait()
    loads["out"].wait()
    text_attention(a1, w_qkv, bias, w_out, qkv, probs, att, p_att)
    copies = [scatter_half(links, p_att, l_att, pair_of(), 0)]

    image_attention(iqkv, ibias, stage, 0, 4)
    copies.append(scatter_half(links, p_att, l_att, pair_of(), 1))
    image_attention(iqkv, ibias, stage, 4, 8)
    finish(copies[0])
    text_norm_two(0, x, p_att, l_att, as_row(gain_two), x1, a2, t)
    copies[0] = share_half(links, a2, pair_of(), 0)
    loads["iout"].wait()
    image_out(stage, tok, iw_out, iy)
    finish(copies[1])
    text_norm_two(1, x, p_att, l_att, as_row(gain_two), x1, a2, t)
    copies[1] = share_half(links, a2, pair_of(), 1)
    image_norm_two(iy, as_row(img_gain_two), iap.at[:IROWS], ypool)

    loads["iup"].wait()
    image_up(iap.at[:IROWS], iw_up, ihsum, 0, 1)
    text_pool_one(x1, mem, x1_pool, t)

    image_up(iap.at[:IROWS], iw_up, ihsum, 1, FF // UP_TILE)
    loads["idown"].wait()
    loads["iproj"].wait()
    images[core, chip] = image_finish(ihsum, ypool, iw_down, iw_proj)
    image_copies = chip_share(links, images.at[core], pair_of())

    finish(copies[0])
    finish(copies[1])
    loads["up"].wait()
    loads["down"].wait()
    text_up(a2, w_up, mem, w_down, x1_pool, dgelu, du, hsum, p_pool, pools, t)
    copies = group_share(links, pools, pair_of())
    finish(image_copies)
    image_copies = sibling_send(links, images.at[core], images.at[core], pair_of())
    finish(pair_copies)
    loads["proj"].wait()
    finish(copies)
    text_embed(pools, mem, w_proj, pooled, tf, scale)
    finish(image_copies)

    score_sums(tf, images, s_ref, e_ref, row_sums, col_sums, t, dp)
    row_copies = group_share(links, row_sums, pair_of())
    col_copies = rank_share(links, col_sums, pair_of())
    finish(col_copies)
    finish(row_copies)
    score_grad(s_ref, e_ref, row_sums, col_sums, pair, images, dts, vec, t)
    finish(group_share(links, dts, pair_of()))
    embed_grad(dts, tf, scale, w_proj, mem, de, dz, gp)

    red_a = [TwoAxes(links, g_a[i], m_a[i], r_a[i], n_a[i], f_a[i], pair_of, "x", "z") for i in range(2)]
    red_b = [TwoAxes(links, g_b[i], m_b[i], r_b[i], n_b[i], f_b[i], pair_of, "z", "x") for i in range(2)]
    red_c = [Reduction(links, g_c[i], m_c[i], r_c[i], f_c[i], pair_of) for i in range(2)]

    def each(*steps):
        for step in steps:
            step()

    dh = hidden_grad(dz, w_down)
    hidden_spread(0, dh, mem_t, dgelu, w_up, du, p_da2)
    copies = [scatter_half(links, p_da2, l_da2, pair_of(), 0)]
    hidden_spread(1, dh, mem_t, dgelu, w_up, du, p_da2)
    down_proj_grad(hsum, dz, de, pooled, proj, g_a[0], g_a[1], t)
    each(red_a[0].cores, red_a[1].cores)
    up_grad(a2, du, g_b[0], g_b[1])
    each(red_b[0].cores, red_b[1].cores)
    sent(copies[0])
    copies.append(scatter_half(links, p_da2, l_da2, pair_of(), 1))
    row_grad(gp, mem, dx2, t)
    vec[t, :, 768:1536] = gain_grad(p_da2, a2, as_row(gain_two))
    each(red_a[0].scatter, red_b[0].scatter, red_a[1].scatter, red_b[1].scatter)
    arrived(copies[0])
    norm_two_grad(0, p_da2, l_da2, x1, as_row(gain_two), dx2, dx1, dy, t)
    copies[0] = share_half(links, dy, pair_of(), 0)
    finish(copies[1])
    norm_two_grad(1, p_da2, l_da2, x1, as_row(gain_two), dx2, dx1, dy, t)
    copies[1] = share_half(links, dy, pair_of(), 1)
    each(red_a[0].scatter_second, red_b[0].scatter_second)
    each(red_a[1].scatter_second, red_b[1].scatter_second)
    each(red_a[0].gather, red_b[0].gather)
    each(red_a[1].gather, red_b[1].gather)
    each(red_a[0].gather_second, red_b[0].gather_second)
    finish(copies[0])
    finish(copies[1])
    each(red_a[1].gather_second, red_b[1].gather_second)
    out_grad(att, dy, g_c[0])
    attention_grad(dy, w_out, w_qkv, qkv, probs, dqkv, p_da1)
    vec[t, :, :768] = gain_grad(p_da1, a1, as_row(gain_one))
    vec_copies = group_share(links, vec, pair_of())
    copies = group_scatter(links, p_da1, l_da1, pair_of())
    qkv_grad(dqkv, a1, g_c[0], g_c[1])
    each(red_c[0].cores, red_c[1].cores, red_c[0].scatter, red_c[1].scatter)
    finish(vec_copies)
    vec_all[dp] = vec[0] + vec[1] + vec[2] + vec[3]
    vec_copies = rank_share(links, vec_all, pair_of())
    each(red_a[1].share, red_a[0].share, red_b[0].share, red_b[1].share)
    proj_all[core, t, :4] = f_a1[core, 2]
    proj_all[core, t, 4:] = f_a1[core, 3, :2]
    proj_copies = group_share(links, proj_all.at[core], pair_of())
    each(red_c[0].gather, red_c[1].gather)
    finish(copies)
    norm_one_grad(p_da1, l_da1, x, as_row(gain_one), dx1, o_input, t)
    finish(proj_copies)
    proj_copies = sibling_send(links, proj_all.at[core], proj_all.at[core], pair_of())
    each(red_a[0].done, red_a[1].done, red_b[0].done, red_b[1].done)
    finish(vec_copies)
    total = vec_all[0]
    for i in range(1, RANKS):
        total = total + vec_all[i]
    o_norms[...] = total[:, :1536]
    o_loss[...] = total[:, 1536:] * (1.0 / 4096.0)
    finish(proj_copies)
    each(red_c[0].share, red_c[1].share, red_c[0].done, red_c[1].done)


def widen(
    loss, norms, grad, a0, a1, b0, b1, c0, c1, full_proj,
    o_loss, o_input, o_one, o_two, o_down, o_up, o_out, o_qkv, o_proj, down, up, out, qkv, proj, stored,
):
    stores = []

    def write(buf, target):
        stores.append(pltpu.make_async_copy(buf, target, stored.at[len(stores)]))
        stores[-1].start()

    def halves(target, first, parts, rows):
        for j in range(2):
            target[first : first + rows, j * HALF : (j + 1) * HALF] = parts[j].reshape(rows, HALF).astype(F32)

    write(grad, o_input)
    halves(down, 0, a0, 512)
    halves(down, 512, a1[:, :2], 256)
    write(down, o_down)
    halves(up, 0, b0, 512)
    halves(up, 512, b1, 256)
    write(up, o_up)
    halves(proj, 0, full_proj, D)
    write(proj, o_proj)
    halves(out, 0, c0[:, :6], BAND)
    write(out, o_out)
    halves(qkv, 0, c0[:, 6:], 320)
    halves(qkv, 320, c1, 256)
    write(qkv, o_qkv)
    o_loss[0, 0] = loss[0, 0]
    o_one[...] = norms[:, :D].reshape(D)
    o_two[...] = norms[:, D:].reshape(D)
    for copy in stores:
        copy.wait()


def on_device(
    text_input, segment_ids, pad_mask, pairing, ln_first, w_qkv, w_out, ln_second, w_up, w_down, text_proj,
    image_tokens, img_ln_first, img_w_qkv, img_w_out, img_ln_second, img_w_up, img_w_down, img_proj,
):
    vmem = pl.BlockSpec(memory_space=VM)
    hbm = pl.BlockSpec(memory_space=pl.ANY)
    shape = jax.ShapeDtypeStruct
    sums = ((4, 4, 32, HALF),) * 2 + ((4, 4, 32, HALF), (4, 4, 16, HALF)) + ((16, 32, HALF), (16, 16, HALF))
    dma = pltpu.SemaphoreType.DMA
    scratch = [
        VM((IROWS, D), BF16), VM((3, D, D), BF16), VM((D, D), BF16), VM((D, FF), BF16), VM((FF, D), BF16), VM((D, D), BF16),
        VM((3, BAND, D), BF16), VM((BAND, D), BF16), VM((D, HID), BF16), VM((HID, D), BF16), VM((D, D), BF16), dma((11,)),
        VM((2 * PAIR, PAIR), F32), VM((PROWS, D), BF16), VM((3, PROWS, D), BF16), VM((6, PROWS, 128), F32), VM((IROWS, D), F32),
        VM((IMGS, D), F32), VM((IMGS, FF), F32), VM((2, CHIPS, IMGS, D), BF16),
        VM((4, 128, 128), F32), VM((CAPS, ROWS), BF16), VM((ROWS, 128), BF16), VM((GROUP, OWN_CAPS, 128), I32),
        VM((GROUP, OWN, D), BF16), VM((3, ROWS, BAND), BF16), VM((4, HALF, 128), F32), VM((ROWS, BAND), BF16),
        VM((GROUP, OWN, D), BF16), VM((3, OWN, D), BF16), VM((OWN, D), F32), VM((OWN_CAPS, D), F32), VM((GROUP, OWN, D), BF16),
        VM((ROWS, HID), F32), VM((CAPS, HID), F32), VM((GROUP, OWN_CAPS, D), F32), VM((GROUP, CAPS, D), BF16),
        VM((CAPS, D), F32), VM((CAPS, 128), F32), VM((CAPS, D), BF16), VM((CAPS, ROWS), F32),
        VM((CAPS, ROWS), F32), VM((GROUP, 1, 128), F32), VM((RANKS, 1, ROWS), F32), VM((GROUP, CAPS, D), BF16),
        VM((CAPS, D), BF16), VM((CAPS, D), BF16), VM((CAPS, D), F32),
        VM((OWN, D), F32), VM((ROWS, HID), BF16), VM((GROUP, OWN, D), BF16), VM((3, OWN, D), BF16), VM((OWN, D), F32),
        VM((GROUP, OWN, D), BF16), VM((3, ROWS, BAND), BF16), VM((GROUP, OWN, D), BF16), VM((3, OWN, D), BF16),
        VM((GROUP, BAND, D), BF16), VM((GROUP, 1, VEC), F32), VM((RANKS, 1, VEC), F32),
    ]
    scratch += [VM((2,) + s, BF16) for s in sums] + [VM(s, BF16) for s in sums]
    scratch += [VM((3,) + s[1:], BF16) for s in sums[:4]] + [VM((15,) + s[1:], BF16) for s in sums[4:]]
    scratch += [VM((3,) + s[2:], BF16) for s in sums[:4]] + [dma((PAIRS, 2))]
    loss, input_grad, norms, *full = pl.pallas_call(
        body,
        out_shape=(
            VM((1, 128), F32), VM((OWN, D), F32), VM((1, 1536), F32),
            *(VM((2,) + s, BF16) for s in sums), VM((2, GROUP, 6, 32, HALF), BF16),
        ),
        in_specs=[vmem] * 3 + [pl.BlockSpec(memory_space=pltpu.SMEM)] + [vmem] * 4 + [hbm] * 11,
        out_specs=(vmem,) * 10,
        scratch_shapes=scratch,
        compiler_params=pltpu.CompilerParams(collective_id=0, has_side_effects=True, vmem_limit_bytes=57 << 20),
        name="lit",
    )(
        text_input, segment_ids.T, pad_mask.T, pairing, ln_first, ln_second, img_ln_first, img_ln_second,
        image_tokens.transpose(1, 0, 2).reshape(IROWS, D), img_w_qkv, img_w_out, img_w_up, img_w_down, img_proj,
        w_qkv.swapaxes(1, 2), w_out, w_up, w_down, text_proj,
    )

    loss, input_grad, one, two, down, up, out, qkv, proj = pl.pallas_call(
        widen,
        out_shape=(
            shape((1, 1), F32), shape((OWN, D), F32), shape((D,), F32), shape((D,), F32), shape((HID, D), F32),
            shape((D, HID), F32), shape((BAND, D), F32), shape((3 * BAND, D), F32), shape((D, D), F32),
        ),
        in_specs=[vmem] * 10,
        out_specs=(pl.BlockSpec(memory_space=pltpu.SMEM), hbm, vmem, vmem, hbm, hbm, hbm, hbm, hbm),
        scratch_shapes=[
            VM((HID, D), F32), VM((D, HID), F32), VM((BAND, D), F32), VM((3 * BAND, D), F32), VM((D, D), F32),
            dma((6,)),
        ],
        compiler_params=pltpu.CompilerParams(vmem_limit_bytes=40 << 20),
        name="widen",
    )(loss, norms, input_grad, *full)
    return (loss.reshape(()), input_grad, one, qkv.reshape(3, BAND, D).swapaxes(1, 2), out, two, up, down, proj)


def solution(mesh):
    rows = P(("dp", "tensor"))
    in_specs = (
        P(("dp", "tensor"), None), P("dp", None), P("dp", None), rows, P(), P(None, None, "tensor"), P("tensor", None), P(),
        P(None, "tensor"), P("tensor", None), P(), P(("dp", "tensor"), None, None), P(), P(), P(), P(), P(), P(), P(),
    )
    out_specs = (
        P(), P(("dp", "tensor"), None), P(), P(None, None, "tensor"), P("tensor", None), P(), P(None, "tensor"),
        P("tensor", None), P(),
    )
    return jax.shard_map(on_device, mesh=mesh, in_specs=in_specs, out_specs=out_specs, check_vma=False)
```

```python
import jax, jax.numpy as jnp
from jax import lax
from jax.experimental import pallas as pl
from jax.experimental.pallas import tpu as pltpu
from jax.sharding import PartitionSpec as P

F32, BF16, I32 = jnp.float32, jnp.bfloat16, jnp.int32
VM = pltpu.VMEM
EPS = 1e-6
NEG = -1e30
D, FF, HID = 768, 3072, 768
IMGS, POS = 16, 50
IROWS = IMGS * POS
HALFP = 56
PAIR = 2 * HALFP
PROWS = PAIR * (IMGS // 2)
TILE = 256
UP_TILE = 768


def dot(a, b):
    return jnp.dot(a, b, preferred_element_type=F32)


def dot_t(a, b):
    return lax.dot_general(a, b, (((1,), (1,)), ((), ())), preferred_element_type=F32)


def t_dot(a, b):
    return lax.dot_general(a, b, (((0,), (0,)), ((), ())), preferred_element_type=F32)


def iota(shape, axis):
    return lax.broadcasted_iota(I32, shape, axis)


def normalized(values):
    centred = values - jnp.mean(values, axis=-1, keepdims=True)
    spread = jnp.mean(centred * centred, axis=-1, keepdims=True)
    scale = lax.rsqrt(spread + EPS)
    return centred * scale, scale


def normal_cdf(u):
    return 0.5 + 0.5 * lax.erf(u * 0.7071067811865476)


def image_bias(bias):
    q, k = iota((2 * PAIR, PAIR), 0), iota((2 * PAIR, PAIR), 1)
    q = jnp.where(q >= PAIR, q - PAIR, q)
    place = jnp.where(k >= HALFP, k - HALFP, k)
    bias[...] = jnp.where(((q >= HALFP) == (k >= HALFP)) & (place < POS), 0.0, NEG)


def image_norm_one(tok, gain, stage):
    def rows(i, c):
        s = pl.ds(pl.multiple_of(i * 160, 160), 160)
        n, _ = normalized(tok[s, :].astype(F32))
        n = n * gain
        for h in range(6):
            stage[h, s, :] = n[:, h * 128 : h * 128 + 128]
        return c

    lax.fori_loop(0, 5, rows, 0)
    stage[:, IROWS:, :] = jnp.zeros((6, PROWS - IROWS, 128), F32)


def tiles(n, body):
    def step(i, c):
        body(i, pl.ds(pl.multiple_of(i * TILE, TILE), TILE))
        return c

    lax.fori_loop(0, n, step, 0)


def image_permute(stage, iap):
    def pair(p, c):
        for h in range(6):
            both = [stage[h, pl.ds(2 * p + i, HALFP, stride=IMGS), :] for i in range(2)]
            iap[pl.ds(pl.multiple_of(p * PAIR, PAIR), PAIR), h * 128 : h * 128 + 128] = jnp.concatenate(both, axis=0).astype(BF16)
        return c
    lax.fori_loop(0, IMGS // 2, pair, 0)


def image_qkv(iap, w, iqkv):
    def step(j, c):
        iqkv[j] = dot(iap[...], w[j]).astype(BF16)
        return c
    lax.fori_loop(0, 3, step, 0)


def stacked(values, low):
    zero = jnp.zeros_like(values)
    return jnp.concatenate([jnp.where(low, values, zero), jnp.where(low, zero, values)], axis=0)


def image_attention(iqkv, bias, stage, first, last, unroll=1):
    low = iota((PAIR, 128), 1) < 64

    def pair(p, c):
        rows = pl.ds(pl.multiple_of(p * PAIR, PAIR), PAIR)
        ones = jnp.ones((PAIR, 128), BF16)
        cols = [pl.ds(h * 128, 128) for h in range(6)]
        s = [dot_t(stacked(iqkv[0, rows, h], low), iqkv[1, rows, h]) * 0.125 + bias[...] for h in cols]
        e = [jnp.exp(x - jnp.max(x, axis=-1, keepdims=True)).astype(BF16) for x in s]
        for i, (h, x) in enumerate(zip(cols, e)):
            o = dot(x, jnp.concatenate([iqkv[2, rows, h], ones], axis=1))
            o = jnp.where(low, o[:PAIR, :128], o[PAIR:, :128]) / jnp.where(low, o[:PAIR, 128:], o[PAIR:, 128:])
            stage[i, pl.ds(2 * p, HALFP, stride=IMGS), :] = o[:HALFP]
            stage[i, pl.ds(2 * p + 1, HALFP, stride=IMGS), :] = o[HALFP:]
        return c

    lax.fori_loop(first, last, pair, 0, unroll=unroll)


def image_out(stage, tok, w, iy):
    def rows(i, c):
        s = pl.ds(pl.multiple_of(i * 160, 160), 160)
        iy[s, :] = tok[s, :].astype(F32) + dot(jnp.concatenate([stage[h, s, :].astype(BF16) for h in range(6)], axis=1), w[...])
        return c
    lax.fori_loop(0, 5, rows, 0)


def image_norm_two(iy, gain, ia, ypool):
    ypool[...] = jnp.zeros_like(ypool)
    def rows(i, c):
        s = pl.ds(pl.multiple_of(i * 160, 160), 160)
        y = iy[s, :]
        ypool[...] += jnp.sum(y.reshape(10, IMGS, D), axis=0)
        n, _ = normalized(y)
        ia[s, :] = (n * gain).astype(BF16)
        return c
    lax.fori_loop(0, 5, rows, 0)


def image_up(ia, w, hsum, first, last):
    def step(i, c):
        s = pl.ds(pl.multiple_of(i * UP_TILE, UP_TILE), UP_TILE)
        for m in range(5):
            u = dot(ia[160 * m : 160 * m + 160, :], w[:, s])
            part = jnp.sum((u * normal_cdf(u)).reshape(10, IMGS, UP_TILE), axis=0)
            total = part if m == 0 else total + part
        hsum[:, s] = total
        return c
    lax.fori_loop(first, last, step, 0)


def as_row(gain):
    return gain[...].reshape(1, D)


def column(values):
    rows = iota((OWN_CAPS, 128), 0)
    out = jnp.zeros((OWN_CAPS, 128), I32)
    for i in range(OWN_CAPS):
        out = jnp.where(rows == i, values[i], out)
    return out


def split_rows(x):
    hi = x.astype(BF16)
    return jnp.concatenate([hi, (x - hi.astype(F32)).astype(BF16)], axis=0)


def image_finish(hsum, ypool, w_down, w_proj):
    both = dot(split_rows(hsum[...]), w_down[...])
    pooled = ((ypool[...] + both[:IMGS] + both[IMGS:]) * (1.0 / POS)).astype(BF16)
    e = dot(pooled, w_proj[...])
    return (e * lax.rsqrt(jnp.sum(e * e, axis=-1, keepdims=True) + EPS)).astype(BF16)


GROUP, RANKS, CHIPS = 4, 32, 16
OWN, ROWS = 128, 512
CAPS, OWN_CAPS = 64, 16
PART = OWN // 2
BAND = 192
HALF = 384
MESH = pl.DeviceIdType.MESH
VEC = 1664
PAIRS = 53


class Links:
    def __init__(self):
        self.dp, self.t = lax.axis_index("dp"), lax.axis_index("tensor")
        self.core, self.chip = lax.rem(self.dp, 2), self.dp // 2
        self.place = {"x": lax.rem(self.chip, 4), "z": self.chip // 4}

    def rank(self, k):
        return lax.rem(self.t + k, GROUP)

    def group_peer(self, k):
        return {"dp": self.dp, "tensor": self.rank(k)}

    def rank_peer(self, k):
        return {"dp": lax.rem(self.dp + k, RANKS), "tensor": self.t}

    def chip_of(self, k):
        return lax.rem(self.chip + k, CHIPS)

    def chip_peer(self, k):
        return {"dp": 2 * self.chip_of(k) + self.core, "tensor": self.t}

    def axis_rank(self, axis, k):
        return lax.rem(self.place[axis] + k, 4)

    def axis_peer(self, axis, k):
        place = dict(self.place)
        place[axis] = self.axis_rank(axis, k)
        return {"dp": 2 * (place["z"] * 4 + place["x"]) + self.core, "tensor": self.t}

    def sibling(self):
        return {"dp": self.dp + 1 - 2 * self.core, "tensor": self.t}

    def greet(self):
        barrier = pltpu.get_barrier_semaphore()
        for k in range(1, GROUP):
            pl.semaphore_signal(barrier, 1, device_id=self.group_peer(k), device_id_type=MESH)
        for k in range(1, RANKS):
            pl.semaphore_signal(barrier, 1, device_id=self.rank_peer(k), device_id_type=MESH)

    def met(self):
        pl.semaphore_wait(pltpu.get_barrier_semaphore(), GROUP - 1 + RANKS - 1)


def send(src, dst, sems, peer):
    pltpu.make_async_remote_copy(src, dst, sems.at[0], sems.at[1], device_id=peer, device_id_type=MESH).start()


def finish(exchange):
    sems, span = exchange
    for i in range(2):
        pltpu.make_async_copy(span, span, sems.at[i]).wait()


def sent(exchange):
    sems, span = exchange
    pltpu.make_async_copy(span, span, sems.at[0]).wait()


def arrived(exchange):
    sems, span = exchange
    pltpu.make_async_copy(span, span, sems.at[1]).wait()


def group_share(links, buf, sems):
    own = buf.at[links.t]
    for k in (1, 3, 2):
        send(own, own, sems, links.group_peer(k))
    return sems, buf.at[pl.ds(0, 3)]


def group_scatter(links, parts, landed, sems):
    for k in (1, 3, 2):
        send(parts.at[links.rank(k)], landed.at[k - 1], sems, links.group_peer(k))
    return sems, landed


def half_rows(h):
    return pl.ds(h * PART, PART)


def share_half(links, buf, sems, h):
    own = buf.at[links.t, half_rows(h)]
    for k in (1, 3, 2):
        send(own, own, sems, links.group_peer(k))
    return sems, buf.at[pl.ds(0, 3), half_rows(h)]


def scatter_half(links, parts, landed, sems, h):
    for k in (1, 3, 2):
        send(parts.at[links.rank(k), half_rows(h)], landed.at[k - 1, half_rows(h)], sems, links.group_peer(k))
    return sems, landed.at[pl.ds(0, 3), half_rows(h)]


def rank_share(links, buf, sems):
    own = buf.at[links.dp]
    for k in range(1, RANKS):
        send(own, own, sems, links.rank_peer(k))
    return sems, buf.at[pl.ds(0, RANKS - 1)]


def chip_share(links, buf, sems):
    own = buf.at[links.chip]
    for k in range(1, CHIPS):
        send(own, own, sems, links.chip_peer(k))
    return sems, buf.at[pl.ds(0, CHIPS - 1)]


def sibling_send(links, src, dst, sems):
    send(src, dst, sems, links.sibling())
    return sems, src


def text_masks(seg_t, pad_t, bias, mem, mem_t):
    seg, pad = seg_t[...].astype(F32).astype(BF16), pad_t[...].astype(F32).astype(BF16)

    def as_column(values):
        pick = jnp.where(iota((ROWS, 32), 0) >> 4 == iota((ROWS, 32), 1), 1.0, 0.0).astype(BF16)
        wide = dot_t(pick, values)
        return jnp.sum(jnp.where(iota((ROWS, 16), 0) & 15 == iota((ROWS, 16), 1), wide, 0.0), axis=1, keepdims=True)

    def as_row(values):
        pick = jnp.where(iota((32, ROWS), 1) >> 4 == iota((32, ROWS), 0), 1.0, 0.0).astype(BF16)
        wide = dot(values, pick)
        return jnp.sum(jnp.where(iota((16, ROWS), 1) & 15 == iota((16, ROWS), 0), wide, 0.0), axis=0, keepdims=True)

    cap_col = as_column(seg) + ((iota((ROWS, 1), 0) >> 4) * 2).astype(F32)
    key_col = jnp.where(as_column(pad) > 0.5, cap_col, -1.0)
    cap_row = as_row(seg) + ((iota((1, ROWS), 1) >> 4) * 2).astype(F32)
    key_row = jnp.where(as_row(pad) > 0.5, cap_row, -1.0)
    for b in range(4):
        rows = slice(128 * b, 128 * b + 128)
        bias[b] = jnp.where(cap_col[rows] == key_row[:, rows], 0.0, NEG)
    mem[...] = jnp.where(iota((CAPS, ROWS), 0).astype(F32) == key_row, 1.0, 0.0).astype(BF16)
    mem_t[...] = jnp.where((iota((ROWS, 128), 1) & 63).astype(F32) == key_col, 1.0, 0.0).astype(BF16)


def text_norm_one(x, gain, a1, t):
    n, _ = normalized(x[...].astype(F32))
    a1[t] = (n * gain).astype(BF16)


def low_half():
    return iota((OWN, 128), 1) < 64


def text_attention(a1, w_t, bias, w_out, qkv, probs, att, parts):
    rows_all = a1[...].reshape(ROWS, D)
    for j in range(3):
        qkv[j] = dot_t(rows_all, w_t[j]).astype(BF16)
    low = low_half()
    blocks = [slice(128 * b, 128 * b + 128) for b in range(4)]
    scores = []
    for b, rows in enumerate(blocks):
        mask = bias[b]
        scores.append(dot_t(stacked(qkv[0, rows, :128], low), qkv[1, rows, :128]) * 0.125 + jnp.concatenate([mask, mask], axis=0))
        scores.append(dot_t(qkv[0, rows, 128:], qkv[1, rows, 128:]) * 0.125 + mask)
    powers = [jnp.exp(x - jnp.max(x, axis=-1, keepdims=True)) for x in scores]
    shares = [x / jnp.sum(x, axis=-1, keepdims=True) for x in powers]
    for b, rows in enumerate(blocks):
        probs[b, :256] = shares[2 * b]
        probs[b, 256:] = shares[2 * b + 1]
        o = dot(shares[2 * b].astype(BF16), qkv[2, rows, :128])
        att[rows, :128] = jnp.where(low, o[:128], o[128:]).astype(BF16)
        att[rows, 128:] = dot(shares[2 * b + 1].astype(BF16), qkv[2, rows, 128:]).astype(BF16)
    parts[...] = dot(att[...], w_out[...]).astype(BF16).reshape(GROUP, OWN, D)


def summed(parts, landed, t, rows):
    return parts[t, rows].astype(F32) + landed[0, rows].astype(F32) + landed[1, rows].astype(F32) + landed[2, rows].astype(F32)


def split3(x):
    hi = x.astype(BF16)
    rest = x - hi.astype(F32)
    mid = rest.astype(BF16)
    return jnp.concatenate([hi, mid, (rest - mid.astype(F32)).astype(BF16)], axis=0)


def own_member(mem, t):
    return mem[pl.ds(pl.multiple_of(t * OWN_CAPS, OWN_CAPS), OWN_CAPS), pl.ds(pl.multiple_of(t * OWN, OWN), OWN)]


def text_norm_two(h, x, parts, landed, gain, x1, a2, t):
    rows = half_rows(h)
    y = x[rows, :].astype(F32) + summed(parts, landed, t, rows)
    x1[rows, :] = y
    n, _ = normalized(y)
    a2[t, rows] = (n * gain).astype(BF16)


def text_pool_one(x1, mem, x1_pool, t):
    own = own_member(mem, t)
    x1_pool[...] = dot(jnp.concatenate([own, own, own], axis=1), split3(x1[...]))


def text_up(a2, w_up, mem, w_down, x1_pool, dgelu, hidden, hsum, part, parts, t):
    for r in range(GROUP):
        rows = slice(r * OWN, r * OWN + OWN)
        u = dot(a2[r], w_up[...])
        phi = normal_cdf(u)
        dgelu[rows, :] = phi + u * (jnp.exp(u * u * -0.5) * 0.3989422804014327)
        hidden[rows, :] = (u * phi).astype(BF16)
    hsum[...] = dot(mem[...], hidden[...])
    both = dot(split_rows(hsum[...]), w_down[...])
    part[...] = (both[:CAPS] + both[CAPS:]).reshape(GROUP, OWN_CAPS, D)
    part[t] += x1_pool[...]
    parts[t] = part[...].reshape(CAPS, D).astype(BF16)


def counts_of(mem):
    return jnp.sum(mem.astype(F32), axis=1, keepdims=True)


def text_embed(parts, mem, w_proj, pooled, tf, scale):
    total = parts[0].astype(F32) + parts[1].astype(F32) + parts[2].astype(F32) + parts[3].astype(F32)
    rows = (total / counts_of(mem[...])).astype(BF16)
    pooled[...] = rows
    e = dot(rows, w_proj[...])
    rs = lax.rsqrt(jnp.sum(e * e, axis=-1, keepdims=True) + EPS)
    tf[...] = rs * e
    scale[...] = jnp.broadcast_to(rs, (CAPS, 128))


def score_sums(tf, images, s_ref, e_ref, row_sums, col_sums, t, dp):
    s = 40.0 * dot_t(tf[...].astype(BF16), images[...].reshape(ROWS, D))
    s_ref[...] = s
    e = jnp.exp(s - 40.0)
    e_ref[...] = e
    diagonal = iota((CAPS, 128), 0) == iota((CAPS, 128), 1)
    row_sums[t] = jnp.sum(jnp.where(diagonal, jnp.sum(e, axis=1, keepdims=True), 0.0), axis=0, keepdims=True)
    col_sums[dp] = jnp.sum(e, axis=0, keepdims=True)


def score_grad(s_ref, e_ref, row_sums, col_sums, pair, images, dts, vec, t):
    diagonal = iota((CAPS, 128), 0) == iota((CAPS, 128), 1)
    rows = jnp.sum(jnp.where(diagonal, row_sums[0] + row_sums[1] + row_sums[2] + row_sums[3], 0.0), axis=1, keepdims=True)
    cols = col_sums[0]
    for i in range(1, RANKS):
        cols = cols + col_sums[i]
    lane = iota((CAPS, ROWS), 1)
    image = ((lane >> 4) & 15) * (2 * CAPS) + (lane >> 8) * CAPS + (lane & 15) + OWN_CAPS * t
    target = jnp.where(pair[...].reshape(CAPS, 128)[:, :1] == image, 1.0, 0.0)
    g = 0.5 * (e_ref[...] / rows + e_ref[...] / cols) - target
    dts[t] = (40.0 * dot(g.astype(BF16), images[...].reshape(ROWS, D))).astype(BF16)
    loss = (
        jnp.sum(40.0 + jnp.log(rows), axis=0, keepdims=True) * (1.0 / GROUP)
        + jnp.sum(40.0 + jnp.log(cols), axis=1, keepdims=True) * (1.0 / RANKS)
        - 2.0 * jnp.sum(jnp.sum(s_ref[...] * target, axis=1, keepdims=True), axis=0, keepdims=True)
    )
    vec[t, :, 1536:] = jnp.broadcast_to(loss, (1, 128))


def embed_grad(dts, tf, scale, w_proj, mem, de_ref, dz_ref, gp_ref):
    dt = dts[0].astype(F32) + dts[1].astype(F32) + dts[2].astype(F32) + dts[3].astype(F32)
    f = tf[...]
    de = (scale[:, :1] * (dt - f * jnp.sum(f * dt, axis=-1, keepdims=True))).astype(BF16)
    gp = dot_t(de, w_proj[...]) / counts_of(mem[...])
    de_ref[...] = de
    gp_ref[...] = gp
    dz_ref[...] = gp.astype(BF16)


def row_grad(gp_ref, mem, dx2, t):
    own = own_member(mem, t)
    gp = gp_ref[pl.ds(pl.multiple_of(t * OWN_CAPS, OWN_CAPS), OWN_CAPS), :]
    dx2[...] = t_dot(jnp.concatenate([own, own, own], axis=0), split3(gp))


def hidden_grad(dz, w_down):
    return split_rows(dot_t(dz[...], w_down[...]))


def hidden_spread(h, dh, mem_t, dgelu, w_up, du, parts):
    blocks = [pl.ds(r * OWN + h * PART, PART) for r in range(GROUP)]
    member = jnp.concatenate([mem_t[b, :] for b in blocks], axis=0)
    slope = jnp.concatenate([dgelu[b, :] for b in blocks], axis=0)
    rows = (dot(member, dh) * slope).astype(BF16)
    total = dot_t(rows, w_up[...]).astype(BF16)
    for r, b in enumerate(blocks):
        du[b, :] = rows[r * PART : (r + 1) * PART]
        parts[r, half_rows(h)] = total[r * PART : (r + 1) * PART]


def gain_grad(parts, normed, gain):
    total = jnp.zeros((1, D), F32)
    for r in range(GROUP):
        total = total + jnp.sum(parts[r].astype(F32) * normed[r].astype(F32), axis=0, keepdims=True)
    return total / gain


def put_chunks(g, first, values):
    rows = g.shape[-2]
    for c in range(values.shape[0] // rows):
        at = first + c
        place = (at,) if len(g.shape) == 4 else (at // 4, at % 4)
        for j in range(2):
            g[(j, *place)] = values[c * rows : (c + 1) * rows, j * HALF : (j + 1) * HALF].astype(BF16)


def down_proj_grad(hsum, dz, de, pooled, proj, g, h, t):
    hs = split_rows(hsum[...])
    dz2 = jnp.concatenate([dz[...], dz[...]], axis=0)
    put_chunks(g, 0, t_dot(hs[:, :256], dz2))
    put_chunks(g, 8, t_dot(hs[:, 256:512], dz2))
    put_chunks(h, 0, t_dot(hs[:, 512:], dz2))
    proj[...] = t_dot(pooled[...], de[...]).astype(BF16).reshape(GROUP, BAND, D)
    put_chunks(h, 8, proj[t])
    h[:, 3, 2:] = jnp.zeros((2, 2, 32, HALF), BF16)


def up_grad(a2, du, g, h):
    for i in range(3):
        rows = t_dot(a2[:, :, i * 256 : (i + 1) * 256].reshape(ROWS, 256), du[...])
        put_chunks(g if i < 2 else h, 8 * i if i < 2 else 0, rows)


def norm_two_grad(h, parts, landed, x1, gain, dx2, dx1, dy, t):
    rows = half_rows(h)
    da = summed(parts, landed, t, rows)
    n, scale = normalized(x1[rows, :])
    d = da * gain
    g = dx2[rows, :] + (d - jnp.mean(d, axis=-1, keepdims=True) - n * jnp.mean(d * n, axis=-1, keepdims=True)) * scale
    dx1[rows, :] = g
    dy[t, rows] = g.astype(BF16)


def attention_grad(dy, w_out, w_t, qkv, probs, dqkv, parts):
    datt = dot_t(dy[...].reshape(ROWS, D), w_out[...]).astype(BF16)
    low = low_half()
    blocks = [slice(128 * b, 128 * b + 128) for b in range(4)]
    sides, raw = [], []
    for b, rows in enumerate(blocks):
        sides.append((stacked(qkv[0, rows, :128], low), stacked(datt[rows, :128], low)))
        sides.append((qkv[0, rows, 128:], datt[rows, 128:]))
        raw.append(dot_t(sides[-2][1], qkv[2, rows, :128]))
        raw.append(dot_t(sides[-1][1], qkv[2, rows, 128:]))
    probs_of = [probs[b, part] for b in range(4) for part in (slice(0, 256), slice(256, 384))]
    ds = [(p * (x - jnp.sum(p * x, axis=-1, keepdims=True))).astype(BF16) for p, x in zip(probs_of, raw)]
    for b, rows in enumerate(blocks):
        for i, cols in ((2 * b, slice(0, 128)), (2 * b + 1, slice(128, BAND))):
            o = dot(ds[i], qkv[1, rows, cols])
            if i % 2 == 0:
                o = jnp.where(low, o[:128], o[128:])
            dqkv[0, rows, cols] = (o * 0.125).astype(BF16)
            dqkv[1, rows, cols] = (t_dot(ds[i], sides[i][0]) * 0.125).astype(BF16)
            dqkv[2, rows, cols] = t_dot(probs_of[i].astype(BF16), sides[i][1]).astype(BF16)
    total = dot(dqkv[0], w_t[0]) + dot(dqkv[1], w_t[1]) + dot(dqkv[2], w_t[2])
    parts[...] = total.astype(BF16).reshape(GROUP, OWN, D)


def out_grad(att, dy, g):
    put_chunks(g, 0, t_dot(att[...], dy[...].reshape(ROWS, D)))


def qkv_grad(dqkv, a1, g, h):
    rows = a1[...].reshape(ROWS, D)
    put_chunks(g, 6, t_dot(dqkv[0], rows))
    keys = t_dot(dqkv[1], rows)
    put_chunks(g, 12, keys[:128])
    put_chunks(h, 0, keys[128:])
    put_chunks(h, 4, t_dot(dqkv[2], rows))


def norm_one_grad(parts, landed, x, gain, dx1, out, t):
    da = summed(parts, landed, t, slice(0, OWN))
    n, scale = normalized(x[...].astype(F32))
    h = da * gain
    out[...] = dx1[...] + (h - jnp.mean(h, axis=-1, keepdims=True) - n * jnp.mean(h * n, axis=-1, keepdims=True)) * scale


class Reduction:
    def __init__(self, links, g, met, landed, full, pair):
        self.links, self.g, self.met, self.landed, self.full, self.pair = links, g, met, landed, full, pair

    def cores(self):
        self.open = sibling_send(self.links, self.g.at[1 - self.links.core], self.met, self.pair())

    def both_cores(self):
        finish(self.open)
        self.met[...] = (self.g[self.links.core].astype(F32) + self.met[...].astype(F32)).astype(BF16)

    def scatter(self):
        self.both_cores()
        sems = self.pair()
        for k in range(1, CHIPS):
            send(self.met.at[self.links.chip_of(k)], self.landed.at[k - 1], sems, self.links.chip_peer(k))
        self.open = sems, self.landed

    def gather(self):
        finish(self.open)
        total = self.met[self.links.chip].astype(F32)
        for k in range(CHIPS - 1):
            total = total + self.landed[k].astype(F32)
        half = self.full.at[self.links.core]
        half[self.links.chip] = total.astype(BF16)
        self.open = chip_share(self.links, half, self.pair())

    def share(self):
        finish(self.open)
        half = self.full.at[self.links.core]
        self.open = sibling_send(self.links, half, half, self.pair())

    def done(self):
        finish(self.open)


class TwoAxes(Reduction):
    def __init__(self, links, g, met, landed, near, full, pair, first, second):
        super().__init__(links, g, met, landed, full, pair)
        self.near, self.first, self.second = near, first, second
        self.i, self.j = links.place[first], links.place[second]

    def spread(self, axis, source, target):
        sems = self.pair()
        for k in (1, 3, 2):
            send(source(k), target(k), sems, self.links.axis_peer(axis, k))
        return sems

    def scatter(self):
        self.both_cores()
        sems = self.spread(
            self.first, lambda k: self.met.at[self.links.axis_rank(self.first, k)], lambda k: self.landed.at[k - 1]
        )
        self.open = sems, self.landed

    def scatter_second(self):
        finish(self.open)
        total = self.met[self.i].astype(F32)
        for k in range(3):
            total = total + self.landed[k].astype(F32)
        self.met[self.i] = total.astype(BF16)
        sems = self.spread(
            self.second, lambda k: self.met.at[self.i, self.links.axis_rank(self.second, k)], lambda k: self.near.at[k - 1]
        )
        self.open = sems, self.near

    def gather(self):
        finish(self.open)
        total = self.met[self.i, self.j].astype(F32)
        for k in range(3):
            total = total + self.near[k].astype(F32)
        core = self.links.core
        self.full[core, self.i, self.j] = total.astype(BF16)
        own = self.full.at[core, self.i, self.j]
        self.open = self.spread(self.second, lambda k: own, lambda k: own), self.full.at[0, 0, pl.ds(0, 3)]

    def gather_second(self):
        finish(self.open)
        own = self.full.at[self.links.core, self.i]
        self.open = self.spread(self.first, lambda k: own, lambda k: own), self.full.at[0, pl.ds(0, 3)]


def body(
    x, seg_t, pad_t, pair_in, gain_one, gain_two, img_gain_one, img_gain_two,
    h_tok, h_iqkv, h_iout, h_iup, h_idown, h_iproj, h_qkv, h_out, h_up, h_down, h_proj,
    o_loss, o_input, o_norms, f_a0, f_a1, f_b0, f_b1, f_c0, f_c1, proj_all,
    tok, iw_qkv, iw_out, iw_up, iw_down, iw_proj, w_qkv, w_out, w_up, w_down, w_proj, load,
    ibias, iap, iqkv, stage, iy, ypool, ihsum, images,
    bias, mem, mem_t, pair, a1, qkv, probs, att, p_att, l_att, x1, x1_pool, a2, dgelu, hsum, p_pool, pools,
    tf, scale, pooled, s_ref, e_ref, row_sums, col_sums, dts, de, dz, gp, dx2, du, p_da2, l_da2, dx1, dy,
    dqkv, p_da1, l_da1, proj, vec, vec_all,
    *work,
):
    g_a, g_b, g_c, m_a, m_b, m_c, r_a, r_b, r_c, n_a, n_b = (work[i : i + 2] for i in range(0, 22, 2))
    f_a, f_b, f_c = (f_a0, f_a1), (f_b0, f_b1), (f_c0, f_c1)
    sems = work[22]
    links = Links()
    t, dp, core, chip = links.t, links.dp, links.core, links.chip
    loads = {}
    count = iter(range(PAIRS))

    def pair_of():
        return sems.at[next(count)]


    def fetch(at, name, src, dst):
        loads[name] = pltpu.make_async_copy(src, dst, load.at[at])
        loads[name].start()

    fetch(0, "tok", h_tok, tok)
    fetch(1, "iqkv", h_iqkv, iw_qkv)
    links.greet()
    text_norm_one(x, as_row(gain_one), a1, t)
    pair[t] = column(pair_in)
    links.met()
    copies = group_share(links, a1, pair_of())
    pair_copies = group_share(links, pair, pair_of())
    fetch(2, "qkv", h_qkv, w_qkv)
    fetch(3, "out", h_out, w_out)
    fetch(4, "iout", h_iout, iw_out)

    text_masks(seg_t, pad_t, bias, mem, mem_t)
    image_bias(ibias)
    loads["tok"].wait()
    image_norm_one(tok, as_row(img_gain_one), stage)
    fetch(5, "iup", h_iup, iw_up)
    fetch(6, "up", h_up, w_up)
    fetch(7, "down", h_down, w_down)
    fetch(8, "idown", h_idown, iw_down)
    fetch(9, "iproj", h_iproj, iw_proj)
    fetch(10, "proj", h_proj, w_proj)
    image_permute(stage, iap)
    loads["iqkv"].wait()
    image_qkv(iap, iw_qkv, iqkv)

    finish(copies)
    loads["qkv"].wait()
    loads["out"].wait()
    text_attention(a1, w_qkv, bias, w_out, qkv, probs, att, p_att)
    copies = [scatter_half(links, p_att, l_att, pair_of(), 0)]

    image_attention(iqkv, ibias, stage, 0, 4)
    copies.append(scatter_half(links, p_att, l_att, pair_of(), 1))
    image_attention(iqkv, ibias, stage, 4, 8)
    finish(copies[0])
    text_norm_two(0, x, p_att, l_att, as_row(gain_two), x1, a2, t)
    copies[0] = share_half(links, a2, pair_of(), 0)
    loads["iout"].wait()
    image_out(stage, tok, iw_out, iy)
    finish(copies[1])
    text_norm_two(1, x, p_att, l_att, as_row(gain_two), x1, a2, t)
    copies[1] = share_half(links, a2, pair_of(), 1)
    image_norm_two(iy, as_row(img_gain_two), iap.at[:IROWS], ypool)

    loads["iup"].wait()
    image_up(iap.at[:IROWS], iw_up, ihsum, 0, 1)
    text_pool_one(x1, mem, x1_pool, t)

    image_up(iap.at[:IROWS], iw_up, ihsum, 1, FF // UP_TILE)
    loads["idown"].wait()
    loads["iproj"].wait()
    images[core, chip] = image_finish(ihsum, ypool, iw_down, iw_proj)
    image_copies = chip_share(links, images.at[core], pair_of())

    finish(copies[0])
    finish(copies[1])
    loads["up"].wait()
    loads["down"].wait()
    text_up(a2, w_up, mem, w_down, x1_pool, dgelu, du, hsum, p_pool, pools, t)
    copies = group_share(links, pools, pair_of())
    finish(image_copies)
    image_copies = sibling_send(links, images.at[core], images.at[core], pair_of())
    finish(pair_copies)
    loads["proj"].wait()
    finish(copies)
    text_embed(pools, mem, w_proj, pooled, tf, scale)
    finish(image_copies)

    score_sums(tf, images, s_ref, e_ref, row_sums, col_sums, t, dp)
    row_copies = group_share(links, row_sums, pair_of())
    col_copies = rank_share(links, col_sums, pair_of())
    finish(col_copies)
    finish(row_copies)
    score_grad(s_ref, e_ref, row_sums, col_sums, pair, images, dts, vec, t)
    finish(group_share(links, dts, pair_of()))
    embed_grad(dts, tf, scale, w_proj, mem, de, dz, gp)

    red_a = [TwoAxes(links, g_a[i], m_a[i], r_a[i], n_a[i], f_a[i], pair_of, "x", "z") for i in range(2)]
    red_b = [TwoAxes(links, g_b[i], m_b[i], r_b[i], n_b[i], f_b[i], pair_of, "z", "x") for i in range(2)]
    red_c = [Reduction(links, g_c[i], m_c[i], r_c[i], f_c[i], pair_of) for i in range(2)]

    def each(*steps):
        for step in steps:
            step()

    dh = hidden_grad(dz, w_down)
    hidden_spread(0, dh, mem_t, dgelu, w_up, du, p_da2)
    copies = [scatter_half(links, p_da2, l_da2, pair_of(), 0)]
    hidden_spread(1, dh, mem_t, dgelu, w_up, du, p_da2)
    down_proj_grad(hsum, dz, de, pooled, proj, g_a[0], g_a[1], t)
    each(red_a[0].cores, red_a[1].cores)
    up_grad(a2, du, g_b[0], g_b[1])
    each(red_b[0].cores, red_b[1].cores)
    sent(copies[0])
    copies.append(scatter_half(links, p_da2, l_da2, pair_of(), 1))
    row_grad(gp, mem, dx2, t)
    vec[t, :, 768:1536] = gain_grad(p_da2, a2, as_row(gain_two))
    each(red_a[0].scatter, red_b[0].scatter, red_a[1].scatter, red_b[1].scatter)
    arrived(copies[0])
    norm_two_grad(0, p_da2, l_da2, x1, as_row(gain_two), dx2, dx1, dy, t)
    copies[0] = share_half(links, dy, pair_of(), 0)
    finish(copies[1])
    norm_two_grad(1, p_da2, l_da2, x1, as_row(gain_two), dx2, dx1, dy, t)
    copies[1] = share_half(links, dy, pair_of(), 1)
    each(red_a[0].scatter_second, red_b[0].scatter_second)
    each(red_a[1].scatter_second, red_b[1].scatter_second)
    each(red_a[0].gather, red_b[0].gather)
    each(red_a[1].gather, red_b[1].gather)
    each(red_a[0].gather_second, red_b[0].gather_second)
    finish(copies[0])
    finish(copies[1])
    out_grad(att, dy, g_c[0])
    attention_grad(dy, w_out, w_qkv, qkv, probs, dqkv, p_da1)
    each(red_a[1].gather_second, red_b[1].gather_second)
    vec[t, :, :768] = gain_grad(p_da1, a1, as_row(gain_one))
    vec_copies = group_share(links, vec, pair_of())
    copies = group_scatter(links, p_da1, l_da1, pair_of())
    qkv_grad(dqkv, a1, g_c[0], g_c[1])
    each(red_c[0].cores, red_c[1].cores, red_c[0].scatter, red_c[1].scatter)
    finish(vec_copies)
    vec_all[dp] = vec[0] + vec[1] + vec[2] + vec[3]
    vec_copies = rank_share(links, vec_all, pair_of())
    each(red_a[1].share, red_a[0].share, red_b[0].share, red_b[1].share)
    proj_all[core, t, :4] = f_a1[core, 2]
    proj_all[core, t, 4:] = f_a1[core, 3, :2]
    proj_copies = group_share(links, proj_all.at[core], pair_of())
    finish(copies)
    norm_one_grad(p_da1, l_da1, x, as_row(gain_one), dx1, o_input, t)
    each(red_c[0].gather, red_c[1].gather)
    finish(proj_copies)
    proj_copies = sibling_send(links, proj_all.at[core], proj_all.at[core], pair_of())
    each(red_a[0].done, red_a[1].done, red_b[0].done, red_b[1].done)
    finish(vec_copies)
    total = vec_all[0]
    for i in range(1, RANKS):
        total = total + vec_all[i]
    o_norms[...] = total[:, :1536]
    o_loss[...] = total[:, 1536:] * (1.0 / 4096.0)
    finish(proj_copies)
    each(red_c[0].share, red_c[1].share, red_c[0].done, red_c[1].done)


def widen(
    loss, norms, grad, a0, a1, b0, b1, c0, c1, full_proj,
    o_loss, o_input, o_one, o_two, o_down, o_up, o_out, o_qkv, o_proj, down, up, out, qkv, proj, stored,
):
    stores = []

    def write(buf, target):
        stores.append(pltpu.make_async_copy(buf, target, stored.at[len(stores)]))
        stores[-1].start()

    def halves(target, first, parts, rows):
        for j in range(2):
            target[first : first + rows, j * HALF : (j + 1) * HALF] = parts[j].reshape(rows, HALF).astype(F32)

    write(grad, o_input)
    halves(down, 0, a0, 512)
    halves(down, 512, a1[:, :2], 256)
    write(down, o_down)
    halves(up, 0, b0, 512)
    halves(up, 512, b1, 256)
    write(up, o_up)
    halves(proj, 0, full_proj, D)
    write(proj, o_proj)
    halves(out, 0, c0[:, :6], BAND)
    write(out, o_out)
    halves(qkv, 0, c0[:, 6:], 320)
    halves(qkv, 320, c1, 256)
    write(qkv, o_qkv)
    o_loss[0, 0] = loss[0, 0]
    o_one[...] = norms[:, :D].reshape(D)
    o_two[...] = norms[:, D:].reshape(D)
    for copy in stores:
        copy.wait()


def on_device(
    text_input, segment_ids, pad_mask, pairing, ln_first, w_qkv, w_out, ln_second, w_up, w_down, text_proj,
    image_tokens, img_ln_first, img_w_qkv, img_w_out, img_ln_second, img_w_up, img_w_down, img_proj,
):
    vmem = pl.BlockSpec(memory_space=VM)
    hbm = pl.BlockSpec(memory_space=pl.ANY)
    shape = jax.ShapeDtypeStruct
    sums = ((4, 4, 32, HALF),) * 2 + ((4, 4, 32, HALF), (4, 4, 16, HALF)) + ((16, 32, HALF), (16, 16, HALF))
    dma = pltpu.SemaphoreType.DMA
    scratch = [
        VM((IROWS, D), BF16), VM((3, D, D), BF16), VM((D, D), BF16), VM((D, FF), BF16), VM((FF, D), BF16), VM((D, D), BF16),
        VM((3, BAND, D), BF16), VM((BAND, D), BF16), VM((D, HID), BF16), VM((HID, D), BF16), VM((D, D), BF16), dma((11,)),
        VM((2 * PAIR, PAIR), F32), VM((PROWS, D), BF16), VM((3, PROWS, D), BF16), VM((6, PROWS, 128), F32), VM((IROWS, D), F32),
        VM((IMGS, D), F32), VM((IMGS, FF), F32), VM((2, CHIPS, IMGS, D), BF16),
        VM((4, 128, 128), F32), VM((CAPS, ROWS), BF16), VM((ROWS, 128), BF16), VM((GROUP, OWN_CAPS, 128), I32),
        VM((GROUP, OWN, D), BF16), VM((3, ROWS, BAND), BF16), VM((4, HALF, 128), F32), VM((ROWS, BAND), BF16),
        VM((GROUP, OWN, D), BF16), VM((3, OWN, D), BF16), VM((OWN, D), F32), VM((OWN_CAPS, D), F32), VM((GROUP, OWN, D), BF16),
        VM((ROWS, HID), F32), VM((CAPS, HID), F32), VM((GROUP, OWN_CAPS, D), F32), VM((GROUP, CAPS, D), BF16),
        VM((CAPS, D), F32), VM((CAPS, 128), F32), VM((CAPS, D), BF16), VM((CAPS, ROWS), F32),
        VM((CAPS, ROWS), F32), VM((GROUP, 1, 128), F32), VM((RANKS, 1, ROWS), F32), VM((GROUP, CAPS, D), BF16),
        VM((CAPS, D), BF16), VM((CAPS, D), BF16), VM((CAPS, D), F32),
        VM((OWN, D), F32), VM((ROWS, HID), BF16), VM((GROUP, OWN, D), BF16), VM((3, OWN, D), BF16), VM((OWN, D), F32),
        VM((GROUP, OWN, D), BF16), VM((3, ROWS, BAND), BF16), VM((GROUP, OWN, D), BF16), VM((3, OWN, D), BF16),
        VM((GROUP, BAND, D), BF16), VM((GROUP, 1, VEC), F32), VM((RANKS, 1, VEC), F32),
    ]
    scratch += [VM((2,) + s, BF16) for s in sums] + [VM(s, BF16) for s in sums]
    scratch += [VM((3,) + s[1:], BF16) for s in sums[:4]] + [VM((15,) + s[1:], BF16) for s in sums[4:]]
    scratch += [VM((3,) + s[2:], BF16) for s in sums[:4]] + [dma((PAIRS, 2))]
    loss, input_grad, norms, *full = pl.pallas_call(
        body,
        out_shape=(
            VM((1, 128), F32), VM((OWN, D), F32), VM((1, 1536), F32),
            *(VM((2,) + s, BF16) for s in sums), VM((2, GROUP, 6, 32, HALF), BF16),
        ),
        in_specs=[vmem] * 3 + [pl.BlockSpec(memory_space=pltpu.SMEM)] + [vmem] * 4 + [hbm] * 11,
        out_specs=(vmem,) * 10,
        scratch_shapes=scratch,
        compiler_params=pltpu.CompilerParams(collective_id=0, has_side_effects=True, vmem_limit_bytes=57 << 20),
        name="lit",
    )(
        text_input, segment_ids.T, pad_mask.T, pairing, ln_first, ln_second, img_ln_first, img_ln_second,
        image_tokens.transpose(1, 0, 2).reshape(IROWS, D), img_w_qkv, img_w_out, img_w_up, img_w_down, img_proj,
        w_qkv.swapaxes(1, 2), w_out, w_up, w_down, text_proj,
    )

    loss, input_grad, one, two, down, up, out, qkv, proj = pl.pallas_call(
        widen,
        out_shape=(
            shape((1, 1), F32), shape((OWN, D), F32), shape((D,), F32), shape((D,), F32), shape((HID, D), F32),
            shape((D, HID), F32), shape((BAND, D), F32), shape((3 * BAND, D), F32), shape((D, D), F32),
        ),
        in_specs=[vmem] * 10,
        out_specs=(pl.BlockSpec(memory_space=pltpu.SMEM), hbm, vmem, vmem, hbm, hbm, hbm, hbm, hbm),
        scratch_shapes=[
            VM((HID, D), F32), VM((D, HID), F32), VM((BAND, D), F32), VM((3 * BAND, D), F32), VM((D, D), F32),
            dma((6,)),
        ],
        compiler_params=pltpu.CompilerParams(vmem_limit_bytes=40 << 20),
        name="widen",
    )(loss, norms, input_grad, *full)
    return (loss.reshape(()), input_grad, one, qkv.reshape(3, BAND, D).swapaxes(1, 2), out, two, up, down, proj)


def solution(mesh):
    rows = P(("dp", "tensor"))
    in_specs = (
        P(("dp", "tensor"), None), P("dp", None), P("dp", None), rows, P(), P(None, None, "tensor"), P("tensor", None), P(),
        P(None, "tensor"), P("tensor", None), P(), P(("dp", "tensor"), None, None), P(), P(), P(), P(), P(), P(), P(),
    )
    out_specs = (
        P(), P(("dp", "tensor"), None), P(), P(None, None, "tensor"), P("tensor", None), P(), P(None, "tensor"),
        P("tensor", None), P(),
    )
    return jax.shard_map(on_device, mesh=mesh, in_specs=in_specs, out_specs=out_specs, check_vma=False)
```

```python
import jax, jax.numpy as jnp
from jax import lax
from jax.experimental import pallas as pl
from jax.experimental.pallas import tpu as pltpu
from jax.sharding import PartitionSpec as P

F32, BF16, I32 = jnp.float32, jnp.bfloat16, jnp.int32
VM = pltpu.VMEM
EPS = 1e-6
NEG = -1e30
D, FF, HID = 768, 3072, 768
IMGS, POS = 16, 50
IROWS = IMGS * POS
HALFP = 56
PAIR = 2 * HALFP
PROWS = PAIR * (IMGS // 2)
TILE = 256
UP_TILE = 768


def dot(a, b):
    return jnp.dot(a, b, preferred_element_type=F32)


def dot_t(a, b):
    return lax.dot_general(a, b, (((1,), (1,)), ((), ())), preferred_element_type=F32)


def t_dot(a, b):
    return lax.dot_general(a, b, (((0,), (0,)), ((), ())), preferred_element_type=F32)


def iota(shape, axis):
    return lax.broadcasted_iota(I32, shape, axis)


def normalized(values):
    centred = values - jnp.mean(values, axis=-1, keepdims=True)
    spread = jnp.mean(centred * centred, axis=-1, keepdims=True)
    scale = lax.rsqrt(spread + EPS)
    return centred * scale, scale


def normal_cdf(u):
    return 0.5 + 0.5 * lax.erf(u * 0.7071067811865476)


def image_bias(bias):
    q, k = iota((2 * PAIR, PAIR), 0), iota((2 * PAIR, PAIR), 1)
    q = jnp.where(q >= PAIR, q - PAIR, q)
    place = jnp.where(k >= HALFP, k - HALFP, k)
    bias[...] = jnp.where(((q >= HALFP) == (k >= HALFP)) & (place < POS), 0.0, NEG)


def image_norm_one(tok, gain, stage):
    def rows(i, c):
        s = pl.ds(pl.multiple_of(i * 160, 160), 160)
        n, _ = normalized(tok[s, :].astype(F32))
        n = n * gain
        for h in range(6):
            stage[h, s, :] = n[:, h * 128 : h * 128 + 128]
        return c

    lax.fori_loop(0, 5, rows, 0)
    stage[:, IROWS:, :] = jnp.zeros((6, PROWS - IROWS, 128), F32)


def tiles(n, body):
    def step(i, c):
        body(i, pl.ds(pl.multiple_of(i * TILE, TILE), TILE))
        return c

    lax.fori_loop(0, n, step, 0)


def image_permute(stage, iap):
    def pair(p, c):
        for h in range(6):
            both = [stage[h, pl.ds(2 * p + i, HALFP, stride=IMGS), :] for i in range(2)]
            iap[pl.ds(pl.multiple_of(p * PAIR, PAIR), PAIR), h * 128 : h * 128 + 128] = jnp.concatenate(both, axis=0).astype(BF16)
        return c
    lax.fori_loop(0, IMGS // 2, pair, 0)


def image_qkv(iap, w, iqkv):
    def step(j, c):
        iqkv[j] = dot(iap[...], w[j]).astype(BF16)
        return c
    lax.fori_loop(0, 3, step, 0)


def stacked(values, low):
    zero = jnp.zeros_like(values)
    return jnp.concatenate([jnp.where(low, values, zero), jnp.where(low, zero, values)], axis=0)


def image_attention(iqkv, bias, stage, first, last, unroll=1):
    low = iota((PAIR, 128), 1) < 64

    def pair(p, c):
        rows = pl.ds(pl.multiple_of(p * PAIR, PAIR), PAIR)
        ones = jnp.ones((PAIR, 128), BF16)
        cols = [pl.ds(h * 128, 128) for h in range(6)]
        s = [dot_t(stacked(iqkv[0, rows, h], low), iqkv[1, rows, h]) * 0.125 + bias[...] for h in cols]
        e = [jnp.exp(x - jnp.max(x, axis=-1, keepdims=True)).astype(BF16) for x in s]
        for i, (h, x) in enumerate(zip(cols, e)):
            o = dot(x, jnp.concatenate([iqkv[2, rows, h], ones], axis=1))
            o = jnp.where(low, o[:PAIR, :128], o[PAIR:, :128]) / jnp.where(low, o[:PAIR, 128:], o[PAIR:, 128:])
            stage[i, pl.ds(2 * p, HALFP, stride=IMGS), :] = o[:HALFP]
            stage[i, pl.ds(2 * p + 1, HALFP, stride=IMGS), :] = o[HALFP:]
        return c

    lax.fori_loop(first, last, pair, 0, unroll=unroll)


def image_out(stage, tok, w, iy):
    def rows(i, c):
        s = pl.ds(pl.multiple_of(i * 160, 160), 160)
        iy[s, :] = tok[s, :].astype(F32) + dot(jnp.concatenate([stage[h, s, :].astype(BF16) for h in range(6)], axis=1), w[...])
        return c
    lax.fori_loop(0, 5, rows, 0)


def image_norm_two(iy, gain, ia, ypool):
    ypool[...] = jnp.zeros_like(ypool)
    def rows(i, c):
        s = pl.ds(pl.multiple_of(i * 160, 160), 160)
        y = iy[s, :]
        ypool[...] += jnp.sum(y.reshape(10, IMGS, D), axis=0)
        n, _ = normalized(y)
        ia[s, :] = (n * gain).astype(BF16)
        return c
    lax.fori_loop(0, 5, rows, 0)


def image_up(ia, w, hsum, first, last):
    def step(i, c):
        s = pl.ds(pl.multiple_of(i * UP_TILE, UP_TILE), UP_TILE)
        for m in range(5):
            u = dot(ia[160 * m : 160 * m + 160, :], w[:, s])
            part = jnp.sum((u * normal_cdf(u)).reshape(10, IMGS, UP_TILE), axis=0)
            total = part if m == 0 else total + part
        hsum[:, s] = total
        return c
    lax.fori_loop(first, last, step, 0)


def as_row(gain):
    return gain[...].reshape(1, D)


def column(values):
    rows = iota((OWN_CAPS, 128), 0)
    out = jnp.zeros((OWN_CAPS, 128), I32)
    for i in range(OWN_CAPS):
        out = jnp.where(rows == i, values[i], out)
    return out


def split_rows(x):
    hi = x.astype(BF16)
    return jnp.concatenate([hi, (x - hi.astype(F32)).astype(BF16)], axis=0)


def image_finish(hsum, ypool, w_down, w_proj):
    both = dot(split_rows(hsum[...]), w_down[...])
    pooled = ((ypool[...] + both[:IMGS] + both[IMGS:]) * (1.0 / POS)).astype(BF16)
    e = dot(pooled, w_proj[...])
    return (e * lax.rsqrt(jnp.sum(e * e, axis=-1, keepdims=True) + EPS)).astype(BF16)


GROUP, RANKS, CHIPS = 4, 32, 16
OWN, ROWS = 128, 512
CAPS, OWN_CAPS = 64, 16
PART = OWN // 2
BAND = 192
HALF = 384
MESH = pl.DeviceIdType.MESH
VEC = 1664
PAIRS = 55


class Links:
    def __init__(self):
        self.dp, self.t = lax.axis_index("dp"), lax.axis_index("tensor")
        self.core, self.chip = lax.rem(self.dp, 2), self.dp // 2
        self.place = {"x": lax.rem(self.chip, 4), "z": self.chip // 4}

    def rank(self, k):
        return lax.rem(self.t + k, GROUP)

    def group_peer(self, k):
        return {"dp": self.dp, "tensor": self.rank(k)}

    def chip_of(self, k):
        return lax.rem(self.chip + k, CHIPS)

    def chip_peer(self, k):
        return {"dp": 2 * self.chip_of(k) + self.core, "tensor": self.t}

    def axis_rank(self, axis, k):
        return lax.rem(self.place[axis] + k, 4)

    def axis_peer(self, axis, k):
        place = dict(self.place)
        place[axis] = self.axis_rank(axis, k)
        return {"dp": 2 * (place["z"] * 4 + place["x"]) + self.core, "tensor": self.t}

    def sibling(self):
        return {"dp": self.dp + 1 - 2 * self.core, "tensor": self.t}

    def greet(self):
        barrier = pltpu.get_barrier_semaphore()
        for k in range(1, GROUP):
            pl.semaphore_signal(barrier, 1, device_id=self.group_peer(k), device_id_type=MESH)
        for k in range(1, CHIPS):
            pl.semaphore_signal(barrier, 1, device_id=self.chip_peer(k), device_id_type=MESH)
        pl.semaphore_signal(barrier, 1, device_id=self.sibling(), device_id_type=MESH)

    def met(self):
        pl.semaphore_wait(pltpu.get_barrier_semaphore(), GROUP - 1 + CHIPS)


def send(src, dst, sems, peer):
    pltpu.make_async_remote_copy(src, dst, sems.at[0], sems.at[1], device_id=peer, device_id_type=MESH).start()


def finish(exchange):
    sems, span = exchange
    for i in range(2):
        pltpu.make_async_copy(span, span, sems.at[i]).wait()


def sent(exchange):
    sems, span = exchange
    pltpu.make_async_copy(span, span, sems.at[0]).wait()


def arrived(exchange):
    sems, span = exchange
    pltpu.make_async_copy(span, span, sems.at[1]).wait()


def group_share(links, buf, sems):
    own = buf.at[links.t]
    for k in (1, 3, 2):
        send(own, own, sems, links.group_peer(k))
    return sems, buf.at[pl.ds(0, 3)]


def group_scatter(links, parts, landed, sems):
    for k in (1, 3, 2):
        send(parts.at[links.rank(k)], landed.at[k - 1], sems, links.group_peer(k))
    return sems, landed


def half_rows(h):
    return pl.ds(h * PART, PART)


def share_half(links, buf, sems, h):
    own = buf.at[links.t, half_rows(h)]
    for k in (1, 3, 2):
        send(own, own, sems, links.group_peer(k))
    return sems, buf.at[pl.ds(0, 3), half_rows(h)]


def scatter_half(links, parts, landed, sems, h):
    for k in (1, 3, 2):
        send(parts.at[links.rank(k), half_rows(h)], landed.at[k - 1, half_rows(h)], sems, links.group_peer(k))
    return sems, landed.at[pl.ds(0, 3), half_rows(h)]


def distance(k):
    x, z = k // 2 % 4, k // 8
    return -(min(x, 4 - x) + min(z, 4 - z))


def chip_share(links, buf, sems):
    own = buf.at[links.chip]
    for k in sorted(range(1, CHIPS), key=lambda k: distance(2 * k)):
        send(own, own, sems, links.chip_peer(k))
    return sems, buf.at[pl.ds(0, CHIPS - 1)]


def sibling_send(links, src, dst, sems):
    send(src, dst, sems, links.sibling())
    return sems, src


def text_masks(seg_t, pad_t, bias, mem, mem_t):
    seg, pad = seg_t[...].astype(F32).astype(BF16), pad_t[...].astype(F32).astype(BF16)

    def as_column(values):
        pick = jnp.where(iota((ROWS, 32), 0) >> 4 == iota((ROWS, 32), 1), 1.0, 0.0).astype(BF16)
        wide = dot_t(pick, values)
        return jnp.sum(jnp.where(iota((ROWS, 16), 0) & 15 == iota((ROWS, 16), 1), wide, 0.0), axis=1, keepdims=True)

    def as_row(values):
        pick = jnp.where(iota((32, ROWS), 1) >> 4 == iota((32, ROWS), 0), 1.0, 0.0).astype(BF16)
        wide = dot(values, pick)
        return jnp.sum(jnp.where(iota((16, ROWS), 1) & 15 == iota((16, ROWS), 0), wide, 0.0), axis=0, keepdims=True)

    cap_col = as_column(seg) + ((iota((ROWS, 1), 0) >> 4) * 2).astype(F32)
    key_col = jnp.where(as_column(pad) > 0.5, cap_col, -1.0)
    cap_row = as_row(seg) + ((iota((1, ROWS), 1) >> 4) * 2).astype(F32)
    key_row = jnp.where(as_row(pad) > 0.5, cap_row, -1.0)
    for b in range(4):
        rows = slice(128 * b, 128 * b + 128)
        bias[b] = jnp.where(cap_col[rows] == key_row[:, rows], 0.0, NEG)
    mem[...] = jnp.where(iota((CAPS, ROWS), 0).astype(F32) == key_row, 1.0, 0.0).astype(BF16)
    mem_t[...] = jnp.where((iota((ROWS, 128), 1) & 63).astype(F32) == key_col, 1.0, 0.0).astype(BF16)


def text_norm_one(x, gain, a1, t):
    n, _ = normalized(x[...].astype(F32))
    a1[t] = (n * gain).astype(BF16)


def low_half():
    return iota((OWN, 128), 1) < 64


def text_attention(a1, w_t, bias, w_out, qkv, probs, att, parts):
    rows_all = a1[...].reshape(ROWS, D)
    for j in range(3):
        qkv[j] = dot_t(rows_all, w_t[j]).astype(BF16)
    low = low_half()
    blocks = [slice(128 * b, 128 * b + 128) for b in range(4)]
    scores = []
    for b, rows in enumerate(blocks):
        mask = bias[b]
        scores.append(dot_t(stacked(qkv[0, rows, :128], low), qkv[1, rows, :128]) * 0.125 + jnp.concatenate([mask, mask], axis=0))
        scores.append(dot_t(qkv[0, rows, 128:], qkv[1, rows, 128:]) * 0.125 + mask)
    powers = [jnp.exp(x - jnp.max(x, axis=-1, keepdims=True)) for x in scores]
    shares = [x / jnp.sum(x, axis=-1, keepdims=True) for x in powers]
    for b, rows in enumerate(blocks):
        probs[b, :256] = shares[2 * b]
        probs[b, 256:] = shares[2 * b + 1]
        o = dot(shares[2 * b].astype(BF16), qkv[2, rows, :128])
        att[rows, :128] = jnp.where(low, o[:128], o[128:]).astype(BF16)
        att[rows, 128:] = dot(shares[2 * b + 1].astype(BF16), qkv[2, rows, 128:]).astype(BF16)
    parts[...] = dot(att[...], w_out[...]).astype(BF16).reshape(GROUP, OWN, D)


def summed(parts, landed, t, rows):
    return parts[t, rows].astype(F32) + landed[0, rows].astype(F32) + landed[1, rows].astype(F32) + landed[2, rows].astype(F32)


def split3(x):
    hi = x.astype(BF16)
    rest = x - hi.astype(F32)
    mid = rest.astype(BF16)
    return jnp.concatenate([hi, mid, (rest - mid.astype(F32)).astype(BF16)], axis=0)


def own_member(mem, t):
    return mem[pl.ds(pl.multiple_of(t * OWN_CAPS, OWN_CAPS), OWN_CAPS), pl.ds(pl.multiple_of(t * OWN, OWN), OWN)]


def text_norm_two(h, x, parts, landed, gain, x1, a2, t):
    rows = half_rows(h)
    y = x[rows, :].astype(F32) + summed(parts, landed, t, rows)
    x1[rows, :] = y
    n, _ = normalized(y)
    a2[t, rows] = (n * gain).astype(BF16)


def text_pool_one(x1, mem, x1_pool, t):
    own = own_member(mem, t)
    x1_pool[...] = dot(jnp.concatenate([own, own, own], axis=1), split3(x1[...]))


def text_up(a2, w_up, mem, w_down, x1_pool, dgelu, hidden, hsum, part, parts, t):
    for r in range(GROUP):
        rows = slice(r * OWN, r * OWN + OWN)
        u = dot(a2[r], w_up[...])
        phi = normal_cdf(u)
        dgelu[rows, :] = phi + u * (jnp.exp(u * u * -0.5) * 0.3989422804014327)
        hidden[rows, :] = (u * phi).astype(BF16)
    hsum[...] = dot(mem[...], hidden[...])
    both = dot(split_rows(hsum[...]), w_down[...])
    part[...] = (both[:CAPS] + both[CAPS:]).reshape(GROUP, OWN_CAPS, D)
    part[t] += x1_pool[...]
    parts[t] = part[...].reshape(CAPS, D).astype(BF16)


def counts_of(mem):
    return jnp.sum(mem.astype(F32), axis=1, keepdims=True)


def text_embed(parts, mem, w_proj, pooled, tf, scale):
    total = parts[0].astype(F32) + parts[1].astype(F32) + parts[2].astype(F32) + parts[3].astype(F32)
    rows = (total / counts_of(mem[...])).astype(BF16)
    pooled[...] = rows
    e = dot(rows, w_proj[...])
    rs = lax.rsqrt(jnp.sum(e * e, axis=-1, keepdims=True) + EPS)
    tf[...] = rs * e
    scale[...] = jnp.broadcast_to(rs, (CAPS, 128))


def score_sums(tf, images, s_ref, e_ref, row_sums, col_sums, t):
    s = 40.0 * dot_t(tf[...].astype(BF16), images[...].reshape(ROWS, D))
    s_ref[...] = s
    e = jnp.exp(s - 40.0)
    e_ref[...] = e
    diagonal = iota((CAPS, 128), 0) == iota((CAPS, 128), 1)
    row_sums[t] = jnp.sum(jnp.where(diagonal, jnp.sum(e, axis=1, keepdims=True), 0.0), axis=0, keepdims=True)
    col_sums[0] = jnp.sum(e, axis=0, keepdims=True)


def score_grad(s_ref, e_ref, row_sums, col_sums, pair, images, dts, vec, t):
    diagonal = iota((CAPS, 128), 0) == iota((CAPS, 128), 1)
    rows = jnp.sum(jnp.where(diagonal, row_sums[0] + row_sums[1] + row_sums[2] + row_sums[3], 0.0), axis=1, keepdims=True)
    cols = col_sums[0]
    for i in range(1, CHIPS):
        cols = cols + col_sums[i]
    lane = iota((CAPS, ROWS), 1)
    image = ((lane >> 4) & 15) * (2 * CAPS) + (lane >> 8) * CAPS + (lane & 15) + OWN_CAPS * t
    target = jnp.where(pair[...].reshape(CAPS, 128)[:, :1] == image, 1.0, 0.0)
    g = 0.5 * (e_ref[...] / rows + e_ref[...] / cols) - target
    dts[t] = (40.0 * dot(g.astype(BF16), images[...].reshape(ROWS, D))).astype(BF16)
    loss = (
        jnp.sum(40.0 + jnp.log(rows), axis=0, keepdims=True) * (1.0 / GROUP)
        + jnp.sum(40.0 + jnp.log(cols), axis=1, keepdims=True) * (1.0 / RANKS)
        - 2.0 * jnp.sum(jnp.sum(s_ref[...] * target, axis=1, keepdims=True), axis=0, keepdims=True)
    )
    vec[t, :, 1536:] = jnp.broadcast_to(loss, (1, 128))


def embed_grad(dts, tf, scale, w_proj, mem, de_ref, dz_ref, gp_ref):
    dt = dts[0].astype(F32) + dts[1].astype(F32) + dts[2].astype(F32) + dts[3].astype(F32)
    f = tf[...]
    de = (scale[:, :1] * (dt - f * jnp.sum(f * dt, axis=-1, keepdims=True))).astype(BF16)
    gp = dot_t(de, w_proj[...]) / counts_of(mem[...])
    de_ref[...] = de
    gp_ref[...] = gp
    dz_ref[...] = gp.astype(BF16)


def row_grad(gp_ref, mem, dx2, t):
    own = own_member(mem, t)
    gp = gp_ref[pl.ds(pl.multiple_of(t * OWN_CAPS, OWN_CAPS), OWN_CAPS), :]
    dx2[...] = t_dot(jnp.concatenate([own, own, own], axis=0), split3(gp))


def hidden_grad(dz, w_down):
    return split_rows(dot_t(dz[...], w_down[...]))


def hidden_spread(h, dh, mem_t, dgelu, w_up, du, parts):
    blocks = [pl.ds(r * OWN + h * PART, PART) for r in range(GROUP)]
    member = jnp.concatenate([mem_t[b, :] for b in blocks], axis=0)
    slope = jnp.concatenate([dgelu[b, :] for b in blocks], axis=0)
    rows = (dot(member, dh) * slope).astype(BF16)
    total = dot_t(rows, w_up[...]).astype(BF16)
    for r, b in enumerate(blocks):
        du[b, :] = rows[r * PART : (r + 1) * PART]
        parts[r, half_rows(h)] = total[r * PART : (r + 1) * PART]


def gain_grad(parts, normed, gain):
    total = jnp.zeros((1, D), F32)
    for r in range(GROUP):
        total = total + jnp.sum(parts[r].astype(F32) * normed[r].astype(F32), axis=0, keepdims=True)
    return total / gain


def put_chunks(g, first, values):
    rows = g.shape[-2]
    for c in range(values.shape[0] // rows):
        at = first + c
        place = (at,) if len(g.shape) == 4 else (at // 4, at % 4)
        for j in range(2):
            g[(j, *place)] = values[c * rows : (c + 1) * rows, j * HALF : (j + 1) * HALF].astype(BF16)


def down_proj_grad(hsum, dz, de, pooled, proj, g, h, t):
    hs = split_rows(hsum[...])
    dz2 = jnp.concatenate([dz[...], dz[...]], axis=0)
    put_chunks(g, 0, t_dot(hs[:, :256], dz2))
    put_chunks(g, 8, t_dot(hs[:, 256:512], dz2))
    put_chunks(h, 0, t_dot(hs[:, 512:], dz2))
    proj[...] = t_dot(pooled[...], de[...]).astype(BF16).reshape(GROUP, BAND, D)
    put_chunks(h, 8, proj[t])
    h[:, 3, 2:] = jnp.zeros((2, 2, 32, HALF), BF16)


def up_grad(a2, du, g, h):
    for i in range(3):
        rows = t_dot(a2[:, :, i * 256 : (i + 1) * 256].reshape(ROWS, 256), du[...])
        put_chunks(g if i < 2 else h, 8 * i if i < 2 else 0, rows)


def norm_two_grad(h, parts, landed, x1, gain, dx2, dx1, dy, t):
    rows = half_rows(h)
    da = summed(parts, landed, t, rows)
    n, scale = normalized(x1[rows, :])
    d = da * gain
    g = dx2[rows, :] + (d - jnp.mean(d, axis=-1, keepdims=True) - n * jnp.mean(d * n, axis=-1, keepdims=True)) * scale
    dx1[rows, :] = g
    dy[t, rows] = g.astype(BF16)


def attention_grad(dy, w_out, w_t, qkv, probs, dqkv, parts):
    datt = dot_t(dy[...].reshape(ROWS, D), w_out[...]).astype(BF16)
    low = low_half()
    blocks = [slice(128 * b, 128 * b + 128) for b in range(4)]
    sides, raw = [], []
    for b, rows in enumerate(blocks):
        sides.append((stacked(qkv[0, rows, :128], low), stacked(datt[rows, :128], low)))
        sides.append((qkv[0, rows, 128:], datt[rows, 128:]))
        raw.append(dot_t(sides[-2][1], qkv[2, rows, :128]))
        raw.append(dot_t(sides[-1][1], qkv[2, rows, 128:]))
    probs_of = [probs[b, part] for b in range(4) for part in (slice(0, 256), slice(256, 384))]
    ds = [(p * (x - jnp.sum(p * x, axis=-1, keepdims=True))).astype(BF16) for p, x in zip(probs_of, raw)]
    for b, rows in enumerate(blocks):
        for i, cols in ((2 * b, slice(0, 128)), (2 * b + 1, slice(128, BAND))):
            o = dot(ds[i], qkv[1, rows, cols])
            if i % 2 == 0:
                o = jnp.where(low, o[:128], o[128:])
            dqkv[0, rows, cols] = (o * 0.125).astype(BF16)
            dqkv[1, rows, cols] = (t_dot(ds[i], sides[i][0]) * 0.125).astype(BF16)
            dqkv[2, rows, cols] = t_dot(probs_of[i].astype(BF16), sides[i][1]).astype(BF16)
    total = dot(dqkv[0], w_t[0]) + dot(dqkv[1], w_t[1]) + dot(dqkv[2], w_t[2])
    parts[...] = total.astype(BF16).reshape(GROUP, OWN, D)


def out_grad(att, dy, g):
    put_chunks(g, 0, t_dot(att[...], dy[...].reshape(ROWS, D)))


def qkv_grad(dqkv, a1, g, h):
    rows = a1[...].reshape(ROWS, D)
    put_chunks(g, 6, t_dot(dqkv[0], rows))
    keys = t_dot(dqkv[1], rows)
    put_chunks(g, 12, keys[:128])
    put_chunks(h, 0, keys[128:])
    put_chunks(h, 4, t_dot(dqkv[2], rows))


def norm_one_grad(parts, landed, x, gain, dx1, out, t):
    da = summed(parts, landed, t, slice(0, OWN))
    n, scale = normalized(x[...].astype(F32))
    h = da * gain
    out[...] = dx1[...] + (h - jnp.mean(h, axis=-1, keepdims=True) - n * jnp.mean(h * n, axis=-1, keepdims=True)) * scale


class Reduction:
    def __init__(self, links, g, met, landed, full, pair):
        self.links, self.g, self.met, self.landed, self.full, self.pair = links, g, met, landed, full, pair

    def cores(self):
        self.open = sibling_send(self.links, self.g.at[1 - self.links.core], self.met, self.pair())

    def both_cores(self):
        finish(self.open)
        self.met[...] = (self.g[self.links.core].astype(F32) + self.met[...].astype(F32)).astype(BF16)

    def scatter(self):
        self.both_cores()
        sems = self.pair()
        for k in range(1, CHIPS):
            send(self.met.at[self.links.chip_of(k)], self.landed.at[k - 1], sems, self.links.chip_peer(k))
        self.open = sems, self.landed

    def gather(self):
        finish(self.open)
        total = self.met[self.links.chip].astype(F32)
        for k in range(CHIPS - 1):
            total = total + self.landed[k].astype(F32)
        half = self.full.at[self.links.core]
        half[self.links.chip] = total.astype(BF16)
        self.open = chip_share(self.links, half, self.pair())

    def share(self):
        finish(self.open)
        half = self.full.at[self.links.core]
        self.open = sibling_send(self.links, half, half, self.pair())

    def done(self):
        finish(self.open)


class TwoAxes(Reduction):
    def __init__(self, links, g, met, landed, near, full, pair, first, second):
        super().__init__(links, g, met, landed, full, pair)
        self.near, self.first, self.second = near, first, second
        self.i, self.j = links.place[first], links.place[second]

    def spread(self, axis, source, target):
        sems = self.pair()
        for k in (1, 3, 2):
            send(source(k), target(k), sems, self.links.axis_peer(axis, k))
        return sems

    def scatter(self):
        self.both_cores()
        sems = self.spread(
            self.first, lambda k: self.met.at[self.links.axis_rank(self.first, k)], lambda k: self.landed.at[k - 1]
        )
        self.open = sems, self.landed

    def scatter_second(self):
        finish(self.open)
        total = self.met[self.i].astype(F32)
        for k in range(3):
            total = total + self.landed[k].astype(F32)
        self.met[self.i] = total.astype(BF16)
        sems = self.spread(
            self.second, lambda k: self.met.at[self.i, self.links.axis_rank(self.second, k)], lambda k: self.near.at[k - 1]
        )
        self.open = sems, self.near

    def gather(self):
        finish(self.open)
        total = self.met[self.i, self.j].astype(F32)
        for k in range(3):
            total = total + self.near[k].astype(F32)
        core = self.links.core
        self.full[core, self.i, self.j] = total.astype(BF16)
        own = self.full.at[core, self.i, self.j]
        self.open = self.spread(self.second, lambda k: own, lambda k: own), self.full.at[0, 0, pl.ds(0, 3)]

    def gather_second(self):
        finish(self.open)
        own = self.full.at[self.links.core, self.i]
        self.open = self.spread(self.first, lambda k: own, lambda k: own), self.full.at[0, pl.ds(0, 3)]


def body(
    x, seg_t, pad_t, pair_in, gain_one, gain_two, img_gain_one, img_gain_two,
    h_tok, h_iqkv, h_iout, h_iup, h_idown, h_iproj, h_qkv, h_out, h_up, h_down, h_proj,
    o_loss, o_input, o_norms, f_a0, f_a1, f_b0, f_b1, f_c0, f_c1, proj_all,
    tok, iw_qkv, iw_out, iw_up, iw_down, iw_proj, w_qkv, w_out, w_up, w_down, w_proj, load,
    ibias, iap, iqkv, stage, iy, ypool, ihsum, images,
    bias, mem, mem_t, pair, a1, qkv, probs, att, p_att, l_att, x1, x1_pool, a2, dgelu, hsum, p_pool, pools,
    tf, scale, pooled, s_ref, e_ref, row_sums, core_sums, col_sums, dts, de, dz, gp, dx2, du, p_da2, l_da2, dx1, dy,
    dqkv, p_da1, l_da1, proj, vec, vec_core, vec_all,
    *work,
):
    g_a, g_b, g_c, m_a, m_b, m_c, r_a, r_b, r_c, n_a, n_b = (work[i : i + 2] for i in range(0, 22, 2))
    f_a, f_b, f_c = (f_a0, f_a1), (f_b0, f_b1), (f_c0, f_c1)
    sems = work[22]
    links = Links()
    t, dp, core, chip = links.t, links.dp, links.core, links.chip
    loads = {}
    count = iter(range(PAIRS))

    def pair_of():
        return sems.at[next(count)]


    def fetch(at, name, src, dst):
        loads[name] = pltpu.make_async_copy(src, dst, load.at[at])
        loads[name].start()

    fetch(0, "tok", h_tok, tok)
    fetch(1, "iqkv", h_iqkv, iw_qkv)
    links.greet()
    text_norm_one(x, as_row(gain_one), a1, t)
    pair[t] = column(pair_in)
    links.met()
    copies = group_share(links, a1, pair_of())
    pair_copies = group_share(links, pair, pair_of())
    fetch(2, "qkv", h_qkv, w_qkv)
    fetch(3, "out", h_out, w_out)
    fetch(4, "iout", h_iout, iw_out)

    text_masks(seg_t, pad_t, bias, mem, mem_t)
    image_bias(ibias)
    loads["tok"].wait()
    image_norm_one(tok, as_row(img_gain_one), stage)
    fetch(5, "iup", h_iup, iw_up)
    fetch(6, "up", h_up, w_up)
    fetch(7, "down", h_down, w_down)
    fetch(8, "idown", h_idown, iw_down)
    fetch(9, "iproj", h_iproj, iw_proj)
    fetch(10, "proj", h_proj, w_proj)
    image_permute(stage, iap)
    loads["iqkv"].wait()
    image_qkv(iap, iw_qkv, iqkv)

    finish(copies)
    loads["qkv"].wait()
    loads["out"].wait()
    text_attention(a1, w_qkv, bias, w_out, qkv, probs, att, p_att)
    copies = [scatter_half(links, p_att, l_att, pair_of(), 0)]

    image_attention(iqkv, ibias, stage, 0, 4)
    copies.append(scatter_half(links, p_att, l_att, pair_of(), 1))
    image_attention(iqkv, ibias, stage, 4, 8)
    finish(copies[0])
    text_norm_two(0, x, p_att, l_att, as_row(gain_two), x1, a2, t)
    copies[0] = share_half(links, a2, pair_of(), 0)
    loads["iout"].wait()
    image_out(stage, tok, iw_out, iy)
    finish(copies[1])
    text_norm_two(1, x, p_att, l_att, as_row(gain_two), x1, a2, t)
    copies[1] = share_half(links, a2, pair_of(), 1)
    image_norm_two(iy, as_row(img_gain_two), iap.at[:IROWS], ypool)

    loads["iup"].wait()
    image_up(iap.at[:IROWS], iw_up, ihsum, 0, 1)
    text_pool_one(x1, mem, x1_pool, t)

    image_up(iap.at[:IROWS], iw_up, ihsum, 1, FF // UP_TILE)
    loads["idown"].wait()
    loads["iproj"].wait()
    images[core, chip] = image_finish(ihsum, ypool, iw_down, iw_proj)
    image_copies = chip_share(links, images.at[core], pair_of())

    finish(copies[0])
    finish(copies[1])
    loads["up"].wait()
    loads["down"].wait()
    text_up(a2, w_up, mem, w_down, x1_pool, dgelu, du, hsum, p_pool, pools, t)
    copies = group_share(links, pools, pair_of())
    finish(image_copies)
    image_copies = sibling_send(links, images.at[core], images.at[core], pair_of())
    finish(pair_copies)
    loads["proj"].wait()
    finish(copies)
    text_embed(pools, mem, w_proj, pooled, tf, scale)
    finish(image_copies)

    score_sums(tf, images, s_ref, e_ref, row_sums, core_sums, t)
    row_copies = group_share(links, row_sums, pair_of())
    finish(sibling_send(links, core_sums.at[0], core_sums.at[1], pair_of()))
    col_sums[chip] = core_sums[0] + core_sums[1]
    col_copies = chip_share(links, col_sums, pair_of())
    finish(col_copies)
    finish(row_copies)
    score_grad(s_ref, e_ref, row_sums, col_sums, pair, images, dts, vec, t)
    finish(group_share(links, dts, pair_of()))
    embed_grad(dts, tf, scale, w_proj, mem, de, dz, gp)

    red_a = [TwoAxes(links, g_a[i], m_a[i], r_a[i], n_a[i], f_a[i], pair_of, "x", "z") for i in range(2)]
    red_b = [TwoAxes(links, g_b[i], m_b[i], r_b[i], n_b[i], f_b[i], pair_of, "z", "x") for i in range(2)]
    red_c = [Reduction(links, g_c[i], m_c[i], r_c[i], f_c[i], pair_of) for i in range(2)]

    def each(*steps):
        for step in steps:
            step()

    dh = hidden_grad(dz, w_down)
    hidden_spread(0, dh, mem_t, dgelu, w_up, du, p_da2)
    copies = [scatter_half(links, p_da2, l_da2, pair_of(), 0)]
    down_proj_grad(hsum, dz, de, pooled, proj, g_a[0], g_a[1], t)
    each(red_a[0].cores, red_a[1].cores)
    hidden_spread(1, dh, mem_t, dgelu, w_up, du, p_da2)
    up_grad(a2, du, g_b[0], g_b[1])
    each(red_b[0].cores, red_b[1].cores, red_a[0].scatter, red_a[1].scatter)
    row_grad(gp, mem, dx2, t)
    sent(copies[0])
    copies.append(scatter_half(links, p_da2, l_da2, pair_of(), 1))
    each(red_b[0].scatter, red_b[1].scatter)
    vec[t, :, 768:1536] = gain_grad(p_da2, a2, as_row(gain_two))
    arrived(copies[0])
    norm_two_grad(0, p_da2, l_da2, x1, as_row(gain_two), dx2, dx1, dy, t)
    copies[0] = share_half(links, dy, pair_of(), 0)
    finish(copies[1])
    norm_two_grad(1, p_da2, l_da2, x1, as_row(gain_two), dx2, dx1, dy, t)
    copies[1] = share_half(links, dy, pair_of(), 1)
    each(red_a[0].scatter_second, red_b[0].scatter_second)
    each(red_a[1].scatter_second, red_b[1].scatter_second)
    each(red_a[0].gather, red_b[0].gather)
    each(red_a[1].gather, red_b[1].gather)
    each(red_a[0].gather_second, red_b[0].gather_second)
    finish(copies[0])
    finish(copies[1])
    out_grad(att, dy, g_c[0])
    attention_grad(dy, w_out, w_qkv, qkv, probs, dqkv, p_da1)
    each(red_a[1].gather_second, red_b[1].gather_second)
    qkv_grad(dqkv, a1, g_c[0], g_c[1])
    each(red_c[0].cores, red_c[1].cores)
    vec[t, :, :768] = gain_grad(p_da1, a1, as_row(gain_one))
    vec_copies = group_share(links, vec, pair_of())
    copies = group_scatter(links, p_da1, l_da1, pair_of())
    each(red_c[0].scatter, red_c[1].scatter)
    finish(vec_copies)
    vec_core[0] = vec[0] + vec[1] + vec[2] + vec[3]
    finish(sibling_send(links, vec_core.at[0], vec_core.at[1], pair_of()))
    vec_all[chip] = vec_core[0] + vec_core[1]
    vec_copies = chip_share(links, vec_all, pair_of())
    each(red_a[1].share, red_a[0].share, red_b[0].share, red_b[1].share)
    proj_all[core, t, :4] = f_a1[core, 2]
    proj_all[core, t, 4:] = f_a1[core, 3, :2]
    proj_copies = group_share(links, proj_all.at[core], pair_of())
    finish(copies)
    norm_one_grad(p_da1, l_da1, x, as_row(gain_one), dx1, o_input, t)
    each(red_c[0].gather, red_c[1].gather)
    finish(proj_copies)
    proj_copies = sibling_send(links, proj_all.at[core], proj_all.at[core], pair_of())
    each(red_a[0].done, red_a[1].done, red_b[0].done, red_b[1].done)
    finish(vec_copies)
    total = vec_all[0]
    for i in range(1, CHIPS):
        total = total + vec_all[i]
    o_norms[...] = total[:, :1536]
    o_loss[...] = total[:, 1536:] * (1.0 / 4096.0)
    finish(proj_copies)
    each(red_c[0].share, red_c[1].share, red_c[0].done, red_c[1].done)


def widen(
    loss, norms, grad, a0, a1, b0, b1, c0, c1, full_proj,
    o_loss, o_input, o_one, o_two, o_down, o_up, o_out, o_qkv, o_proj, down, up, out, qkv, proj, stored,
):
    stores = []

    def write(buf, target):
        stores.append(pltpu.make_async_copy(buf, target, stored.at[len(stores)]))
        stores[-1].start()

    def halves(target, first, parts, rows):
        for j in range(2):
            target[first : first + rows, j * HALF : (j + 1) * HALF] = parts[j].reshape(rows, HALF).astype(F32)

    write(grad, o_input)
    halves(down, 0, a0, 512)
    halves(down, 512, a1[:, :2], 256)
    write(down, o_down)
    halves(up, 0, b0, 512)
    halves(up, 512, b1, 256)
    write(up, o_up)
    halves(proj, 0, full_proj, D)
    write(proj, o_proj)
    halves(out, 0, c0[:, :6], BAND)
    write(out, o_out)
    halves(qkv, 0, c0[:, 6:], 320)
    halves(qkv, 320, c1, 256)
    write(qkv, o_qkv)
    o_loss[0, 0] = loss[0, 0]
    o_one[...] = norms[:, :D].reshape(D)
    o_two[...] = norms[:, D:].reshape(D)
    for copy in stores:
        copy.wait()


def on_device(
    text_input, segment_ids, pad_mask, pairing, ln_first, w_qkv, w_out, ln_second, w_up, w_down, text_proj,
    image_tokens, img_ln_first, img_w_qkv, img_w_out, img_ln_second, img_w_up, img_w_down, img_proj,
):
    vmem = pl.BlockSpec(memory_space=VM)
    hbm = pl.BlockSpec(memory_space=pl.ANY)
    shape = jax.ShapeDtypeStruct
    sums = ((4, 4, 32, HALF),) * 2 + ((4, 4, 32, HALF), (4, 4, 16, HALF)) + ((16, 32, HALF), (16, 16, HALF))
    dma = pltpu.SemaphoreType.DMA
    scratch = [
        VM((IROWS, D), BF16), VM((3, D, D), BF16), VM((D, D), BF16), VM((D, FF), BF16), VM((FF, D), BF16), VM((D, D), BF16),
        VM((3, BAND, D), BF16), VM((BAND, D), BF16), VM((D, HID), BF16), VM((HID, D), BF16), VM((D, D), BF16), dma((11,)),
        VM((2 * PAIR, PAIR), F32), VM((PROWS, D), BF16), VM((3, PROWS, D), BF16), VM((6, PROWS, 128), F32), VM((IROWS, D), F32),
        VM((IMGS, D), F32), VM((IMGS, FF), F32), VM((2, CHIPS, IMGS, D), BF16),
        VM((4, 128, 128), F32), VM((CAPS, ROWS), BF16), VM((ROWS, 128), BF16), VM((GROUP, OWN_CAPS, 128), I32),
        VM((GROUP, OWN, D), BF16), VM((3, ROWS, BAND), BF16), VM((4, HALF, 128), F32), VM((ROWS, BAND), BF16),
        VM((GROUP, OWN, D), BF16), VM((3, OWN, D), BF16), VM((OWN, D), F32), VM((OWN_CAPS, D), F32), VM((GROUP, OWN, D), BF16),
        VM((ROWS, HID), F32), VM((CAPS, HID), F32), VM((GROUP, OWN_CAPS, D), F32), VM((GROUP, CAPS, D), BF16),
        VM((CAPS, D), F32), VM((CAPS, 128), F32), VM((CAPS, D), BF16), VM((CAPS, ROWS), F32),
        VM((CAPS, ROWS), F32), VM((GROUP, 1, 128), F32), VM((2, 1, ROWS), F32), VM((CHIPS, 1, ROWS), F32), VM((GROUP, CAPS, D), BF16),
        VM((CAPS, D), BF16), VM((CAPS, D), BF16), VM((CAPS, D), F32),
        VM((OWN, D), F32), VM((ROWS, HID), BF16), VM((GROUP, OWN, D), BF16), VM((3, OWN, D), BF16), VM((OWN, D), F32),
        VM((GROUP, OWN, D), BF16), VM((3, ROWS, BAND), BF16), VM((GROUP, OWN, D), BF16), VM((3, OWN, D), BF16),
        VM((GROUP, BAND, D), BF16), VM((GROUP, 1, VEC), F32), VM((2, 1, VEC), F32), VM((CHIPS, 1, VEC), F32),
    ]
    scratch += [VM((2,) + s, BF16) for s in sums] + [VM(s, BF16) for s in sums]
    scratch += [VM((3,) + s[1:], BF16) for s in sums[:4]] + [VM((15,) + s[1:], BF16) for s in sums[4:]]
    scratch += [VM((3,) + s[2:], BF16) for s in sums[:4]] + [dma((PAIRS, 2))]
    loss, input_grad, norms, *full = pl.pallas_call(
        body,
        out_shape=(
            VM((1, 128), F32), VM((OWN, D), F32), VM((1, 1536), F32),
            *(VM((2,) + s, BF16) for s in sums), VM((2, GROUP, 6, 32, HALF), BF16),
        ),
        in_specs=[vmem] * 3 + [pl.BlockSpec(memory_space=pltpu.SMEM)] + [vmem] * 4 + [hbm] * 11,
        out_specs=(vmem,) * 10,
        scratch_shapes=scratch,
        compiler_params=pltpu.CompilerParams(collective_id=0, has_side_effects=True, vmem_limit_bytes=57 << 20),
        name="lit",
    )(
        text_input, segment_ids.T, pad_mask.T, pairing, ln_first, ln_second, img_ln_first, img_ln_second,
        image_tokens.transpose(1, 0, 2).reshape(IROWS, D), img_w_qkv, img_w_out, img_w_up, img_w_down, img_proj,
        w_qkv.swapaxes(1, 2), w_out, w_up, w_down, text_proj,
    )

    loss, input_grad, one, two, down, up, out, qkv, proj = pl.pallas_call(
        widen,
        out_shape=(
            shape((1, 1), F32), shape((OWN, D), F32), shape((D,), F32), shape((D,), F32), shape((HID, D), F32),
            shape((D, HID), F32), shape((BAND, D), F32), shape((3 * BAND, D), F32), shape((D, D), F32),
        ),
        in_specs=[vmem] * 10,
        out_specs=(pl.BlockSpec(memory_space=pltpu.SMEM), hbm, vmem, vmem, hbm, hbm, hbm, hbm, hbm),
        scratch_shapes=[
            VM((HID, D), F32), VM((D, HID), F32), VM((BAND, D), F32), VM((3 * BAND, D), F32), VM((D, D), F32),
            dma((6,)),
        ],
        compiler_params=pltpu.CompilerParams(vmem_limit_bytes=40 << 20),
        name="widen",
    )(loss, norms, input_grad, *full)
    return (loss.reshape(()), input_grad, one, qkv.reshape(3, BAND, D).swapaxes(1, 2), out, two, up, down, proj)


def solution(mesh):
    rows = P(("dp", "tensor"))
    in_specs = (
        P(("dp", "tensor"), None), P("dp", None), P("dp", None), rows, P(), P(None, None, "tensor"), P("tensor", None), P(),
        P(None, "tensor"), P("tensor", None), P(), P(("dp", "tensor"), None, None), P(), P(), P(), P(), P(), P(), P(),
    )
    out_specs = (
        P(), P(("dp", "tensor"), None), P(), P(None, None, "tensor"), P("tensor", None), P(), P(None, "tensor"),
        P("tensor", None), P(),
    )
    return jax.shard_map(on_device, mesh=mesh, in_specs=in_specs, out_specs=out_specs, check_vma=False)
```

```python
import jax, jax.numpy as jnp
from jax import lax
from jax.experimental import pallas as pl
from jax.experimental.pallas import tpu as pltpu
from jax.sharding import PartitionSpec as P

F32, BF16, I32 = jnp.float32, jnp.bfloat16, jnp.int32
VM = pltpu.VMEM
EPS = 1e-6
NEG = -1e30
D, FF, HID = 768, 3072, 768
IMGS, POS = 16, 50
IROWS = IMGS * POS
HALFP = 56
PAIR = 2 * HALFP
PROWS = PAIR * (IMGS // 2)
TILE = 256
UP_TILE = 768


def dot(a, b):
    return jnp.dot(a, b, preferred_element_type=F32)


def dot_t(a, b):
    return lax.dot_general(a, b, (((1,), (1,)), ((), ())), preferred_element_type=F32)


def t_dot(a, b):
    return lax.dot_general(a, b, (((0,), (0,)), ((), ())), preferred_element_type=F32)


def iota(shape, axis):
    return lax.broadcasted_iota(I32, shape, axis)


def normalized(values):
    centred = values - jnp.mean(values, axis=-1, keepdims=True)
    spread = jnp.mean(centred * centred, axis=-1, keepdims=True)
    scale = lax.rsqrt(spread + EPS)
    return centred * scale, scale


def normal_cdf(u):
    return 0.5 + 0.5 * lax.erf(u * 0.7071067811865476)


def image_bias(bias):
    q, k = iota((2 * PAIR, PAIR), 0), iota((2 * PAIR, PAIR), 1)
    q = jnp.where(q >= PAIR, q - PAIR, q)
    place = jnp.where(k >= HALFP, k - HALFP, k)
    bias[...] = jnp.where(((q >= HALFP) == (k >= HALFP)) & (place < POS), 0.0, NEG)


def image_norm_one(tok, gain, stage):
    def rows(i, c):
        s = pl.ds(pl.multiple_of(i * 160, 160), 160)
        n, _ = normalized(tok[s, :].astype(F32))
        n = n * gain
        for h in range(6):
            stage[h, s, :] = n[:, h * 128 : h * 128 + 128]
        return c

    lax.fori_loop(0, 5, rows, 0)
    stage[:, IROWS:, :] = jnp.zeros((6, PROWS - IROWS, 128), F32)


def tiles(n, body):
    def step(i, c):
        body(i, pl.ds(pl.multiple_of(i * TILE, TILE), TILE))
        return c

    lax.fori_loop(0, n, step, 0)


def image_permute(stage, iap):
    def pair(p, c):
        for h in range(6):
            both = [stage[h, pl.ds(2 * p + i, HALFP, stride=IMGS), :] for i in range(2)]
            iap[pl.ds(pl.multiple_of(p * PAIR, PAIR), PAIR), h * 128 : h * 128 + 128] = jnp.concatenate(both, axis=0).astype(BF16)
        return c
    lax.fori_loop(0, IMGS // 2, pair, 0)


def image_qkv(iap, w, iqkv):
    def step(j, c):
        iqkv[j] = dot(iap[...], w[j]).astype(BF16)
        return c
    lax.fori_loop(0, 3, step, 0)


def stacked(values, low):
    zero = jnp.zeros_like(values)
    return jnp.concatenate([jnp.where(low, values, zero), jnp.where(low, zero, values)], axis=0)


def image_attention(iqkv, bias, stage, first, last, unroll=1):
    low = iota((PAIR, 128), 1) < 64

    def pair(p, c):
        rows = pl.ds(pl.multiple_of(p * PAIR, PAIR), PAIR)
        ones = jnp.ones((PAIR, 128), BF16)
        cols = [pl.ds(h * 128, 128) for h in range(6)]
        s = [dot_t(stacked(iqkv[0, rows, h], low), iqkv[1, rows, h]) * 0.125 + bias[...] for h in cols]
        e = [jnp.exp(x - jnp.max(x, axis=-1, keepdims=True)).astype(BF16) for x in s]
        for i, (h, x) in enumerate(zip(cols, e)):
            o = dot(x, jnp.concatenate([iqkv[2, rows, h], ones], axis=1))
            o = jnp.where(low, o[:PAIR, :128], o[PAIR:, :128]) / jnp.where(low, o[:PAIR, 128:], o[PAIR:, 128:])
            stage[i, pl.ds(2 * p, HALFP, stride=IMGS), :] = o[:HALFP]
            stage[i, pl.ds(2 * p + 1, HALFP, stride=IMGS), :] = o[HALFP:]
        return c

    lax.fori_loop(first, last, pair, 0, unroll=unroll)


def image_out(stage, tok, w, iy):
    def rows(i, c):
        s = pl.ds(pl.multiple_of(i * 160, 160), 160)
        iy[s, :] = tok[s, :].astype(F32) + dot(jnp.concatenate([stage[h, s, :].astype(BF16) for h in range(6)], axis=1), w[...])
        return c
    lax.fori_loop(0, 5, rows, 0)


def image_norm_two(iy, gain, ia, ypool):
    ypool[...] = jnp.zeros_like(ypool)
    def rows(i, c):
        s = pl.ds(pl.multiple_of(i * 160, 160), 160)
        y = iy[s, :]
        ypool[...] += jnp.sum(y.reshape(10, IMGS, D), axis=0)
        n, _ = normalized(y)
        ia[s, :] = (n * gain).astype(BF16)
        return c
    lax.fori_loop(0, 5, rows, 0)


def image_up(ia, w, hsum, first, last):
    def step(i, c):
        s = pl.ds(pl.multiple_of(i * UP_TILE, UP_TILE), UP_TILE)
        for m in range(5):
            u = dot(ia[160 * m : 160 * m + 160, :], w[:, s])
            part = jnp.sum((u * normal_cdf(u)).reshape(10, IMGS, UP_TILE), axis=0)
            total = part if m == 0 else total + part
        hsum[:, s] = total
        return c
    lax.fori_loop(first, last, step, 0)


def as_row(gain):
    return gain[...].reshape(1, D)


def column(values):
    rows = iota((OWN_CAPS, 128), 0)
    out = jnp.zeros((OWN_CAPS, 128), I32)
    for i in range(OWN_CAPS):
        out = jnp.where(rows == i, values[i], out)
    return out


def split_rows(x):
    hi = x.astype(BF16)
    return jnp.concatenate([hi, (x - hi.astype(F32)).astype(BF16)], axis=0)


def image_finish(hsum, ypool, w_down, w_proj):
    both = dot(split_rows(hsum[...]), w_down[...])
    pooled = ((ypool[...] + both[:IMGS] + both[IMGS:]) * (1.0 / POS)).astype(BF16)
    e = dot(pooled, w_proj[...])
    return (e * lax.rsqrt(jnp.sum(e * e, axis=-1, keepdims=True) + EPS)).astype(BF16)


GROUP, RANKS, CHIPS = 4, 32, 16
OWN, ROWS = 128, 512
CAPS, OWN_CAPS = 64, 16
PART = OWN // 2
BAND = 192
HALF = 384
MESH = pl.DeviceIdType.MESH
VEC = 1664
PAIRS = 55


class Links:
    def __init__(self):
        self.dp, self.t = lax.axis_index("dp"), lax.axis_index("tensor")
        self.core, self.chip = lax.rem(self.dp, 2), self.dp // 2
        self.place = {"x": lax.rem(self.chip, 4), "z": self.chip // 4}

    def rank(self, k):
        return lax.rem(self.t + k, GROUP)

    def group_peer(self, k):
        return {"dp": self.dp, "tensor": self.rank(k)}

    def chip_of(self, k):
        return lax.rem(self.chip + k, CHIPS)

    def chip_peer(self, k):
        return {"dp": 2 * self.chip_of(k) + self.core, "tensor": self.t}

    def axis_rank(self, axis, k):
        return lax.rem(self.place[axis] + k, 4)

    def axis_peer(self, axis, k):
        place = dict(self.place)
        place[axis] = self.axis_rank(axis, k)
        return {"dp": 2 * (place["z"] * 4 + place["x"]) + self.core, "tensor": self.t}

    def sibling(self):
        return {"dp": self.dp + 1 - 2 * self.core, "tensor": self.t}

    def greet(self):
        barrier = pltpu.get_barrier_semaphore()
        for k in range(1, GROUP):
            pl.semaphore_signal(barrier, 1, device_id=self.group_peer(k), device_id_type=MESH)
        for k in range(1, CHIPS):
            pl.semaphore_signal(barrier, 1, device_id=self.chip_peer(k), device_id_type=MESH)
        pl.semaphore_signal(barrier, 1, device_id=self.sibling(), device_id_type=MESH)

    def met(self):
        pl.semaphore_wait(pltpu.get_barrier_semaphore(), GROUP - 1 + CHIPS)


def send(src, dst, sems, peer):
    pltpu.make_async_remote_copy(src, dst, sems.at[0], sems.at[1], device_id=peer, device_id_type=MESH).start()


def finish(exchange):
    sems, span = exchange
    for i in range(2):
        pltpu.make_async_copy(span, span, sems.at[i]).wait()


def sent(exchange):
    sems, span = exchange
    pltpu.make_async_copy(span, span, sems.at[0]).wait()


def arrived(exchange):
    sems, span = exchange
    pltpu.make_async_copy(span, span, sems.at[1]).wait()


def group_share(links, buf, sems):
    own = buf.at[links.t]
    for k in (1, 3, 2):
        send(own, own, sems, links.group_peer(k))
    return sems, buf.at[pl.ds(0, 3)]


def group_scatter(links, parts, landed, sems):
    for k in (1, 3, 2):
        send(parts.at[links.rank(k)], landed.at[k - 1], sems, links.group_peer(k))
    return sems, landed


def half_rows(h):
    return pl.ds(h * PART, PART)


def share_half(links, buf, sems, h):
    own = buf.at[links.t, half_rows(h)]
    for k in (1, 3, 2):
        send(own, own, sems, links.group_peer(k))
    return sems, buf.at[pl.ds(0, 3), half_rows(h)]


def scatter_half(links, parts, landed, sems, h):
    for k in (1, 3, 2):
        send(parts.at[links.rank(k), half_rows(h)], landed.at[k - 1, half_rows(h)], sems, links.group_peer(k))
    return sems, landed.at[pl.ds(0, 3), half_rows(h)]


def distance(k):
    x, z = k // 2 % 4, k // 8
    return -(min(x, 4 - x) + min(z, 4 - z))


def chip_share(links, buf, sems):
    own = buf.at[links.chip]
    for k in sorted(range(1, CHIPS), key=lambda k: distance(2 * k)):
        send(own, own, sems, links.chip_peer(k))
    return sems, buf.at[pl.ds(0, CHIPS - 1)]


def sibling_send(links, src, dst, sems):
    send(src, dst, sems, links.sibling())
    return sems, src


def text_masks(seg_t, pad_t, bias, mem, mem_t):
    seg, pad = seg_t[...].astype(F32).astype(BF16), pad_t[...].astype(F32).astype(BF16)

    def as_column(values):
        pick = jnp.where(iota((ROWS, 32), 0) >> 4 == iota((ROWS, 32), 1), 1.0, 0.0).astype(BF16)
        wide = dot_t(pick, values)
        return jnp.sum(jnp.where(iota((ROWS, 16), 0) & 15 == iota((ROWS, 16), 1), wide, 0.0), axis=1, keepdims=True)

    def as_row(values):
        pick = jnp.where(iota((32, ROWS), 1) >> 4 == iota((32, ROWS), 0), 1.0, 0.0).astype(BF16)
        wide = dot(values, pick)
        return jnp.sum(jnp.where(iota((16, ROWS), 1) & 15 == iota((16, ROWS), 0), wide, 0.0), axis=0, keepdims=True)

    cap_col = as_column(seg) + ((iota((ROWS, 1), 0) >> 4) * 2).astype(F32)
    key_col = jnp.where(as_column(pad) > 0.5, cap_col, -1.0)
    cap_row = as_row(seg) + ((iota((1, ROWS), 1) >> 4) * 2).astype(F32)
    key_row = jnp.where(as_row(pad) > 0.5, cap_row, -1.0)
    for b in range(4):
        rows = slice(128 * b, 128 * b + 128)
        bias[b] = jnp.where(cap_col[rows] == key_row[:, rows], 0.0, NEG)
    mem[...] = jnp.where(iota((CAPS, ROWS), 0).astype(F32) == key_row, 1.0, 0.0).astype(BF16)
    mem_t[...] = jnp.where((iota((ROWS, 128), 1) & 63).astype(F32) == key_col, 1.0, 0.0).astype(BF16)


def text_norm_one(x, gain, a1, t):
    n, _ = normalized(x[...].astype(F32))
    a1[t] = (n * gain).astype(BF16)


def low_half():
    return iota((OWN, 128), 1) < 64


def text_attention(a1, w_t, bias, w_out, qkv, probs, att, parts):
    rows_all = a1[...].reshape(ROWS, D)
    for j in range(3):
        qkv[j] = dot_t(rows_all, w_t[j]).astype(BF16)
    low = low_half()
    blocks = [slice(128 * b, 128 * b + 128) for b in range(4)]
    scores = []
    for b, rows in enumerate(blocks):
        mask = bias[b]
        scores.append(dot_t(stacked(qkv[0, rows, :128], low), qkv[1, rows, :128]) * 0.125 + jnp.concatenate([mask, mask], axis=0))
        scores.append(dot_t(qkv[0, rows, 128:], qkv[1, rows, 128:]) * 0.125 + mask)
    powers = [jnp.exp(x - jnp.max(x, axis=-1, keepdims=True)) for x in scores]
    shares = [x / jnp.sum(x, axis=-1, keepdims=True) for x in powers]
    for b, rows in enumerate(blocks):
        probs[b, :256] = shares[2 * b]
        probs[b, 256:] = shares[2 * b + 1]
        o = dot(shares[2 * b].astype(BF16), qkv[2, rows, :128])
        att[rows, :128] = jnp.where(low, o[:128], o[128:]).astype(BF16)
        att[rows, 128:] = dot(shares[2 * b + 1].astype(BF16), qkv[2, rows, 128:]).astype(BF16)
    parts[...] = dot(att[...], w_out[...]).astype(BF16).reshape(GROUP, OWN, D)


def summed(parts, landed, t, rows):
    return parts[t, rows].astype(F32) + landed[0, rows].astype(F32) + landed[1, rows].astype(F32) + landed[2, rows].astype(F32)


def split3(x):
    hi = x.astype(BF16)
    rest = x - hi.astype(F32)
    mid = rest.astype(BF16)
    return jnp.concatenate([hi, mid, (rest - mid.astype(F32)).astype(BF16)], axis=0)


def own_member(mem, t):
    return mem[pl.ds(pl.multiple_of(t * OWN_CAPS, OWN_CAPS), OWN_CAPS), pl.ds(pl.multiple_of(t * OWN, OWN), OWN)]


def text_norm_two(h, x, parts, landed, gain, x1, a2, t):
    rows = half_rows(h)
    y = x[rows, :].astype(F32) + summed(parts, landed, t, rows)
    x1[rows, :] = y
    n, _ = normalized(y)
    a2[t, rows] = (n * gain).astype(BF16)


def text_pool_one(x1, mem, x1_pool, t):
    own = own_member(mem, t)
    x1_pool[...] = dot(jnp.concatenate([own, own, own], axis=1), split3(x1[...]))


def text_up(a2, w_up, mem, w_down, x1_pool, dgelu, hidden, hsum, part, parts, t):
    for r in range(GROUP):
        rows = slice(r * OWN, r * OWN + OWN)
        u = dot(a2[r], w_up[...])
        phi = normal_cdf(u)
        dgelu[rows, :] = phi + u * (jnp.exp(u * u * -0.5) * 0.3989422804014327)
        hidden[rows, :] = (u * phi).astype(BF16)
    hsum[...] = dot(mem[...], hidden[...])
    both = dot(split_rows(hsum[...]), w_down[...])
    part[...] = (both[:CAPS] + both[CAPS:]).reshape(GROUP, OWN_CAPS, D)
    part[t] += x1_pool[...]
    parts[t] = part[...].reshape(CAPS, D).astype(BF16)


def counts_of(mem):
    return jnp.sum(mem.astype(F32), axis=1, keepdims=True)


def text_embed(parts, mem, w_proj, pooled, tf, scale):
    total = parts[0].astype(F32) + parts[1].astype(F32) + parts[2].astype(F32) + parts[3].astype(F32)
    rows = (total / counts_of(mem[...])).astype(BF16)
    pooled[...] = rows
    e = dot(rows, w_proj[...])
    rs = lax.rsqrt(jnp.sum(e * e, axis=-1, keepdims=True) + EPS)
    tf[...] = rs * e
    scale[...] = jnp.broadcast_to(rs, (CAPS, 128))


def score_sums(tf, images, s_ref, e_ref, row_sums, col_sums, t):
    s = 40.0 * dot_t(tf[...].astype(BF16), images[...].reshape(ROWS, D))
    s_ref[...] = s
    e = jnp.exp(s - 40.0)
    e_ref[...] = e
    diagonal = iota((CAPS, 128), 0) == iota((CAPS, 128), 1)
    row_sums[t] = jnp.sum(jnp.where(diagonal, jnp.sum(e, axis=1, keepdims=True), 0.0), axis=0, keepdims=True)
    col_sums[0] = jnp.sum(e, axis=0, keepdims=True)


def score_grad(s_ref, e_ref, row_sums, col_sums, pair, images, dts, vec, t):
    diagonal = iota((CAPS, 128), 0) == iota((CAPS, 128), 1)
    rows = jnp.sum(jnp.where(diagonal, row_sums[0] + row_sums[1] + row_sums[2] + row_sums[3], 0.0), axis=1, keepdims=True)
    cols = col_sums[0]
    for i in range(1, CHIPS):
        cols = cols + col_sums[i]
    lane = iota((CAPS, ROWS), 1)
    image = ((lane >> 4) & 15) * (2 * CAPS) + (lane >> 8) * CAPS + (lane & 15) + OWN_CAPS * t
    target = jnp.where(pair[...].reshape(CAPS, 128)[:, :1] == image, 1.0, 0.0)
    g = 0.5 * (e_ref[...] / rows + e_ref[...] / cols) - target
    dts[t] = (40.0 * dot(g.astype(BF16), images[...].reshape(ROWS, D))).astype(BF16)
    loss = (
        jnp.sum(40.0 + jnp.log(rows), axis=0, keepdims=True) * (1.0 / GROUP)
        + jnp.sum(40.0 + jnp.log(cols), axis=1, keepdims=True) * (1.0 / RANKS)
        - 2.0 * jnp.sum(jnp.sum(s_ref[...] * target, axis=1, keepdims=True), axis=0, keepdims=True)
    )
    vec[t, :, 1536:] = jnp.broadcast_to(loss, (1, 128))


def embed_grad(dts, tf, scale, w_proj, mem, de_ref, dz_ref, gp_ref):
    dt = dts[0].astype(F32) + dts[1].astype(F32) + dts[2].astype(F32) + dts[3].astype(F32)
    f = tf[...]
    de = (scale[:, :1] * (dt - f * jnp.sum(f * dt, axis=-1, keepdims=True))).astype(BF16)
    gp = dot_t(de, w_proj[...]) / counts_of(mem[...])
    de_ref[...] = de
    gp_ref[...] = gp
    dz_ref[...] = gp.astype(BF16)


def row_grad(gp_ref, mem, dx2, t):
    own = own_member(mem, t)
    gp = gp_ref[pl.ds(pl.multiple_of(t * OWN_CAPS, OWN_CAPS), OWN_CAPS), :]
    dx2[...] = t_dot(jnp.concatenate([own, own, own], axis=0), split3(gp))


def hidden_grad(dz, w_down):
    return split_rows(dot_t(dz[...], w_down[...]))


def hidden_spread(h, dh, mem_t, dgelu, w_up, du, parts):
    blocks = [pl.ds(r * OWN + h * PART, PART) for r in range(GROUP)]
    member = jnp.concatenate([mem_t[b, :] for b in blocks], axis=0)
    slope = jnp.concatenate([dgelu[b, :] for b in blocks], axis=0)
    rows = (dot(member, dh) * slope).astype(BF16)
    total = dot_t(rows, w_up[...]).astype(BF16)
    for r, b in enumerate(blocks):
        du[b, :] = rows[r * PART : (r + 1) * PART]
        parts[r, half_rows(h)] = total[r * PART : (r + 1) * PART]


def gain_grad(parts, normed, gain):
    total = jnp.zeros((1, D), F32)
    for r in range(GROUP):
        total = total + jnp.sum(parts[r].astype(F32) * normed[r].astype(F32), axis=0, keepdims=True)
    return total / gain


def put_chunks(g, first, values):
    rows = g.shape[-2]
    for c in range(values.shape[0] // rows):
        at = first + c
        place = (at,) if len(g.shape) == 4 else (at // 4, at % 4)
        for j in range(2):
            g[(j, *place)] = values[c * rows : (c + 1) * rows, j * HALF : (j + 1) * HALF].astype(BF16)


def down_proj_grad(hsum, dz, de, pooled, proj, g, h, t):
    hs = split_rows(hsum[...])
    dz2 = jnp.concatenate([dz[...], dz[...]], axis=0)
    put_chunks(g, 0, t_dot(hs[:, :256], dz2))
    put_chunks(g, 8, t_dot(hs[:, 256:512], dz2))
    put_chunks(h, 0, t_dot(hs[:, 512:], dz2))
    proj[...] = t_dot(pooled[...], de[...]).astype(BF16).reshape(GROUP, BAND, D)
    put_chunks(h, 8, proj[t])
    h[:, 3, 2:] = jnp.zeros((2, 2, 32, HALF), BF16)


def up_grad(a2, du, g, h):
    for i in range(3):
        rows = t_dot(a2[:, :, i * 256 : (i + 1) * 256].reshape(ROWS, 256), du[...])
        put_chunks(g if i < 2 else h, 8 * i if i < 2 else 0, rows)


def norm_two_grad(h, parts, landed, x1, gain, dx2, dx1, dy, t):
    rows = half_rows(h)
    da = summed(parts, landed, t, rows)
    n, scale = normalized(x1[rows, :])
    d = da * gain
    g = dx2[rows, :] + (d - jnp.mean(d, axis=-1, keepdims=True) - n * jnp.mean(d * n, axis=-1, keepdims=True)) * scale
    dx1[rows, :] = g
    dy[t, rows] = g.astype(BF16)


def attention_grad(dy, w_out, w_t, qkv, probs, dqkv, parts):
    datt = dot_t(dy[...].reshape(ROWS, D), w_out[...]).astype(BF16)
    low = low_half()
    blocks = [slice(128 * b, 128 * b + 128) for b in range(4)]
    sides, raw = [], []
    for b, rows in enumerate(blocks):
        sides.append((stacked(qkv[0, rows, :128], low), stacked(datt[rows, :128], low)))
        sides.append((qkv[0, rows, 128:], datt[rows, 128:]))
        raw.append(dot_t(sides[-2][1], qkv[2, rows, :128]))
        raw.append(dot_t(sides[-1][1], qkv[2, rows, 128:]))
    probs_of = [probs[b, part] for b in range(4) for part in (slice(0, 256), slice(256, 384))]
    ds = [(p * (x - jnp.sum(p * x, axis=-1, keepdims=True))).astype(BF16) for p, x in zip(probs_of, raw)]
    for b, rows in enumerate(blocks):
        for i, cols in ((2 * b, slice(0, 128)), (2 * b + 1, slice(128, BAND))):
            o = dot(ds[i], qkv[1, rows, cols])
            if i % 2 == 0:
                o = jnp.where(low, o[:128], o[128:])
            dqkv[0, rows, cols] = (o * 0.125).astype(BF16)
            dqkv[1, rows, cols] = (t_dot(ds[i], sides[i][0]) * 0.125).astype(BF16)
            dqkv[2, rows, cols] = t_dot(probs_of[i].astype(BF16), sides[i][1]).astype(BF16)
    total = dot(dqkv[0], w_t[0]) + dot(dqkv[1], w_t[1]) + dot(dqkv[2], w_t[2])
    parts[...] = total.astype(BF16).reshape(GROUP, OWN, D)


def out_grad(att, dy, g):
    put_chunks(g, 0, t_dot(att[...], dy[...].reshape(ROWS, D)))


def qkv_grad(dqkv, a1, g, h):
    rows = a1[...].reshape(ROWS, D)
    put_chunks(g, 6, t_dot(dqkv[0], rows))
    keys = t_dot(dqkv[1], rows)
    put_chunks(g, 12, keys[:128])
    put_chunks(h, 0, keys[128:])
    put_chunks(h, 4, t_dot(dqkv[2], rows))


def norm_one_grad(parts, landed, x, gain, dx1, out, t):
    da = summed(parts, landed, t, slice(0, OWN))
    n, scale = normalized(x[...].astype(F32))
    h = da * gain
    out[...] = dx1[...] + (h - jnp.mean(h, axis=-1, keepdims=True) - n * jnp.mean(h * n, axis=-1, keepdims=True)) * scale


class Reduction:
    def __init__(self, links, g, met, landed, full, pair):
        self.links, self.g, self.met, self.landed, self.full, self.pair = links, g, met, landed, full, pair

    def cores(self):
        self.open = sibling_send(self.links, self.g.at[1 - self.links.core], self.met, self.pair())

    def both_cores(self):
        finish(self.open)
        self.met[...] = (self.g[self.links.core].astype(F32) + self.met[...].astype(F32)).astype(BF16)

    def scatter(self):
        self.both_cores()
        sems = self.pair()
        for k in range(1, CHIPS):
            send(self.met.at[self.links.chip_of(k)], self.landed.at[k - 1], sems, self.links.chip_peer(k))
        self.open = sems, self.landed

    def gather(self):
        finish(self.open)
        total = self.met[self.links.chip].astype(F32)
        for k in range(CHIPS - 1):
            total = total + self.landed[k].astype(F32)
        half = self.full.at[self.links.core]
        half[self.links.chip] = total.astype(BF16)
        self.open = chip_share(self.links, half, self.pair())

    def share(self):
        finish(self.open)
        half = self.full.at[self.links.core]
        self.open = sibling_send(self.links, half, half, self.pair())

    def done(self):
        finish(self.open)


class TwoAxes(Reduction):
    def __init__(self, links, g, met, landed, near, full, pair, first, second):
        super().__init__(links, g, met, landed, full, pair)
        self.near, self.first, self.second = near, first, second
        self.i, self.j = links.place[first], links.place[second]

    def spread(self, axis, source, target):
        sems = self.pair()
        for k in (1, 3, 2):
            send(source(k), target(k), sems, self.links.axis_peer(axis, k))
        return sems

    def scatter(self):
        self.both_cores()
        sems = self.spread(
            self.first, lambda k: self.met.at[self.links.axis_rank(self.first, k)], lambda k: self.landed.at[k - 1]
        )
        self.open = sems, self.landed

    def scatter_second(self):
        finish(self.open)
        total = self.met[self.i].astype(F32)
        for k in range(3):
            total = total + self.landed[k].astype(F32)
        self.met[self.i] = total.astype(BF16)
        sems = self.spread(
            self.second, lambda k: self.met.at[self.i, self.links.axis_rank(self.second, k)], lambda k: self.near.at[k - 1]
        )
        self.open = sems, self.near

    def gather(self):
        finish(self.open)
        total = self.met[self.i, self.j].astype(F32)
        for k in range(3):
            total = total + self.near[k].astype(F32)
        core = self.links.core
        self.full[core, self.i, self.j] = total.astype(BF16)
        own = self.full.at[core, self.i, self.j]
        self.open = self.spread(self.second, lambda k: own, lambda k: own), self.full.at[0, 0, pl.ds(0, 3)]

    def gather_second(self):
        finish(self.open)
        own = self.full.at[self.links.core, self.i]
        self.open = self.spread(self.first, lambda k: own, lambda k: own), self.full.at[0, pl.ds(0, 3)]


def body(
    x, seg_t, pad_t, pair_in, gain_one, gain_two, img_gain_one, img_gain_two,
    h_tok, h_iqkv, h_iout, h_iup, h_idown, h_iproj, h_qkv, h_out, h_up, h_down, h_proj,
    o_loss, o_input, o_norms, f_a0, f_a1, f_b0, f_b1, f_c0, f_c1, proj_all,
    tok, iw_qkv, iw_out, iw_up, iw_down, iw_proj, w_qkv, w_out, w_up, w_down, w_proj, load,
    ibias, iap, iqkv, stage, iy, ypool, ihsum, images,
    bias, mem, mem_t, pair, a1, qkv, probs, att, p_att, l_att, x1, x1_pool, a2, dgelu, hsum, p_pool, pools,
    tf, scale, pooled, s_ref, e_ref, row_sums, core_sums, col_sums, dts, de, dz, gp, dx2, du, p_da2, l_da2, dx1, dy,
    dqkv, p_da1, l_da1, proj, vec, vec_core, vec_all,
    *work,
):
    g_a, g_b, g_c, m_a, m_b, m_c, r_a, r_b, r_c, n_a, n_b = (work[i : i + 2] for i in range(0, 22, 2))
    f_a, f_b, f_c = (f_a0, f_a1), (f_b0, f_b1), (f_c0, f_c1)
    sems = work[22]
    links = Links()
    t, dp, core, chip = links.t, links.dp, links.core, links.chip
    loads = {}
    count = iter(range(PAIRS))

    def pair_of():
        return sems.at[next(count)]


    def fetch(at, name, src, dst):
        loads[name] = pltpu.make_async_copy(src, dst, load.at[at])
        loads[name].start()

    fetch(0, "tok", h_tok, tok)
    fetch(1, "iqkv", h_iqkv, iw_qkv)
    links.greet()
    text_norm_one(x, as_row(gain_one), a1, t)
    pair[t] = column(pair_in)
    links.met()
    copies = group_share(links, a1, pair_of())
    pair_copies = group_share(links, pair, pair_of())
    fetch(2, "qkv", h_qkv, w_qkv)
    fetch(3, "out", h_out, w_out)
    fetch(4, "iout", h_iout, iw_out)

    text_masks(seg_t, pad_t, bias, mem, mem_t)
    image_bias(ibias)
    loads["tok"].wait()
    image_norm_one(tok, as_row(img_gain_one), stage)
    fetch(5, "iup", h_iup, iw_up)
    fetch(6, "up", h_up, w_up)
    fetch(7, "down", h_down, w_down)
    fetch(8, "idown", h_idown, iw_down)
    fetch(9, "iproj", h_iproj, iw_proj)
    fetch(10, "proj", h_proj, w_proj)
    image_permute(stage, iap)
    loads["iqkv"].wait()
    image_qkv(iap, iw_qkv, iqkv)

    finish(copies)
    loads["qkv"].wait()
    loads["out"].wait()
    text_attention(a1, w_qkv, bias, w_out, qkv, probs, att, p_att)
    copies = [scatter_half(links, p_att, l_att, pair_of(), 0)]

    image_attention(iqkv, ibias, stage, 0, 4)
    copies.append(scatter_half(links, p_att, l_att, pair_of(), 1))
    image_attention(iqkv, ibias, stage, 4, 8)
    finish(copies[0])
    text_norm_two(0, x, p_att, l_att, as_row(gain_two), x1, a2, t)
    copies[0] = share_half(links, a2, pair_of(), 0)
    loads["iout"].wait()
    image_out(stage, tok, iw_out, iy)
    finish(copies[1])
    text_norm_two(1, x, p_att, l_att, as_row(gain_two), x1, a2, t)
    copies[1] = share_half(links, a2, pair_of(), 1)
    image_norm_two(iy, as_row(img_gain_two), iap.at[:IROWS], ypool)

    loads["iup"].wait()
    image_up(iap.at[:IROWS], iw_up, ihsum, 0, 1)
    text_pool_one(x1, mem, x1_pool, t)

    image_up(iap.at[:IROWS], iw_up, ihsum, 1, FF // UP_TILE)
    loads["idown"].wait()
    loads["iproj"].wait()
    images[core, chip] = image_finish(ihsum, ypool, iw_down, iw_proj)
    image_copies = chip_share(links, images.at[core], pair_of())

    finish(copies[0])
    finish(copies[1])
    loads["up"].wait()
    loads["down"].wait()
    text_up(a2, w_up, mem, w_down, x1_pool, dgelu, du, hsum, p_pool, pools, t)
    copies = group_share(links, pools, pair_of())
    finish(image_copies)
    image_copies = sibling_send(links, images.at[core], images.at[core], pair_of())
    finish(pair_copies)
    loads["proj"].wait()
    finish(copies)
    text_embed(pools, mem, w_proj, pooled, tf, scale)
    finish(image_copies)

    score_sums(tf, images, s_ref, e_ref, row_sums, core_sums, t)
    row_copies = group_share(links, row_sums, pair_of())
    finish(sibling_send(links, core_sums.at[0], core_sums.at[1], pair_of()))
    col_sums[chip] = core_sums[0] + core_sums[1]
    col_copies = chip_share(links, col_sums, pair_of())
    finish(col_copies)
    finish(row_copies)
    score_grad(s_ref, e_ref, row_sums, col_sums, pair, images, dts, vec, t)
    finish(group_share(links, dts, pair_of()))
    embed_grad(dts, tf, scale, w_proj, mem, de, dz, gp)

    red_a = [TwoAxes(links, g_a[i], m_a[i], r_a[i], n_a[i], f_a[i], pair_of, "x", "z") for i in range(2)]
    red_b = [TwoAxes(links, g_b[i], m_b[i], r_b[i], n_b[i], f_b[i], pair_of, "z", "x") for i in range(2)]
    red_c = [Reduction(links, g_c[i], m_c[i], r_c[i], f_c[i], pair_of) for i in range(2)]

    def each(*steps):
        for step in steps:
            step()

    dh = hidden_grad(dz, w_down)
    hidden_spread(0, dh, mem_t, dgelu, w_up, du, p_da2)
    copies = [scatter_half(links, p_da2, l_da2, pair_of(), 0)]
    down_proj_grad(hsum, dz, de, pooled, proj, g_a[0], g_a[1], t)
    each(red_a[0].cores, red_a[1].cores)
    hidden_spread(1, dh, mem_t, dgelu, w_up, du, p_da2)
    up_grad(a2, du, g_b[0], g_b[1])
    each(red_b[0].cores, red_b[1].cores, red_a[0].scatter, red_a[1].scatter)
    row_grad(gp, mem, dx2, t)
    sent(copies[0])
    copies.append(scatter_half(links, p_da2, l_da2, pair_of(), 1))
    each(red_b[0].scatter, red_b[1].scatter)
    vec[t, :, 768:1536] = gain_grad(p_da2, a2, as_row(gain_two))
    arrived(copies[0])
    norm_two_grad(0, p_da2, l_da2, x1, as_row(gain_two), dx2, dx1, dy, t)
    copies[0] = share_half(links, dy, pair_of(), 0)
    finish(copies[1])
    norm_two_grad(1, p_da2, l_da2, x1, as_row(gain_two), dx2, dx1, dy, t)
    copies[1] = share_half(links, dy, pair_of(), 1)
    each(red_a[0].scatter_second, red_b[0].scatter_second)
    each(red_a[1].scatter_second, red_b[1].scatter_second)
    each(red_a[0].gather, red_b[0].gather)
    each(red_a[1].gather, red_b[1].gather)
    each(red_a[0].gather_second, red_b[0].gather_second)
    finish(copies[0])
    finish(copies[1])
    out_grad(att, dy, g_c[0])
    attention_grad(dy, w_out, w_qkv, qkv, probs, dqkv, p_da1)
    each(red_a[1].gather_second, red_b[1].gather_second)
    qkv_grad(dqkv, a1, g_c[0], g_c[1])
    each(red_c[0].cores, red_c[1].cores)
    vec[t, :, :768] = gain_grad(p_da1, a1, as_row(gain_one))
    vec_copies = group_share(links, vec, pair_of())
    copies = group_scatter(links, p_da1, l_da1, pair_of())
    each(red_c[0].scatter, red_c[1].scatter)
    finish(vec_copies)
    vec_core[0] = vec[0] + vec[1] + vec[2] + vec[3]
    finish(sibling_send(links, vec_core.at[0], vec_core.at[1], pair_of()))
    vec_all[chip] = vec_core[0] + vec_core[1]
    vec_copies = chip_share(links, vec_all, pair_of())
    red_a[1].share()
    proj_all[core, t, :4] = f_a1[core, 2]
    proj_all[core, t, 4:] = f_a1[core, 3, :2]
    proj_copies = group_share(links, proj_all.at[core], pair_of())
    finish(copies)
    norm_one_grad(p_da1, l_da1, x, as_row(gain_one), dx1, o_input, t)
    each(red_c[0].gather, red_c[1].gather)
    each(red_a[0].share, red_b[0].share, red_b[1].share)
    finish(proj_copies)
    proj_copies = sibling_send(links, proj_all.at[core], proj_all.at[core], pair_of())
    each(red_a[0].done, red_a[1].done, red_b[0].done, red_b[1].done)
    finish(vec_copies)
    total = vec_all[0]
    for i in range(1, CHIPS):
        total = total + vec_all[i]
    o_norms[...] = total[:, :1536]
    o_loss[...] = total[:, 1536:] * (1.0 / 4096.0)
    finish(proj_copies)
    each(red_c[0].share, red_c[1].share, red_c[0].done, red_c[1].done)


def widen(
    loss, norms, grad, a0, a1, b0, b1, c0, c1, full_proj,
    o_loss, o_input, o_one, o_two, o_down, o_up, o_out, o_qkv, o_proj, down, up, out, qkv, proj, stored,
):
    stores = []

    def write(buf, target):
        stores.append(pltpu.make_async_copy(buf, target, stored.at[len(stores)]))
        stores[-1].start()

    def block(buf, target, first, parts, rows):
        for j in range(2):
            buf[first : first + rows, j * HALF : (j + 1) * HALF] = parts[j].reshape(rows, HALF).astype(F32)
        write(buf.at[pl.ds(first, rows)], target.at[pl.ds(first, rows)])

    write(grad, o_input)
    for buf, target, whole, rest in ((down, o_down, a0, a1[:, :2]), (up, o_up, b0, b1)):
        block(buf, target, 0, whole[:, :2], 256)
        block(buf, target, 256, whole[:, 2:], 256)
        block(buf, target, 512, rest, 256)
    for r in range(GROUP):
        block(proj, o_proj, r * BAND, full_proj[:, r], BAND)
    block(qkv, o_qkv, 0, c0[:, 6:], 320)
    block(qkv, o_qkv, 320, c1, 256)
    block(out, o_out, 0, c0[:, :6], BAND)
    o_loss[0, 0] = loss[0, 0]
    o_one[...] = norms[:, :D].reshape(D)
    o_two[...] = norms[:, D:].reshape(D)
    for copy in stores:
        copy.wait()


def on_device(
    text_input, segment_ids, pad_mask, pairing, ln_first, w_qkv, w_out, ln_second, w_up, w_down, text_proj,
    image_tokens, img_ln_first, img_w_qkv, img_w_out, img_ln_second, img_w_up, img_w_down, img_proj,
):
    vmem = pl.BlockSpec(memory_space=VM)
    hbm = pl.BlockSpec(memory_space=pl.ANY)
    shape = jax.ShapeDtypeStruct
    sums = ((4, 4, 32, HALF),) * 2 + ((4, 4, 32, HALF), (4, 4, 16, HALF)) + ((16, 32, HALF), (16, 16, HALF))
    dma = pltpu.SemaphoreType.DMA
    scratch = [
        VM((IROWS, D), BF16), VM((3, D, D), BF16), VM((D, D), BF16), VM((D, FF), BF16), VM((FF, D), BF16), VM((D, D), BF16),
        VM((3, BAND, D), BF16), VM((BAND, D), BF16), VM((D, HID), BF16), VM((HID, D), BF16), VM((D, D), BF16), dma((11,)),
        VM((2 * PAIR, PAIR), F32), VM((PROWS, D), BF16), VM((3, PROWS, D), BF16), VM((6, PROWS, 128), F32), VM((IROWS, D), F32),
        VM((IMGS, D), F32), VM((IMGS, FF), F32), VM((2, CHIPS, IMGS, D), BF16),
        VM((4, 128, 128), F32), VM((CAPS, ROWS), BF16), VM((ROWS, 128), BF16), VM((GROUP, OWN_CAPS, 128), I32),
        VM((GROUP, OWN, D), BF16), VM((3, ROWS, BAND), BF16), VM((4, HALF, 128), F32), VM((ROWS, BAND), BF16),
        VM((GROUP, OWN, D), BF16), VM((3, OWN, D), BF16), VM((OWN, D), F32), VM((OWN_CAPS, D), F32), VM((GROUP, OWN, D), BF16),
        VM((ROWS, HID), F32), VM((CAPS, HID), F32), VM((GROUP, OWN_CAPS, D), F32), VM((GROUP, CAPS, D), BF16),
        VM((CAPS, D), F32), VM((CAPS, 128), F32), VM((CAPS, D), BF16), VM((CAPS, ROWS), F32),
        VM((CAPS, ROWS), F32), VM((GROUP, 1, 128), F32), VM((2, 1, ROWS), F32), VM((CHIPS, 1, ROWS), F32), VM((GROUP, CAPS, D), BF16),
        VM((CAPS, D), BF16), VM((CAPS, D), BF16), VM((CAPS, D), F32),
        VM((OWN, D), F32), VM((ROWS, HID), BF16), VM((GROUP, OWN, D), BF16), VM((3, OWN, D), BF16), VM((OWN, D), F32),
        VM((GROUP, OWN, D), BF16), VM((3, ROWS, BAND), BF16), VM((GROUP, OWN, D), BF16), VM((3, OWN, D), BF16),
        VM((GROUP, BAND, D), BF16), VM((GROUP, 1, VEC), F32), VM((2, 1, VEC), F32), VM((CHIPS, 1, VEC), F32),
    ]
    scratch += [VM((2,) + s, BF16) for s in sums] + [VM(s, BF16) for s in sums]
    scratch += [VM((3,) + s[1:], BF16) for s in sums[:4]] + [VM((15,) + s[1:], BF16) for s in sums[4:]]
    scratch += [VM((3,) + s[2:], BF16) for s in sums[:4]] + [dma((PAIRS, 2))]
    loss, input_grad, norms, *full = pl.pallas_call(
        body,
        out_shape=(
            VM((1, 128), F32), VM((OWN, D), F32), VM((1, 1536), F32),
            *(VM((2,) + s, BF16) for s in sums), VM((2, GROUP, 6, 32, HALF), BF16),
        ),
        in_specs=[vmem] * 3 + [pl.BlockSpec(memory_space=pltpu.SMEM)] + [vmem] * 4 + [hbm] * 11,
        out_specs=(vmem,) * 10,
        scratch_shapes=scratch,
        compiler_params=pltpu.CompilerParams(collective_id=0, has_side_effects=True, vmem_limit_bytes=57 << 20),
        name="lit",
    )(
        text_input, segment_ids.T, pad_mask.T, pairing, ln_first, ln_second, img_ln_first, img_ln_second,
        image_tokens.transpose(1, 0, 2).reshape(IROWS, D), img_w_qkv, img_w_out, img_w_up, img_w_down, img_proj,
        w_qkv.swapaxes(1, 2), w_out, w_up, w_down, text_proj,
    )

    loss, input_grad, one, two, down, up, out, qkv, proj = pl.pallas_call(
        widen,
        out_shape=(
            shape((1, 1), F32), shape((OWN, D), F32), shape((D,), F32), shape((D,), F32), shape((HID, D), F32),
            shape((D, HID), F32), shape((BAND, D), F32), shape((3 * BAND, D), F32), shape((D, D), F32),
        ),
        in_specs=[vmem] * 10,
        out_specs=(pl.BlockSpec(memory_space=pltpu.SMEM), hbm, vmem, vmem, hbm, hbm, hbm, hbm, hbm),
        scratch_shapes=[
            VM((HID, D), F32), VM((D, HID), F32), VM((BAND, D), F32), VM((3 * BAND, D), F32), VM((D, D), F32),
            dma((14,)),
        ],
        compiler_params=pltpu.CompilerParams(vmem_limit_bytes=40 << 20),
        name="widen",
    )(loss, norms, input_grad, *full)
    return (loss.reshape(()), input_grad, one, qkv.reshape(3, BAND, D).swapaxes(1, 2), out, two, up, down, proj)


def solution(mesh):
    rows = P(("dp", "tensor"))
    in_specs = (
        P(("dp", "tensor"), None), P("dp", None), P("dp", None), rows, P(), P(None, None, "tensor"), P("tensor", None), P(),
        P(None, "tensor"), P("tensor", None), P(), P(("dp", "tensor"), None, None), P(), P(), P(), P(), P(), P(), P(),
    )
    out_specs = (
        P(), P(("dp", "tensor"), None), P(), P(None, None, "tensor"), P("tensor", None), P(), P(None, "tensor"),
        P("tensor", None), P(),
    )
    return jax.shard_map(on_device, mesh=mesh, in_specs=in_specs, out_specs=out_specs, check_vma=False)
```
